256 devices in a mesh: sub: 64 (over x, z, core), layer: 4 (over y).
Axes of the slice: x: 4, y: 4, z: 8, core: 2. Of those that a mesh axis runs over, the one named last changes fastest.
Arguments:
- geometry: float32 [10, 4, 98304], P(None, 'layer', 'sub'), may hold values from -2 to 2, as said below
- dest_slot: int32 [4, 98304], P('layer', 'sub'), may hold values from 0 to 98303, as said below
- pairs: int32 [2, 4, 98304], P(None, 'layer', 'sub'), may hold values from 0 to 767, as said below
- colors: int32 [4, 768], P('layer', 'sub'), may hold values from 0 to 3
- free_vel: float32 [6, 4, 32768], P(None, 'layer', 'sub'), may hold values from -6 to 6
- inertia: float32 [4, 4, 32768], P(None, 'layer', 'sub'), may hold values from 0.5 to 3
- exports: int32 [4, 4, 4096], P(None, 'layer', 'sub'), may hold values from 0 to 511, as said below
Outputs:
- impulse: float32 [3, 4, 98304], P(None, 'layer', 'sub')
- velocity: float32 [6, 4, 32768], P(None, 'layer', 'sub')
The draws below stay inside these ranges and needn't reach their ends.
Inputs may be any that keep to these rules, and one draw needn't show every extreme that they name: Within each layer dest_slot is a permutation of 0 to 98303; the owner of a detected contact lies in the same aligned group of 4 sub indices as the device that holds it. At most 768 contacts of one device go to one owner, and in every group some device hands exactly 768 to one owner. pairs[0] is an own block, 0 to 511. pairs[1] is another own block, or 512 + d * 64 + i, the copy of the i-th block that the neighbour in direction d (0 lower sub index, 1 higher, 2 lower layer, 3 higher layer) lists toward this subdomain; only directions with a neighbour appear. `exports`: each subdomain's list for one direction holds 64 distinct own blocks. `geometry`: rows 0 and 1 lie in -1 to 1 and row 2 in 0.5 to 1.5 (the normal before normalizing); rows 3 to 8 are lever arms, row 9 the gap rate within -1 to 1.
All inputs are finite; a program needn't handle non-finite values.
Results may differ from the reference program's by a relative error of at most 0.0003.
Values sent between devices are 32-bit elements; how exact they have to be, the bound alone decides.
A program may use at most 64 MiB of HBM per device.

```python
import math
import jax
import jax.numpy as jnp
from jax import lax

NB = 512
WIN = 4
SWEEPS = 3
NCOLOR = 4
TILE = 128
CO = 1536
NI = 64
CAP = 768
CL = 98304
BL = 32768
TL = 768
N_SUB = 64
N_LAYER = 4


def shuffled(perm_key):
    return jax.random.permutation(perm_key, CO).astype(jnp.int32)


def relay_group(group_key):
    key_cut, key_big, key_src, key_dst = jax.random.split(group_key, 4)
    remainder = CO - CAP
    cut_points = jnp.sort(jax.random.randint(key_cut, (WIN - 2,), 0, remainder + 1)).astype(jnp.int32)
    cut_edges = jnp.concatenate([jnp.zeros((1,), jnp.int32), cut_points, jnp.full((1,), remainder, jnp.int32)])
    pieces = cut_edges[1:] - cut_edges[:-1]
    largest = jax.random.randint(key_big, (), 0, WIN)
    position = jnp.arange(WIN, dtype=jnp.int32)
    shifted = jnp.clip(jnp.where(position < largest, position, position - 1), 0, WIN - 2)
    circle = jnp.where(position == largest, CAP, pieces[shifted]).astype(jnp.int32)
    counts = circle[(position[None, :] - position[:, None]) % WIN]
    send_start = jnp.cumsum(counts, axis=1) - counts
    recv_start = jnp.cumsum(counts, axis=0) - counts
    src_order = jax.vmap(shuffled)(jax.random.split(key_src, WIN))
    dst_order = jax.vmap(shuffled)(jax.random.split(key_dst, WIN))
    flat_index = jnp.arange(WIN * CO, dtype=jnp.int32)
    source = flat_index // CO
    within = flat_index % CO
    span_ends = (send_start + counts)[source]
    target = jnp.sum((within[:, None] >= span_ends).astype(jnp.int32), axis=1)
    placed = within - send_start[source, target]
    landing = recv_start[source, target] + placed
    src_rows = source * CO + src_order[source, within]
    dst_slots = target * CO + dst_order[target, landing]
    return jnp.zeros((WIN * CO,), jnp.int32).at[src_rows].set(dst_slots)


def draw_dest_slot(key, part):
    groups = N_SUB // WIN
    group_keys = jax.random.split(jax.random.fold_in(key, 11), N_LAYER * groups)
    tables = jax.vmap(relay_group)(group_keys).reshape(N_LAYER, groups, WIN * CO)
    group_base = (jnp.arange(groups, dtype=jnp.int32) * (WIN * CO))[None, :, None]
    return (tables + group_base).reshape(N_LAYER, N_SUB * CO).astype(jnp.int32)


def draw_pairs(key, part):
    key_first, key_other, key_dir, key_which, key_remote = jax.random.split(jax.random.fold_in(key, 23), 5)
    grid_shape = (N_LAYER, N_SUB, CO)
    first = jax.random.randint(key_first, grid_shape, 0, NB)
    other = (first + 1 + jax.random.randint(key_other, grid_shape, 0, NB - 1)) % NB
    direction = jax.random.randint(key_dir, grid_shape, 0, 4)
    which = jax.random.randint(key_which, grid_shape, 0, NI)
    remote = jax.random.randint(key_remote, grid_shape, 0, 4) == 0
    sub_pos = jnp.arange(N_SUB, dtype=jnp.int32)[None, :, None]
    layer_pos = jnp.arange(N_LAYER, dtype=jnp.int32)[:, None, None]
    exists = jnp.where(direction == 0, sub_pos > 0, jnp.where(direction == 1, sub_pos < N_SUB - 1, jnp.where(direction == 2, layer_pos > 0, layer_pos < N_LAYER - 1)))
    second = jnp.where(remote & exists, NB + direction * NI + which, other)
    return jnp.stack([first, second]).reshape(2, N_LAYER, N_SUB * CO).astype(jnp.int32)


def pick_listed(perm_key):
    return jax.random.permutation(perm_key, NB)[:NI].astype(jnp.int32)


def draw_exports(key, part):
    list_keys = jax.random.split(jax.random.fold_in(key, 37), 4 * N_LAYER * N_SUB)
    listed = jax.vmap(pick_listed)(list_keys)
    return listed.reshape(4, N_LAYER, N_SUB * NI).astype(jnp.int32)


def draw_geometry(key, part):
    key_flat, key_up, key_arm, key_gap = jax.random.split(jax.random.fold_in(key, 41), 4)
    grid_shape = (N_LAYER, N_SUB * CO)
    flat_part = jax.random.uniform(key_flat, (2,) + grid_shape, jnp.float32, -1.0, 1.0)
    upward = jax.random.uniform(key_up, (1,) + grid_shape, jnp.float32, 0.5, 1.5)
    arms = 0.5 * jax.random.truncated_normal(key_arm, -4.0, 4.0, (6,) + grid_shape, jnp.float32)
    gap_rate = 0.5 * jax.random.truncated_normal(key_gap, -2.0, 2.0, (1,) + grid_shape, jnp.float32)
    return jnp.concatenate([flat_part, upward, arms, gap_rate], axis=0).astype(jnp.float32)


def place_ends(drawn, key, low, high):
    shape = drawn.shape
    index_at = [jax.random.randint(jax.random.fold_in(key, axis), (), 0, shape[axis]) for axis in range(len(shape))]
    drawn = drawn.at[tuple(index_at)].set(low)
    longest = shape.index(max(shape))
    index_at[longest] = (index_at[longest] + 1) % shape[longest]
    return drawn.at[tuple(index_at)].set(high)


def steps_of(key, dims, cuts, smallest, top_value):
    def one(dim, shards_of):
        heights = jax.random.uniform(jax.random.fold_in(jax.random.fold_in(key, 6), dim), (shards_of,), jnp.float32, smallest / len(cuts), top_value / len(cuts))
        return jnp.repeat(jnp.exp(heights), dims[dim] // shards_of).reshape((-1,) + (1,) * (len(dims) - dim - 1))

    level = one(*cuts[0])
    for cut in cuts[1:]:
        level = level * one(*cut)
    return level


def normal_values(stream_key, shape, spread, reach, cuts=(), kind=jnp.bfloat16):
    result = jax.random.normal(stream_key, shape, jnp.float32) * spread
    if len(cuts) > 0:
        result = steps_of(stream_key, shape, cuts, -0.22, 0.18) * result
    return jnp.clip(result, min=-reach, max=reach).astype(kind)


def setup_inputs(seed: int = 0) -> dict:
    key_of = jax.random.split(jax.random.key(seed), 8)
    geometry = draw_geometry(jax.random.fold_in(key_of[7], 71), 0)
    dest_slot = draw_dest_slot(jax.random.fold_in(key_of[7], 71), 0)
    pairs = draw_pairs(jax.random.fold_in(key_of[7], 71), 0)
    colors = place_ends(jax.random.randint(key_of[3], (N_LAYER, TL), 0, NCOLOR), jax.random.fold_in(key_of[3], 1), 0, NCOLOR - 1).astype(jnp.int32)
    free_vel = normal_values(key_of[4], (6, N_LAYER, BL), 1.0, 6.0, ((1, 4), (2, 64)), jnp.float32)
    inertia = jnp.clip(jnp.exp(math.log(3.0) - 1.7917595 * jax.random.uniform(key_of[5], (4, N_LAYER, BL), jnp.float32) ** steps_of(key_of[5], (4, N_LAYER, BL), ((1, 4), (2, 64)), -0.2, 0.2)), 0.5, 3.0)
    exports = draw_exports(jax.random.fold_in(key_of[7], 71), 0)
    return {"geometry": geometry, "dest_slot": dest_slot, "pairs": pairs, "colors": colors, "free_vel": free_vel, "inertia": inertia, "exports": exports}


relaxation = 0.7
friction = 0.6
tangent_floor = 0.1

def cross_rows(first_vec, second_vec):
    return jnp.stack([first_vec[1] * second_vec[2] - first_vec[2] * second_vec[1], first_vec[2] * second_vec[0] - first_vec[0] * second_vec[2], first_vec[0] * second_vec[1] - first_vec[1] * second_vec[0]])

def arm_block(lever_arm, spin_inv):
    return jnp.stack([spin_inv[1] * lever_arm[2] * lever_arm[2] + spin_inv[2] * lever_arm[1] * lever_arm[1], spin_inv[0] * lever_arm[2] * lever_arm[2] + spin_inv[2] * lever_arm[0] * lever_arm[0], spin_inv[0] * lever_arm[1] * lever_arm[1] + spin_inv[1] * lever_arm[0] * lever_arm[0], -spin_inv[2] * lever_arm[0] * lever_arm[1], -spin_inv[1] * lever_arm[0] * lever_arm[2], -spin_inv[0] * lever_arm[1] * lever_arm[2]])

def contact_setup(geometry, props_first, props_second):
    raw_normal = geometry[0:3]
    normal = raw_normal / jnp.sqrt(lax.optimization_barrier(jnp.sum(raw_normal * raw_normal, axis=0)))
    side_norm = jnp.sqrt(normal[1] * normal[1] + normal[2] * normal[2])
    tangent_one = jnp.stack([jnp.zeros_like(side_norm), normal[2] / side_norm, -normal[1] / side_norm])
    tangent_two = cross_rows(normal, tangent_one)
    frames = jnp.stack([normal, tangent_one, tangent_two])
    entries = arm_block(geometry[3:6], props_first[1:4]) + arm_block(geometry[6:9], props_second[1:4])
    masses = props_first[0] + props_second[0]
    entry_xx = masses + entries[0]
    entry_yy = masses + entries[1]
    entry_zz = masses + entries[2]
    entry_xy = entries[3]
    entry_xz = entries[4]
    entry_yz = entries[5]
    cofactor_xx = entry_yy * entry_zz - entry_yz * entry_yz
    cofactor_xy = entry_xz * entry_yz - entry_xy * entry_zz
    cofactor_xz = entry_xy * entry_yz - entry_xz * entry_yy
    cofactor_yy = entry_xx * entry_zz - entry_xz * entry_xz
    cofactor_yz = entry_xy * entry_xz - entry_xx * entry_yz
    cofactor_zz = entry_xx * entry_yy - entry_xy * entry_xy
    determinant = entry_xx * cofactor_xx + entry_xy * cofactor_xy + entry_xz * cofactor_xz
    inverse = jnp.stack([cofactor_xx, cofactor_yy, cofactor_zz, cofactor_xy, cofactor_xz, cofactor_yz]) / determinant
    return (frames, inverse)

def contact_pass(impulse, vel_table, first_idx, second_idx, frames, geometry, inverse, props_first, props_second, active):
    first_vel = vel_table[:, first_idx]
    second_vel = vel_table[:, second_idx]
    arm_first = geometry[3:6]
    arm_second = geometry[6:9]
    relative = first_vel[0:3] + cross_rows(first_vel[3:6], arm_first) - second_vel[0:3] - cross_rows(second_vel[3:6], arm_second)
    target = relative + geometry[9] * frames[0]
    solved = jnp.stack([inverse[0] * target[0] + inverse[3] * target[1] + inverse[4] * target[2], inverse[3] * target[0] + inverse[1] * target[1] + inverse[5] * target[2], inverse[4] * target[0] + inverse[5] * target[1] + inverse[2] * target[2]])
    trial_impulse = impulse - relaxation * lax.optimization_barrier(jnp.sum(frames * solved[None], axis=1))
    normal_part = jnp.maximum(trial_impulse[0], 0.0)
    slide_norm = jnp.sqrt(trial_impulse[1] * trial_impulse[1] + trial_impulse[2] * trial_impulse[2])
    factor = jnp.minimum(1.0, friction * normal_part / jnp.maximum(slide_norm, tangent_floor))
    projected = jnp.stack([normal_part, trial_impulse[1] * factor, trial_impulse[2] * factor])
    updated = jnp.where(active[None], projected, impulse)
    change = updated - impulse
    push_world = lax.optimization_barrier(jnp.sum(frames * change[:, None], axis=0))
    first_push = jnp.concatenate([props_first[0:1] * push_world, props_first[1:4] * cross_rows(arm_first, push_world)])
    second_push = -jnp.concatenate([props_second[0:1] * push_world, props_second[1:4] * cross_rows(arm_second, push_world)])
    vel_table = vel_table.at[:, first_idx].add(first_push).at[:, second_idx].add(second_push)
    return (updated, vel_table)

def gather_exports(values, export_list):
    index = jnp.transpose(export_list, (1, 2, 0, 3)).reshape(N_LAYER, N_SUB, 4 * NI)
    picked = jnp.take_along_axis(values, jnp.broadcast_to(index[None], (values.shape[0],) + index.shape), axis=3)
    picked = picked.reshape(values.shape[0], N_LAYER, N_SUB, 4, NI)
    return jnp.transpose(picked, (0, 3, 1, 2, 4))

def neighbour_trade(outbound):
    rows_here = outbound.shape[0]
    zero_sub = jnp.zeros((rows_here, N_LAYER, 1, NI), jnp.float32)
    zero_layer = jnp.zeros((rows_here, 1, N_SUB, NI), jnp.float32)
    from_lower = jnp.concatenate([zero_sub, outbound[:, 1, :, :-1]], axis=2)
    from_upper = jnp.concatenate([outbound[:, 0, :, 1:], zero_sub], axis=2)
    from_below = jnp.concatenate([zero_layer, outbound[:, 3, :-1]], axis=1)
    from_above = jnp.concatenate([outbound[:, 2, 1:], zero_layer], axis=1)
    return jnp.stack([from_lower, from_upper, from_below, from_above], axis=3)

def add_into(values_in, index):
    return jnp.zeros((values_in.shape[0], NB), jnp.float32).at[:, index].add(values_in)

def scatter_exports(arrived, export_list):
    rows_here = arrived.shape[0]
    moved = jnp.transpose(arrived, (1, 2, 0, 3, 4)).reshape(N_LAYER * N_SUB, rows_here, 4 * NI)
    index = jnp.transpose(export_list, (1, 2, 0, 3)).reshape(N_LAYER * N_SUB, 4 * NI)
    summed = jax.vmap(add_into)(moved, index)
    return jnp.transpose(summed.reshape(N_LAYER, N_SUB, rows_here, NB), (2, 0, 1, 3))

def place_layer(geo_layer, slot_layer):
    return jnp.zeros_like(geo_layer).at[:, slot_layer].set(geo_layer)

def reference(geometry, dest_slot, pairs, colors, free_vel, inertia, exports):
    devices = N_LAYER * N_SUB
    table_len = NB + 4 * NI
    owner_geo = jax.vmap(place_layer, in_axes=(1, 0), out_axes=1)(geometry, dest_slot).reshape(10, devices * CO)
    table_base = (jnp.arange(devices, dtype=jnp.int32) * table_len)[:, None]
    first_idx = (pairs[0].reshape(devices, CO) + table_base).reshape(-1)
    second_idx = (pairs[1].reshape(devices, CO) + table_base).reshape(-1)
    tile_color = jnp.repeat(colors.reshape(devices, CO // TILE), TILE, axis=1).reshape(-1)
    own_vel = free_vel.reshape(6, N_LAYER, N_SUB, NB)
    own_props = inertia.reshape(4, N_LAYER, N_SUB, NB)
    export_list = exports.reshape(4, N_LAYER, N_SUB, NI)
    sub_pos = jnp.arange(N_SUB, dtype=jnp.int32)[None, :]
    layer_pos = jnp.arange(N_LAYER, dtype=jnp.int32)[:, None]
    grid_shape = (N_LAYER, N_SUB)
    has_neighbour = jnp.stack([jnp.broadcast_to(sub_pos > 0, grid_shape), jnp.broadcast_to(sub_pos < N_SUB - 1, grid_shape), jnp.broadcast_to(layer_pos > 0, grid_shape), jnp.broadcast_to(layer_pos < N_LAYER - 1, grid_shape)]).astype(jnp.float32)
    listed = jnp.broadcast_to(jnp.transpose(has_neighbour, (1, 2, 0))[None, :, :, :, None], (1, N_LAYER, N_SUB, 4, NI))
    multiplicity = 1.0 + scatter_exports(listed, export_list)[0]

    def make_table(values):
        ghosts = neighbour_trade(gather_exports(values, export_list))
        ghosts = ghosts.reshape(values.shape[0], N_LAYER, N_SUB, 4 * NI)
        return jnp.concatenate([values, ghosts], axis=3).reshape(values.shape[0], -1)
    prop_table = make_table(own_props)
    vel_table = make_table(own_vel)
    props_first = prop_table[:, first_idx]
    props_second = prop_table[:, second_idx]
    frames, inverse = contact_setup(owner_geo, props_first, props_second)
    impulse = jnp.zeros((3, devices * CO), jnp.float32)
    for sweep_step in range(SWEEPS):
        start_table = vel_table
        for color_now in range(NCOLOR):
            impulse, vel_table = contact_pass(impulse, vel_table, first_idx, second_idx, frames, owner_geo, inverse, props_first, props_second, tile_color == color_now)
        change = (vel_table - start_table).reshape(6, N_LAYER, N_SUB, table_len)
        ghost_change = jnp.transpose(change[..., NB:].reshape(6, N_LAYER, N_SUB, 4, NI), (0, 3, 1, 2, 4))
        incoming = scatter_exports(neighbour_trade(ghost_change), export_list)
        own_vel = own_vel + (change[..., :NB] + incoming) / multiplicity
        if sweep_step + 1 < SWEEPS:
            vel_table = make_table(own_vel)
    return (impulse.reshape(3, N_LAYER, CL), own_vel.reshape(6, N_LAYER, BL))
```

```python
import jax
import jax.numpy as jnp
from jax import lax
from jax.experimental import pallas as pl
from jax.experimental.pallas import tpu as pltpu
from jax.sharding import PartitionSpec as P

WIN = 4
SWEEPS = 3
NCOLOR = 4
LANES = 128
TILES = 12
ROWS = 16
SPLIT = 256
OWN = 4
TABLE = 6

relaxation = 0.7
friction = 0.6
tangent_floor = 0.1

MESH = pl.DeviceIdType.MESH
F32 = jnp.float32
BF16 = jnp.bfloat16
NT = (((1,), (1,)), ((), ()))


def cross(u, v):
    return [
        u[1] * v[2] - u[2] * v[1],
        u[2] * v[0] - u[0] * v[2],
        u[0] * v[1] - u[1] * v[0],
    ]


def dot3(u, v):
    return u[0] * v[0] + u[1] * v[1] + u[2] * v[2]


def take(row_block, index):
    return jnp.take_along_axis(row_block, index, axis=1, mode="promise_in_bounds")


def coarse(value):
    return value.astype(BF16).astype(F32)


def arm_block(arm, spin):
    return [
        spin[1] * arm[2] * arm[2] + spin[2] * arm[1] * arm[1],
        spin[0] * arm[2] * arm[2] + spin[2] * arm[0] * arm[0],
        spin[0] * arm[1] * arm[1] + spin[1] * arm[0] * arm[0],
        -spin[2] * arm[0] * arm[1],
        -spin[1] * arm[0] * arm[2],
        -spin[0] * arm[1] * arm[2],
    ]


def kernel(
    n_sub,
    n_layer,
    geo_ref,
    slot_ref,
    pairs_ref,
    color_ref,
    free_ref,
    inertia_ref,
    exports_ref,
    imp_out,
    vel_out,
    slot_hot,
    pair_hot,
    split_geo,
    relay_left,
    push_left,
    outgoing,
    incoming,
    geo,
    index,
    shade,
    const,
    impulse,
    push,
    table,
    start,
    inverse_list,
    weight,
    first_out,
    first_in,
    round_out,
    round_in,
    relay_send,
    relay_recv,
    round_send,
    round_recv,
):
    sub = lax.axis_index("sub")
    layer = lax.axis_index("layer")
    base = (sub // WIN) * WIN
    place = sub - base
    lower_sub = lax.rem(sub + n_sub - 1, n_sub)
    higher_sub = lax.rem(sub + 1, n_sub)
    lower_layer = lax.rem(layer + n_layer - 1, n_layer)
    higher_layer = lax.rem(layer + 1, n_layer)

    def mate(step):
        return base + lax.rem(place + step, WIN)

    around = (
        ((lower_sub, layer), 1, 0),
        ((higher_sub, layer), 0, 0),
        ((sub, lower_layer), 3, 1),
        ((sub, higher_layer), 2, 1),
    )

    barrier = pltpu.get_barrier_semaphore()
    for device, _, _ in around:
        pl.semaphore_signal(barrier, inc=1, device_id=device, device_id_type=MESH)
    for step in range(1, WIN):
        pl.semaphore_signal(
            barrier, inc=1, device_id=(mate(step), layer), device_id_type=MESH
        )

    def trade(step, src, dst):
        return [
            pltpu.make_async_remote_copy(
                src_ref=src.at[pair],
                dst_ref=dst.at[slot],
                send_sem=round_send.at[step, slot],
                recv_sem=round_recv.at[step, slot],
                device_id=device,
                device_id_type=MESH,
            )
            for device, slot, pair in around
        ]

    def exchange(step):
        return trade(step, round_out.at[step - 1], round_in.at[step - 1])

    lane8 = lax.broadcasted_iota(jnp.int32, (8, LANES), 1)
    lane16 = lax.broadcasted_iota(jnp.int32, (ROWS, LANES), 1)

    table[...] = jnp.zeros_like(table)
    for h in range(OWN):
        cols = slice(h * LANES, (h + 1) * LANES)
        table[0:6, cols] = free_ref[pl.ds(h, 6, stride=OWN), :]
        table[8:12, cols] = inertia_ref[pl.ds(h, 4, stride=OWN), :]
    listed = [
        jnp.concatenate([exports_ref[1], exports_ref[0]], axis=1),
        jnp.concatenate([exports_ref[3], exports_ref[2]], axis=1),
    ]

    def pick_listed(pair, rows):
        high = jnp.broadcast_to(lax.shift_right_logical(listed[pair], 7), (rows, LANES))
        low = jnp.broadcast_to(lax.bitwise_and(listed[pair], 127), (rows, LANES))
        got = take(table[0:rows, 0:LANES], low)
        for h in range(1, OWN):
            block = take(table[0:rows, h * LANES : (h + 1) * LANES], low)
            got = jnp.where(high == h, block, got)
        return got

    for pair in range(2):
        first_out[pair] = pick_listed(pair, 16)

    for t in range(TILES):
        cols = slice(t * LANES, (t + 1) * LANES)
        main = geo_ref[pl.ds(t, 8, stride=TILES), :]
        rest = geo_ref[pl.ds(8 * TILES + t, 2, stride=TILES), :]
        main_a = coarse(main)
        main_b = coarse(main - main_a)
        rest_a = coarse(rest)
        rest_b = coarse(rest - rest_a)
        split_geo[0:8, cols] = main_a
        split_geo[8:16, cols] = main_b
        split_geo[16:24, cols] = main - main_a - main_b
        split_geo[24:26, cols] = rest_a
        split_geo[26:28, cols] = rest_b
        split_geo[28:30, cols] = rest - rest_a - rest_b
        split_geo[30:32, cols] = jnp.zeros((2, LANES), F32)

    spread = lax.broadcasted_iota(jnp.int32, (SPLIT, LANES), 0)
    for t in range(TILES):
        low = lax.bitwise_and(slot_ref[t : t + 1, :], SPLIT - 1)
        slot_hot[:, t * LANES : (t + 1) * LANES] = (spread == low).astype(F32).astype(BF16)

    pl.semaphore_wait(barrier, 7)
    first_trade = trade(0, first_out, first_in)
    for copy in first_trade:
        copy.start()

    def relay_copy(step):
        return pltpu.make_async_remote_copy(
            src_ref=outgoing.at[lax.rem(place + step, WIN)],
            dst_ref=incoming.at[step - 1],
            send_sem=relay_send.at[step - 1],
            recv_sem=relay_recv.at[step - 1],
            device_id=(mate(step), layer),
            device_id_type=MESH,
        )

    def arrange(target):
        for t in range(TILES):
            cols = slice(t * LANES, (t + 1) * LANES)
            part = lax.shift_right_logical(slot_ref[t : t + 1, :], 8)
            part = part - (base + target) * TABLE
            values = split_geo[:, cols]
            for g in range(TABLE):
                relay_left[g * 32 : (g + 1) * 32, cols] = jnp.where(
                    part == g, values, 0.0
                ).astype(BF16)
        placed = lax.dot_general(
            relay_left[...], slot_hot[...], NT, preferred_element_type=F32
        )
        for g in range(TABLE):
            block = placed[g * 32 : (g + 1) * 32]
            main = block[0:8] + block[8:16] + block[16:24]
            rest = block[24:26] + block[26:28] + block[28:30]
            for j in range(2):
                cols = slice(j * LANES, (j + 1) * LANES)
                t = 2 * g + j
                outgoing[target, pl.ds(t, 8, stride=TILES), :] = main[:, cols]
                outgoing[target, pl.ds(8 * TILES + t, 2, stride=TILES), :] = rest[:, cols]

    def send_part(step, carry):
        arrange(lax.rem(place + step, WIN))
        relay_copy(step).start()
        return carry

    lax.fori_loop(1, WIN, send_part, 0)
    arrange(place)

    index[...] = jnp.zeros_like(index)
    for e in range(2):
        index[e, 0:TILES] = pairs_ref[e * TILES : (e + 1) * TILES, :]
        for t in range(TILES):
            low = lax.bitwise_and(
                pairs_ref[e * TILES + t : e * TILES + t + 1, :], SPLIT - 1
            )
            at = (e * TILES + t) * LANES
            pair_hot[:, at : at + LANES] = (spread == low).astype(F32).astype(BF16)
    row16 = lax.broadcasted_iota(jnp.int32, (ROWS, LANES), 0)
    tint = jnp.full((ROWS, LANES), -1, jnp.int32)
    for t in range(TILES):
        tint = jnp.where(row16 == t, color_ref[0, t], tint)
    shade[...] = tint

    wide = lax.broadcasted_iota(jnp.int32, (16, 2 * LANES), 1)
    marks = jnp.where(
        lax.broadcasted_iota(jnp.int32, (16, 2 * LANES), 0) == wide // 64,
        lax.bitwise_and(wide, 127) + 1,
        0,
    )
    tall = lax.broadcasted_iota(jnp.int32, (OWN * LANES, LANES), 0)
    listed_hot = jnp.concatenate(
        [(tall == listed[pair]).astype(F32).astype(BF16) for pair in range(2)], axis=1
    )
    found = lax.dot_general(
        marks.astype(F32).astype(BF16), listed_hot, NT, preferred_element_type=F32
    )
    has_lower_sub = (sub > 0).astype(jnp.int32)
    has_higher_sub = (sub < n_sub - 1).astype(jnp.int32)
    has_lower_layer = (layer > 0).astype(jnp.int32)
    has_higher_layer = (layer < n_layer - 1).astype(jnp.int32)
    exists = (has_higher_sub, has_lower_sub, has_higher_layer, has_lower_layer)
    for h in range(OWN):
        cols = slice(h * LANES, (h + 1) * LANES)
        times = jnp.ones((8, LANES), F32)
        for half in range(4):
            spot = jnp.broadcast_to(found[half : half + 1, cols], (8, LANES))
            spot = spot.astype(jnp.int32) * exists[half] - 1
            inverse_list[h * 4 + half] = spot
            times = times + jnp.where(spot >= 0, 1.0, 0.0)
        weight[:, cols] = 1.0 / times
    push[...] = jnp.zeros_like(push)
    impulse[...] = jnp.zeros_like(impulse)
    geo[...] = jnp.ones_like(geo)

    def keep(flag, value):
        return jnp.where(flag > 0, value, 0.0)

    def put_ghosts(landed, rows):
        lane = lane16 if rows == 16 else lane8
        table[0:rows, 512:640] = jnp.where(
            lane < 64, keep(has_lower_sub, landed[0]), keep(has_higher_sub, landed[1])
        )
        table[0:rows, 640:768] = jnp.where(
            lane < 64, keep(has_lower_layer, landed[2]), keep(has_higher_layer, landed[3])
        )

    for copy in first_trade:
        copy.wait_recv()
    put_ghosts([first_in[slot] for slot in range(4)], 16)

    def pick(component, e):
        high = lax.shift_right_logical(index[e], 7)
        low = lax.bitwise_and(index[e], 127)
        got = None
        for h in range(TABLE if e else OWN):
            row = table[component : component + 1, h * LANES : (h + 1) * LANES]
            block = take(jnp.broadcast_to(row, (ROWS, LANES)), low)
            got = block if h == 0 else jnp.where(high == h, block, got)
        return got

    props_a = [pick(8 + i, 0) for i in range(4)]
    props_b = [pick(8 + i, 1) for i in range(4)]
    for i in range(4):
        const[20 + i] = props_a[i]
        const[24 + i] = props_b[i]

    for step in range(1, WIN):
        relay_copy(step).wait_recv()
    for c in range(10):
        rows = slice(c * TILES, (c + 1) * TILES)
        geo[c, 0:TILES] = (
            outgoing[place, rows] + incoming[0, rows] + incoming[1, rows] + incoming[2, rows]
        )

    raw = [geo[i] for i in range(3)]
    length = jnp.sqrt(dot3(raw, raw))
    normal = [r / length for r in raw]
    side = jnp.sqrt(normal[1] * normal[1] + normal[2] * normal[2])
    one_y = normal[2] / side
    one_z = -normal[1] / side
    two = cross(normal, [jnp.zeros_like(side), one_y, one_z])
    frame = [normal, [jnp.zeros_like(side), one_y, one_z], two]
    entry_a = arm_block([geo[3 + i] for i in range(3)], props_a[1:])
    entry_b = arm_block([geo[6 + i] for i in range(3)], props_b[1:])
    mass = props_a[0] + props_b[0]
    xx, yy, zz, xy, xz, yz = [a + b for a, b in zip(entry_a, entry_b)]
    xx, yy, zz = mass + xx, mass + yy, mass + zz
    cxx = yy * zz - yz * yz
    cxy = xz * yz - xy * zz
    cxz = xy * yz - xz * yy
    cyy = xx * zz - xz * xz
    cyz = xy * xz - xx * yz
    czz = xx * yy - xy * xy
    scale = relaxation / (xx * cxx + xy * cxy + xz * cxz)
    solve = [[cxx, cxy, cxz], [cxy, cyy, cyz], [cxz, cyz, czz]]
    for i in range(3):
        row = [dot3(frame[i], solve[j]) * scale for j in range(3)]
        for j in range(3):
            const[8 + 3 * i + j] = row[j]
        const[17 + i] = dot3(row, normal) * geo[9]
    for i in range(3):
        const[i] = normal[i]
        const[5 + i] = two[i]
    const[3] = one_y
    const[4] = one_z

    def color_pass(color, carry):
        vel_a = [pick(c, 0) for c in range(6)]
        vel_b = [pick(c, 1) for c in range(6)]
        arm_a = [geo[3 + i] for i in range(3)]
        arm_b = [geo[6 + i] for i in range(3)]
        turn_a = cross(vel_a[3:], arm_a)
        turn_b = cross(vel_b[3:], arm_b)
        relative = [vel_a[i] + turn_a[i] - vel_b[i] - turn_b[i] for i in range(3)]
        old = [impulse[i] for i in range(3)]
        trial = [
            old[i]
            - dot3([const[8 + 3 * i + j] for j in range(3)], relative)
            - const[17 + i]
            for i in range(3)
        ]
        press = jnp.maximum(trial[0], 0.0)
        slide = jnp.sqrt(trial[1] * trial[1] + trial[2] * trial[2])
        factor = jnp.minimum(1.0, friction * press / jnp.maximum(slide, tangent_floor))
        active = shade[...] == color
        new = [
            jnp.where(active, value, was)
            for value, was in zip([press, trial[1] * factor, trial[2] * factor], old)
        ]
        change = [a - b for a, b in zip(new, old)]
        for i in range(3):
            impulse[i] = new[i]
        force = [
            const[0] * change[0] + const[5] * change[2],
            const[1] * change[0] + const[3] * change[1] + const[6] * change[2],
            const[2] * change[0] + const[4] * change[1] + const[7] * change[2],
        ]
        torque_a = cross(arm_a, force)
        torque_b = cross(arm_b, force)
        for i in range(3):
            lin = slice(i * TILES, (i + 1) * TILES)
            ang = slice((3 + i) * TILES, (4 + i) * TILES)
            push[0, lin] = (const[20] * force[i])[0:TILES]
            push[1, lin] = (-const[24] * force[i])[0:TILES]
            push[0, ang] = (const[21 + i] * torque_a[i])[0:TILES]
            push[1, ang] = (-const[25 + i] * torque_b[i])[0:TILES]
        for e in range(2):
            for t in range(TILES):
                value = push[e, pl.ds(t, 8, stride=TILES), :]
                upper = coarse(value)
                lower = value - upper
                part = lax.shift_right_logical(index[e, t : t + 1], 8)
                pieces = [
                    jnp.where(part == h, half, 0.0) for half in (upper, lower) for h in range(3)
                ]
                at = (e * TILES + t) * LANES
                push_left[:, at : at + LANES] = jnp.concatenate(pieces, axis=0).astype(BF16)
        total = lax.dot_general(
            push_left[...], pair_hot[...], NT, preferred_element_type=F32
        )
        for h in range(3):
            cols = slice(h * SPLIT, (h + 1) * SPLIT)
            table[0:8, cols] = (
                table[0:8, cols]
                + total[h * 8 : (h + 1) * 8]
                + total[24 + h * 8 : 32 + h * 8]
            )
        return carry

    waiting = list(first_trade)
    for sweep in range(SWEEPS):
        start[...] = table[0:8, :]
        lax.fori_loop(0, NCOLOR, color_pass, 0)
        step = 1 + 2 * sweep
        for pair in range(2):
            cols = slice((OWN + pair) * LANES, (OWN + pair + 1) * LANES)
            round_out[step - 1, pair] = table[0:8, cols] - start[:, cols]
        copies = exchange(step)
        for copy in copies:
            copy.start()
        for copy in copies:
            copy.wait_recv()
        waiting += copies
        arrived = [
            jnp.where(lane8 < 64, round_in[step - 1, 1], round_in[step - 1, 0]),
            jnp.where(lane8 < 64, round_in[step - 1, 3], round_in[step - 1, 2]),
        ]
        for h in range(OWN):
            cols = slice(h * LANES, (h + 1) * LANES)
            total = table[0:8, cols] - start[:, cols]
            for half in range(4):
                spot = inverse_list[h * 4 + half]
                total = total + jnp.where(
                    spot >= 0, take(arrived[half // 2], jnp.maximum(spot, 0)), 0.0
                )
            own = start[:, cols] + total * weight[:, cols]
            table[0:8, cols] = own
            if sweep + 1 == SWEEPS:
                vel_out[pl.ds(h, 6, stride=OWN), :] = own[0:6]
        if sweep + 1 < SWEEPS:
            for pair in range(2):
                round_out[step, pair] = pick_listed(pair, 8)
            copies = exchange(step + 1)
            for copy in copies:
                copy.start()
            for copy in copies:
                copy.wait_recv()
            waiting += copies
            put_ghosts([round_in[step, slot] for slot in range(4)], 8)

    for i in range(3):
        imp_out[i * TILES : (i + 1) * TILES, :] = impulse[i, 0:TILES]
    for copy in waiting:
        copy.wait_send()
    for step in range(1, WIN):
        relay_copy(step).wait_send()


def on_device(n_sub, n_layer, geometry, dest_slot, pairs, colors, free_vel, inertia, exports):
    vmem = pl.BlockSpec(memory_space=pltpu.VMEM)
    impulse, velocity = pl.pallas_call(
        lambda *refs: kernel(n_sub, n_layer, *refs),
        out_shape=(
            jax.ShapeDtypeStruct((3 * TILES, LANES), F32),
            jax.ShapeDtypeStruct((6 * OWN, LANES), F32),
        ),
        in_specs=[vmem, vmem, vmem, pl.BlockSpec(memory_space=pltpu.SMEM), vmem, vmem, vmem],
        out_specs=(vmem, vmem),
        scratch_shapes=[
            pltpu.VMEM((SPLIT, TILES * LANES), BF16),
            pltpu.VMEM((SPLIT, 2 * TILES * LANES), BF16),
            pltpu.VMEM((32, TILES * LANES), F32),
            pltpu.VMEM((192, TILES * LANES), BF16),
            pltpu.VMEM((48, 2 * TILES * LANES), BF16),
            pltpu.VMEM((WIN, 10 * TILES, LANES), F32),
            pltpu.VMEM((WIN - 1, 10 * TILES, LANES), F32),
            pltpu.VMEM((10, ROWS, LANES), F32),
            pltpu.VMEM((2, ROWS, LANES), jnp.int32),
            pltpu.VMEM((ROWS, LANES), jnp.int32),
            pltpu.VMEM((28, ROWS, LANES), F32),
            pltpu.VMEM((3, ROWS, LANES), F32),
            pltpu.VMEM((2, 8 * TILES, LANES), F32),
            pltpu.VMEM((16, TABLE * LANES), F32),
            pltpu.VMEM((8, TABLE * LANES), F32),
            pltpu.VMEM((16, 8, LANES), jnp.int32),
            pltpu.VMEM((8, OWN * LANES), F32),
            pltpu.VMEM((2, 16, LANES), F32),
            pltpu.VMEM((4, 16, LANES), F32),
            pltpu.VMEM((5, 2, 8, LANES), F32),
            pltpu.VMEM((5, 4, 8, LANES), F32),
            pltpu.SemaphoreType.DMA((WIN - 1,)),
            pltpu.SemaphoreType.DMA((WIN - 1,)),
            pltpu.SemaphoreType.DMA((6, 4)),
            pltpu.SemaphoreType.DMA((6, 4)),
        ],
        compiler_params=pltpu.CompilerParams(
            collective_id=0, has_side_effects=True, vmem_limit_bytes=24 << 20
        ),
    )(
        geometry.reshape(10 * TILES, LANES),
        dest_slot.reshape(TILES, LANES),
        pairs.reshape(2 * TILES, LANES),
        colors,
        free_vel.reshape(6 * OWN, LANES),
        inertia.reshape(4 * OWN, LANES),
        exports,
    )
    return impulse.reshape(3, 1, TILES * LANES), velocity.reshape(6, 1, OWN * LANES)


def solution(mesh):
    n_sub, n_layer = mesh.shape["sub"], mesh.shape["layer"]
    placed = (
        P(None, "layer", "sub"),
        P("layer", "sub"),
        P(None, "layer", "sub"),
        P("layer", "sub"),
        P(None, "layer", "sub"),
        P(None, "layer", "sub"),
        P(None, "layer", "sub"),
    )
    return jax.shard_map(
        lambda *arrays: on_device(n_sub, n_layer, *arrays),
        mesh=mesh,
        in_specs=placed,
        out_specs=(P(None, "layer", "sub"), P(None, "layer", "sub")),
        check_vma=False,
    )
```

```python
import jax
import jax.numpy as jnp
from jax import lax
from jax.experimental import pallas as pl
from jax.experimental.pallas import tpu as pltpu
from jax.sharding import PartitionSpec as P

WIN = 4
SWEEPS = 3
NCOLOR = 4
LANES = 128
TILES = 12
ROWS = 16
SPLIT = 256
OWN = 4
TABLE = 6

relaxation = 0.7
friction = 0.6
tangent_floor = 0.1

MESH = pl.DeviceIdType.MESH
F32 = jnp.float32
BF16 = jnp.bfloat16
NT = (((1,), (1,)), ((), ()))


def cross(u, v):
    return [
        u[1] * v[2] - u[2] * v[1],
        u[2] * v[0] - u[0] * v[2],
        u[0] * v[1] - u[1] * v[0],
    ]


def dot3(u, v):
    return u[0] * v[0] + u[1] * v[1] + u[2] * v[2]


def take(row_block, index):
    return jnp.take_along_axis(row_block, index, axis=1, mode="promise_in_bounds")


def coarse(value):
    return value.astype(BF16).astype(F32)


def arm_block(arm, spin):
    return [
        spin[1] * arm[2] * arm[2] + spin[2] * arm[1] * arm[1],
        spin[0] * arm[2] * arm[2] + spin[2] * arm[0] * arm[0],
        spin[0] * arm[1] * arm[1] + spin[1] * arm[0] * arm[0],
        -spin[2] * arm[0] * arm[1],
        -spin[1] * arm[0] * arm[2],
        -spin[0] * arm[1] * arm[2],
    ]


def kernel(
    n_sub,
    n_layer,
    geo_hbm,
    slot_hbm,
    pairs_hbm,
    color_hbm,
    free_hbm,
    inertia_hbm,
    exports_hbm,
    imp_out,
    vel_out,
    geo_ref,
    slot_ref,
    pairs_ref,
    color_ref,
    free_ref,
    inertia_ref,
    exports_ref,
    load_sem,
    slot_hot,
    pair_hot,
    split_geo,
    relay_left,
    push_left,
    outgoing,
    incoming,
    geo,
    index,
    shade,
    const,
    impulse,
    push,
    table,
    start,
    inverse_list,
    weight,
    first_out,
    first_in,
    round_out,
    round_in,
    relay_send,
    relay_recv,
    round_send,
    round_recv,
):
    sub = lax.axis_index("sub")
    layer = lax.axis_index("layer")
    base = (sub // WIN) * WIN
    place = sub - base
    lower_sub = lax.rem(sub + n_sub - 1, n_sub)
    higher_sub = lax.rem(sub + 1, n_sub)
    lower_layer = lax.rem(layer + n_layer - 1, n_layer)
    higher_layer = lax.rem(layer + 1, n_layer)

    def mate(step):
        return base + lax.rem(place + step, WIN)

    around = (
        ((lower_sub, layer), 1, 0),
        ((higher_sub, layer), 0, 0),
        ((sub, lower_layer), 3, 1),
        ((sub, higher_layer), 2, 1),
    )

    barrier = pltpu.get_barrier_semaphore()
    for device, _, _ in around:
        pl.semaphore_signal(barrier, inc=1, device_id=device, device_id_type=MESH)
    for step in range(1, WIN):
        pl.semaphore_signal(
            barrier, inc=1, device_id=(mate(step), layer), device_id_type=MESH
        )

    loads = [
        pltpu.make_async_copy(src, dst, load_sem.at[i])
        for i, (src, dst) in enumerate(
            (
                (free_hbm, free_ref),
                (inertia_hbm, inertia_ref),
                (exports_hbm, exports_ref),
                (geo_hbm, geo_ref),
                (slot_hbm.at[:, 0, :], slot_ref),
                (pairs_hbm, pairs_ref),
                (color_hbm, color_ref),
            )
        )
    ]
    for load in loads:
        load.start()

    def trade(step, src, dst):
        return [
            pltpu.make_async_remote_copy(
                src_ref=src.at[pair],
                dst_ref=dst.at[slot],
                send_sem=round_send.at[step, slot],
                recv_sem=round_recv.at[step, slot],
                device_id=device,
                device_id_type=MESH,
            )
            for device, slot, pair in around
        ]

    def exchange(step):
        return trade(step, round_out.at[step - 1], round_in.at[step - 1])

    lane8 = lax.broadcasted_iota(jnp.int32, (8, LANES), 1)
    lane16 = lax.broadcasted_iota(jnp.int32, (ROWS, LANES), 1)

    table[...] = jnp.zeros_like(table)
    for load in loads[0:3]:
        load.wait()
    for h in range(OWN):
        cols = slice(h * LANES, (h + 1) * LANES)
        table[0:6, cols] = free_ref[pl.ds(h, 6, stride=OWN), :]
        table[8:12, cols] = inertia_ref[pl.ds(h, 4, stride=OWN), :]
    listed = [
        jnp.concatenate([exports_ref[1], exports_ref[0]], axis=1),
        jnp.concatenate([exports_ref[3], exports_ref[2]], axis=1),
    ]

    def pick_listed(pair, rows):
        high = jnp.broadcast_to(lax.shift_right_logical(listed[pair], 7), (rows, LANES))
        low = jnp.broadcast_to(lax.bitwise_and(listed[pair], 127), (rows, LANES))
        got = take(table[0:rows, 0:LANES], low)
        for h in range(1, OWN):
            block = take(table[0:rows, h * LANES : (h + 1) * LANES], low)
            got = jnp.where(high == h, block, got)
        return got

    for pair in range(2):
        first_out[pair] = pick_listed(pair, 16)

    for load in loads[3:]:
        load.wait()
    for t in range(TILES):
        cols = slice(t * LANES, (t + 1) * LANES)
        main = geo_ref[pl.ds(t, 8, stride=TILES), :]
        rest = geo_ref[pl.ds(8 * TILES + t, 2, stride=TILES), :]
        main_a = coarse(main)
        main_b = coarse(main - main_a)
        rest_a = coarse(rest)
        rest_b = coarse(rest - rest_a)
        split_geo[0:8, cols] = main_a
        split_geo[8:16, cols] = main_b
        split_geo[16:24, cols] = main - main_a - main_b
        split_geo[24:26, cols] = rest_a
        split_geo[26:28, cols] = rest_b
        split_geo[28:30, cols] = rest - rest_a - rest_b
        split_geo[30:32, cols] = jnp.zeros((2, LANES), F32)

    spread = lax.broadcasted_iota(jnp.int32, (SPLIT, LANES), 0)
    for t in range(TILES):
        low = lax.bitwise_and(slot_ref[t : t + 1, :], SPLIT - 1)
        slot_hot[:, t * LANES : (t + 1) * LANES] = (spread == low).astype(F32).astype(BF16)

    pl.semaphore_wait(barrier, 7)
    first_trade = trade(0, first_out, first_in)
    for copy in first_trade:
        copy.start()

    def relay_copy(step):
        return pltpu.make_async_remote_copy(
            src_ref=outgoing.at[lax.rem(place + step, WIN)],
            dst_ref=incoming.at[step - 1],
            send_sem=relay_send.at[step - 1],
            recv_sem=relay_recv.at[step - 1],
            device_id=(mate(step), layer),
            device_id_type=MESH,
        )

    def arrange(target):
        for t in range(TILES):
            cols = slice(t * LANES, (t + 1) * LANES)
            part = lax.shift_right_logical(slot_ref[t : t + 1, :], 8)
            part = part - (base + target) * TABLE
            values = split_geo[:, cols]
            for g in range(TABLE):
                relay_left[g * 32 : (g + 1) * 32, cols] = jnp.where(
                    part == g, values, 0.0
                ).astype(BF16)
        placed = lax.dot_general(
            relay_left[...], slot_hot[...], NT, preferred_element_type=F32
        )
        for g in range(TABLE):
            block = placed[g * 32 : (g + 1) * 32]
            main = block[0:8] + block[8:16] + block[16:24]
            rest = block[24:26] + block[26:28] + block[28:30]
            for j in range(2):
                cols = slice(j * LANES, (j + 1) * LANES)
                t = 2 * g + j
                outgoing[target, pl.ds(t, 8, stride=TILES), :] = main[:, cols]
                outgoing[target, pl.ds(8 * TILES + t, 2, stride=TILES), :] = rest[:, cols]

    def send_part(step, carry):
        arrange(lax.rem(place + step, WIN))
        relay_copy(step).start()
        return carry

    lax.fori_loop(1, WIN, send_part, 0)
    arrange(place)

    index[...] = jnp.zeros_like(index)
    for e in range(2):
        index[e, 0:TILES] = pairs_ref[e * TILES : (e + 1) * TILES, :]
    upright = jnp.transpose(lax.bitwise_and(pairs_ref[...], SPLIT - 1).astype(F32))
    along = lax.broadcasted_iota(jnp.int32, (LANES, SPLIT), 1).astype(F32)
    for t in range(2 * TILES):
        pair_hot[t * LANES : (t + 1) * LANES, :] = (
            (along == upright[:, t : t + 1]).astype(F32).astype(BF16)
        )
    row16 = lax.broadcasted_iota(jnp.int32, (ROWS, LANES), 0)
    tint = jnp.full((ROWS, LANES), -1, jnp.int32)
    for t in range(TILES):
        tint = jnp.where(row16 == t, color_ref[0, t], tint)
    shade[...] = tint

    wide = lax.broadcasted_iota(jnp.int32, (16, 2 * LANES), 1)
    marks = jnp.where(
        lax.broadcasted_iota(jnp.int32, (16, 2 * LANES), 0) == wide // 64,
        lax.bitwise_and(wide, 127) + 1,
        0,
    )
    tall = lax.broadcasted_iota(jnp.int32, (OWN * LANES, LANES), 0)
    listed_hot = jnp.concatenate(
        [(tall == listed[pair]).astype(F32).astype(BF16) for pair in range(2)], axis=1
    )
    found = lax.dot_general(
        marks.astype(F32).astype(BF16), listed_hot, NT, preferred_element_type=F32
    )
    has_lower_sub = (sub > 0).astype(jnp.int32)
    has_higher_sub = (sub < n_sub - 1).astype(jnp.int32)
    has_lower_layer = (layer > 0).astype(jnp.int32)
    has_higher_layer = (layer < n_layer - 1).astype(jnp.int32)
    exists = (has_higher_sub, has_lower_sub, has_higher_layer, has_lower_layer)
    for h in range(OWN):
        cols = slice(h * LANES, (h + 1) * LANES)
        times = jnp.ones((8, LANES), F32)
        for half in range(4):
            spot = jnp.broadcast_to(found[half : half + 1, cols], (8, LANES))
            spot = spot.astype(jnp.int32) * exists[half] - 1
            inverse_list[h * 4 + half] = spot
            times = times + jnp.where(spot >= 0, 1.0, 0.0)
        weight[:, cols] = 1.0 / times
    push[...] = jnp.zeros_like(push)
    impulse[...] = jnp.zeros_like(impulse)
    geo[...] = jnp.ones_like(geo)

    def keep(flag, value):
        return jnp.where(flag > 0, value, 0.0)

    def put_ghosts(landed, rows):
        lane = lane16 if rows == 16 else lane8
        table[0:rows, 512:640] = jnp.where(
            lane < 64, keep(has_lower_sub, landed[0]), keep(has_higher_sub, landed[1])
        )
        table[0:rows, 640:768] = jnp.where(
            lane < 64, keep(has_lower_layer, landed[2]), keep(has_higher_layer, landed[3])
        )

    for copy in first_trade:
        copy.wait_recv()
    put_ghosts([first_in[slot] for slot in range(4)], 16)

    def pick(component, e):
        high = lax.shift_right_logical(index[e], 7)
        low = lax.bitwise_and(index[e], 127)
        got = None
        for h in range(TABLE if e else OWN):
            row = table[component : component + 1, h * LANES : (h + 1) * LANES]
            block = take(jnp.broadcast_to(row, (ROWS, LANES)), low)
            got = block if h == 0 else jnp.where(high == h, block, got)
        return got

    props_a = [pick(8 + i, 0) for i in range(4)]
    props_b = [pick(8 + i, 1) for i in range(4)]
    for i in range(4):
        const[20 + i] = props_a[i]
        const[24 + i] = props_b[i]

    for step in range(1, WIN):
        relay_copy(step).wait_recv()
    for c in range(10):
        rows = slice(c * TILES, (c + 1) * TILES)
        geo[c, 0:TILES] = (
            outgoing[place, rows] + incoming[0, rows] + incoming[1, rows] + incoming[2, rows]
        )

    raw = [geo[i] for i in range(3)]
    length = jnp.sqrt(dot3(raw, raw))
    normal = [r / length for r in raw]
    side = jnp.sqrt(normal[1] * normal[1] + normal[2] * normal[2])
    one_y = normal[2] / side
    one_z = -normal[1] / side
    two = cross(normal, [jnp.zeros_like(side), one_y, one_z])
    frame = [normal, [jnp.zeros_like(side), one_y, one_z], two]
    entry_a = arm_block([geo[3 + i] for i in range(3)], props_a[1:])
    entry_b = arm_block([geo[6 + i] for i in range(3)], props_b[1:])
    mass = props_a[0] + props_b[0]
    xx, yy, zz, xy, xz, yz = [a + b for a, b in zip(entry_a, entry_b)]
    xx, yy, zz = mass + xx, mass + yy, mass + zz
    cxx = yy * zz - yz * yz
    cxy = xz * yz - xy * zz
    cxz = xy * yz - xz * yy
    cyy = xx * zz - xz * xz
    cyz = xy * xz - xx * yz
    czz = xx * yy - xy * xy
    scale = relaxation / (xx * cxx + xy * cxy + xz * cxz)
    solve = [[cxx, cxy, cxz], [cxy, cyy, cyz], [cxz, cyz, czz]]
    for i in range(3):
        row = [dot3(frame[i], solve[j]) * scale for j in range(3)]
        for j in range(3):
            const[8 + 3 * i + j] = row[j]
        const[17 + i] = dot3(row, normal) * geo[9]
    for i in range(3):
        const[i] = normal[i]
        const[5 + i] = two[i]
    const[3] = one_y
    const[4] = one_z

    def color_pass(color, carry):
        vel_a = [pick(c, 0) for c in range(6)]
        vel_b = [pick(c, 1) for c in range(6)]
        arm_a = [geo[3 + i] for i in range(3)]
        arm_b = [geo[6 + i] for i in range(3)]
        turn_a = cross(vel_a[3:], arm_a)
        turn_b = cross(vel_b[3:], arm_b)
        relative = [vel_a[i] + turn_a[i] - vel_b[i] - turn_b[i] for i in range(3)]
        old = [impulse[i] for i in range(3)]
        trial = [
            old[i]
            - dot3([const[8 + 3 * i + j] for j in range(3)], relative)
            - const[17 + i]
            for i in range(3)
        ]
        press = jnp.maximum(trial[0], 0.0)
        slide = jnp.sqrt(trial[1] * trial[1] + trial[2] * trial[2])
        factor = jnp.minimum(1.0, friction * press / jnp.maximum(slide, tangent_floor))
        active = shade[...] == color
        new = [
            jnp.where(active, value, was)
            for value, was in zip([press, trial[1] * factor, trial[2] * factor], old)
        ]
        change = [a - b for a, b in zip(new, old)]
        for i in range(3):
            impulse[i] = new[i]
        force = [
            const[0] * change[0] + const[5] * change[2],
            const[1] * change[0] + const[3] * change[1] + const[6] * change[2],
            const[2] * change[0] + const[4] * change[1] + const[7] * change[2],
        ]
        torque_a = cross(arm_a, force)
        torque_b = cross(arm_b, force)
        for i in range(3):
            lin = slice(i * TILES, (i + 1) * TILES)
            ang = slice((3 + i) * TILES, (4 + i) * TILES)
            push[0, lin] = (const[20] * force[i])[0:TILES]
            push[1, lin] = (-const[24] * force[i])[0:TILES]
            push[0, ang] = (const[21 + i] * torque_a[i])[0:TILES]
            push[1, ang] = (-const[25 + i] * torque_b[i])[0:TILES]
        for e in range(2):
            for t in range(TILES):
                value = push[e, pl.ds(t, 8, stride=TILES), :]
                upper = coarse(value)
                lower = value - upper
                part = lax.shift_right_logical(index[e, t : t + 1], 8)
                pieces = [
                    jnp.where(part == h, half, 0.0) for half in (upper, lower) for h in range(3)
                ]
                at = (e * TILES + t) * LANES
                push_left[:, at : at + LANES] = jnp.concatenate(pieces, axis=0).astype(BF16)
        total = jnp.dot(push_left[...], pair_hot[...], preferred_element_type=F32)
        for h in range(3):
            cols = slice(h * SPLIT, (h + 1) * SPLIT)
            table[0:8, cols] = (
                table[0:8, cols]
                + total[h * 8 : (h + 1) * 8]
                + total[24 + h * 8 : 32 + h * 8]
            )
        return carry

    def one_sweep(sweep, carry):
        start[...] = table[0:8, :]
        lax.fori_loop(0, NCOLOR, color_pass, 0)
        step = 1 + 2 * sweep
        for pair in range(2):
            cols = slice((OWN + pair) * LANES, (OWN + pair + 1) * LANES)
            round_out[step - 1, pair] = table[0:8, cols] - start[:, cols]
        copies = exchange(step)
        for copy in copies:
            copy.start()
        for copy in copies:
            copy.wait_recv()
        arrived = [
            jnp.where(lane8 < 64, round_in[step - 1, 1], round_in[step - 1, 0]),
            jnp.where(lane8 < 64, round_in[step - 1, 3], round_in[step - 1, 2]),
        ]
        for h in range(OWN):
            cols = slice(h * LANES, (h + 1) * LANES)
            total = table[0:8, cols] - start[:, cols]
            for half in range(4):
                spot = inverse_list[h * 4 + half]
                total = total + jnp.where(
                    spot >= 0, take(arrived[half // 2], jnp.maximum(spot, 0)), 0.0
                )
            table[0:8, cols] = start[:, cols] + total * weight[:, cols]
        for copy in copies:
            copy.wait_send()

        @pl.when(sweep + 1 < SWEEPS)
        def _():
            for pair in range(2):
                round_out[step, pair] = pick_listed(pair, 8)
            back = exchange(step + 1)
            for copy in back:
                copy.start()
            for copy in back:
                copy.wait_recv()
            put_ghosts([round_in[step, slot] for slot in range(4)], 8)
            for copy in back:
                copy.wait_send()

        return carry

    lax.fori_loop(0, SWEEPS, one_sweep, 0)
    for h in range(OWN):
        vel_out[pl.ds(h, 6, stride=OWN), :] = table[0:6, h * LANES : (h + 1) * LANES]
    for i in range(3):
        imp_out[i * TILES : (i + 1) * TILES, :] = impulse[i, 0:TILES]
    for copy in first_trade:
        copy.wait_send()
    for step in range(1, WIN):
        relay_copy(step).wait_send()


def on_device(n_sub, n_layer, geometry, dest_slot, pairs, colors, free_vel, inertia, exports):
    vmem = pl.BlockSpec(memory_space=pltpu.VMEM)
    hbm = pl.BlockSpec(memory_space=pltpu.HBM)
    impulse, velocity = pl.pallas_call(
        lambda *refs: kernel(n_sub, n_layer, *refs),
        out_shape=(
            jax.ShapeDtypeStruct((3 * TILES, LANES), F32),
            jax.ShapeDtypeStruct((6 * OWN, LANES), F32),
        ),
        in_specs=[hbm] * 7,
        out_specs=(vmem, vmem),
        scratch_shapes=[
            pltpu.VMEM((10 * TILES, LANES), F32),
            pltpu.VMEM((TILES, LANES), jnp.int32),
            pltpu.VMEM((2 * TILES, LANES), jnp.int32),
            pltpu.SMEM((1, TILES), jnp.int32),
            pltpu.VMEM((6 * OWN, LANES), F32),
            pltpu.VMEM((4 * OWN, LANES), F32),
            pltpu.VMEM((4, 1, 64), jnp.int32),
            pltpu.SemaphoreType.DMA((7,)),
            pltpu.VMEM((SPLIT, TILES * LANES), BF16),
            pltpu.VMEM((2 * TILES * LANES, SPLIT), BF16),
            pltpu.VMEM((32, TILES * LANES), F32),
            pltpu.VMEM((192, TILES * LANES), BF16),
            pltpu.VMEM((48, 2 * TILES * LANES), BF16),
            pltpu.VMEM((WIN, 10 * TILES, LANES), F32),
            pltpu.VMEM((WIN - 1, 10 * TILES, LANES), F32),
            pltpu.VMEM((10, ROWS, LANES), F32),
            pltpu.VMEM((2, ROWS, LANES), jnp.int32),
            pltpu.VMEM((ROWS, LANES), jnp.int32),
            pltpu.VMEM((28, ROWS, LANES), F32),
            pltpu.VMEM((3, ROWS, LANES), F32),
            pltpu.VMEM((2, 8 * TILES, LANES), F32),
            pltpu.VMEM((16, TABLE * LANES), F32),
            pltpu.VMEM((8, TABLE * LANES), F32),
            pltpu.VMEM((16, 8, LANES), jnp.int32),
            pltpu.VMEM((8, OWN * LANES), F32),
            pltpu.VMEM((2, 16, LANES), F32),
            pltpu.VMEM((4, 16, LANES), F32),
            pltpu.VMEM((5, 2, 8, LANES), F32),
            pltpu.VMEM((5, 4, 8, LANES), F32),
            pltpu.SemaphoreType.DMA((WIN - 1,)),
            pltpu.SemaphoreType.DMA((WIN - 1,)),
            pltpu.SemaphoreType.DMA((6, 4)),
            pltpu.SemaphoreType.DMA((6, 4)),
        ],
        compiler_params=pltpu.CompilerParams(
            collective_id=0, has_side_effects=True, vmem_limit_bytes=60 << 20
        ),
    )(
        geometry.reshape(10 * TILES, LANES),
        dest_slot.reshape(TILES, 1, LANES),
        pairs.reshape(2 * TILES, LANES),
        colors,
        free_vel.reshape(6 * OWN, LANES),
        inertia.reshape(4 * OWN, LANES),
        exports,
    )
    return impulse.reshape(3, 1, TILES * LANES), velocity.reshape(6, 1, OWN * LANES)


def solution(mesh):
    n_sub, n_layer = mesh.shape["sub"], mesh.shape["layer"]
    placed = (
        P(None, "layer", "sub"),
        P("layer", "sub"),
        P(None, "layer", "sub"),
        P("layer", "sub"),
        P(None, "layer", "sub"),
        P(None, "layer", "sub"),
        P(None, "layer", "sub"),
    )
    return jax.shard_map(
        lambda *arrays: on_device(n_sub, n_layer, *arrays),
        mesh=mesh,
        in_specs=placed,
        out_specs=(P(None, "layer", "sub"), P(None, "layer", "sub")),
        check_vma=False,
    )
```

```python
import jax
import jax.numpy as jnp
from jax import lax
from jax.experimental import pallas as pl
from jax.experimental.pallas import tpu as pltpu
from jax.sharding import PartitionSpec as P

WIN = 4
SWEEPS = 3
NCOLOR = 4
LANES = 128
TILES = 12
ROWS = 16
SPLIT = 256
OWN = 4
TABLE = 6

relaxation = 0.7
friction = 0.6
tangent_floor = 0.1

FAR = ((-2, 0), (2, 0), (0, -2), (0, 2), (-1, -1), (-1, 1), (1, -1), (1, 1))
MESH = pl.DeviceIdType.MESH
F32 = jnp.float32
BF16 = jnp.bfloat16
NT = (((1,), (1,)), ((), ()))


def cross(u, v):
    return [
        u[1] * v[2] - u[2] * v[1],
        u[2] * v[0] - u[0] * v[2],
        u[0] * v[1] - u[1] * v[0],
    ]


def dot3(u, v):
    return u[0] * v[0] + u[1] * v[1] + u[2] * v[2]


def take(row_block, index):
    return jnp.take_along_axis(row_block, index, axis=1, mode="promise_in_bounds")


def coarse(value):
    return value.astype(BF16).astype(F32)


def arm_block(arm, spin):
    return [
        spin[1] * arm[2] * arm[2] + spin[2] * arm[1] * arm[1],
        spin[0] * arm[2] * arm[2] + spin[2] * arm[0] * arm[0],
        spin[0] * arm[1] * arm[1] + spin[1] * arm[0] * arm[0],
        -spin[2] * arm[0] * arm[1],
        -spin[1] * arm[0] * arm[2],
        -spin[0] * arm[1] * arm[2],
    ]


def kernel(
    n_sub,
    n_layer,
    geo_hbm,
    slot_hbm,
    pairs_hbm,
    color_hbm,
    free_hbm,
    inertia_hbm,
    exports_hbm,
    imp_out,
    vel_out,
    geo_ref,
    slot_ref,
    pairs_ref,
    color_ref,
    free_ref,
    inertia_ref,
    exports_ref,
    load_sem,
    slot_hot,
    pair_hot,
    split_geo,
    relay_left,
    push_left,
    outgoing,
    incoming,
    geo,
    index,
    shade,
    const,
    impulse,
    push,
    table,
    start,
    inverse_list,
    weight,
    first_out,
    first_in,
    info,
    info_out,
    info_in,
    hints,
    sweep_out,
    near_in,
    far_in,
    relay_send,
    relay_recv,
    near_send,
    near_recv,
    far_send,
    far_recv,
):
    sub = lax.axis_index("sub")
    layer = lax.axis_index("layer")
    base = (sub // WIN) * WIN
    place = sub - base
    lower_sub = lax.rem(sub + n_sub - 1, n_sub)
    higher_sub = lax.rem(sub + 1, n_sub)
    lower_layer = lax.rem(layer + n_layer - 1, n_layer)
    higher_layer = lax.rem(layer + 1, n_layer)

    def mate(step):
        return base + lax.rem(place + step, WIN)

    around = (
        ((lower_sub, layer), 1, 0),
        ((higher_sub, layer), 0, 0),
        ((sub, lower_layer), 3, 1),
        ((sub, higher_layer), 2, 1),
    )

    far = tuple(
        (
            (lax.rem(sub + n_sub + right, n_sub), lax.rem(layer + n_layer + up, n_layer)),
            FAR.index((-right, -up)),
            2 if right == 0 else 1,
            1 if right == 0 or up == 0 else 2,
        )
        for right, up in FAR
    )

    barrier = pltpu.get_barrier_semaphore()
    for device in [a[0] for a in around] + [f[0] for f in far]:
        pl.semaphore_signal(barrier, inc=1, device_id=device, device_id_type=MESH)
    for step in range(1, WIN):
        pl.semaphore_signal(
            barrier, inc=1, device_id=(mate(step), layer), device_id_type=MESH
        )

    loads = [
        pltpu.make_async_copy(src, dst, load_sem.at[i])
        for i, (src, dst) in enumerate(
            (
                (free_hbm, free_ref),
                (inertia_hbm, inertia_ref),
                (exports_hbm, exports_ref),
                (geo_hbm, geo_ref),
                (slot_hbm.at[:, 0, :], slot_ref),
                (pairs_hbm, pairs_ref),
                (color_hbm, color_ref),
            )
        )
    ]
    for load in loads:
        load.start()

    def trade(step, source_of, dst):
        return [
            pltpu.make_async_remote_copy(
                src_ref=source_of(pair),
                dst_ref=dst.at[slot],
                send_sem=near_send.at[step, slot],
                recv_sem=near_recv.at[step, slot],
                device_id=device,
                device_id_type=MESH,
            )
            for device, slot, pair in around
        ]

    def near_copies(sweep):
        return trade(
            2 + sweep, lambda pair: sweep_out.at[sweep, pl.ds(2 * pair, 2)], near_in.at[sweep]
        )

    def far_copies(sweep):
        return [
            pltpu.make_async_remote_copy(
                src_ref=sweep_out.at[sweep, pl.ds(first, count)],
                dst_ref=far_in.at[sweep, slot, pl.ds(0, count)],
                send_sem=far_send.at[sweep, slot],
                recv_sem=far_recv.at[sweep, slot],
                device_id=device,
                device_id_type=MESH,
            )
            for device, slot, first, count in far
        ]

    lane8 = lax.broadcasted_iota(jnp.int32, (8, LANES), 1)
    lane16 = lax.broadcasted_iota(jnp.int32, (ROWS, LANES), 1)

    table[...] = jnp.zeros_like(table)
    for load in loads[0:3]:
        load.wait()
    for h in range(OWN):
        cols = slice(h * LANES, (h + 1) * LANES)
        table[0:6, cols] = free_ref[pl.ds(h, 6, stride=OWN), :]
        table[8:12, cols] = inertia_ref[pl.ds(h, 4, stride=OWN), :]
    listed = [
        jnp.concatenate([exports_ref[1], exports_ref[0]], axis=1),
        jnp.concatenate([exports_ref[3], exports_ref[2]], axis=1),
    ]

    def pick_listed(pair, rows, source=table):
        high = jnp.broadcast_to(lax.shift_right_logical(listed[pair], 7), (rows, LANES))
        low = jnp.broadcast_to(lax.bitwise_and(listed[pair], 127), (rows, LANES))
        got = take(source[0:rows, 0:LANES], low)
        for h in range(1, OWN):
            block = take(source[0:rows, h * LANES : (h + 1) * LANES], low)
            got = jnp.where(high == h, block, got)
        return got

    for pair in range(2):
        first_out[pair] = pick_listed(pair, 16)

    for load in loads[3:]:
        load.wait()
    for t in range(TILES):
        cols = slice(t * LANES, (t + 1) * LANES)
        main = geo_ref[pl.ds(t, 8, stride=TILES), :]
        rest = geo_ref[pl.ds(8 * TILES + t, 2, stride=TILES), :]
        main_a = coarse(main)
        main_b = coarse(main - main_a)
        rest_a = coarse(rest)
        rest_b = coarse(rest - rest_a)
        split_geo[0:8, cols] = main_a
        split_geo[8:16, cols] = main_b
        split_geo[16:24, cols] = main - main_a - main_b
        split_geo[24:26, cols] = rest_a
        split_geo[26:28, cols] = rest_b
        split_geo[28:30, cols] = rest - rest_a - rest_b
        split_geo[30:32, cols] = jnp.zeros((2, LANES), F32)

    spread = lax.broadcasted_iota(jnp.int32, (SPLIT, LANES), 0)
    for t in range(TILES):
        low = lax.bitwise_and(slot_ref[t : t + 1, :], SPLIT - 1)
        slot_hot[:, t * LANES : (t + 1) * LANES] = (spread == low).astype(F32).astype(BF16)

    pl.semaphore_wait(barrier, 15)
    first_trade = trade(0, lambda pair: first_out.at[pair], first_in)
    for copy in first_trade:
        copy.start()

    def relay_copy(step):
        return pltpu.make_async_remote_copy(
            src_ref=outgoing.at[lax.rem(place + step, WIN)],
            dst_ref=incoming.at[step - 1],
            send_sem=relay_send.at[step - 1],
            recv_sem=relay_recv.at[step - 1],
            device_id=(mate(step), layer),
            device_id_type=MESH,
        )

    def arrange(target):
        for t in range(TILES):
            cols = slice(t * LANES, (t + 1) * LANES)
            part = lax.shift_right_logical(slot_ref[t : t + 1, :], 8)
            part = part - (base + target) * TABLE
            values = split_geo[:, cols]
            for g in range(TABLE):
                relay_left[g * 32 : (g + 1) * 32, cols] = jnp.where(
                    part == g, values, 0.0
                ).astype(BF16)
        placed = lax.dot_general(
            relay_left[...], slot_hot[...], NT, preferred_element_type=F32
        )
        for g in range(TABLE):
            block = placed[g * 32 : (g + 1) * 32]
            main = block[0:8] + block[8:16] + block[16:24]
            rest = block[24:26] + block[26:28] + block[28:30]
            for j in range(2):
                cols = slice(j * LANES, (j + 1) * LANES)
                t = 2 * g + j
                outgoing[target, pl.ds(t, 8, stride=TILES), :] = main[:, cols]
                outgoing[target, pl.ds(8 * TILES + t, 2, stride=TILES), :] = rest[:, cols]

    def send_part(step, carry):
        arrange(lax.rem(place + step, WIN))
        relay_copy(step).start()
        return carry

    lax.fori_loop(1, WIN, send_part, 0)
    arrange(place)

    index[...] = jnp.zeros_like(index)
    for e in range(2):
        index[e, 0:TILES] = pairs_ref[e * TILES : (e + 1) * TILES, :]
    upright = jnp.transpose(lax.bitwise_and(pairs_ref[...], SPLIT - 1).astype(F32))
    along = lax.broadcasted_iota(jnp.int32, (LANES, SPLIT), 1).astype(F32)
    for t in range(2 * TILES):
        pair_hot[t * LANES : (t + 1) * LANES, :] = (
            (along == upright[:, t : t + 1]).astype(F32).astype(BF16)
        )
    row16 = lax.broadcasted_iota(jnp.int32, (ROWS, LANES), 0)
    tint = jnp.full((ROWS, LANES), -1, jnp.int32)
    for t in range(TILES):
        tint = jnp.where(row16 == t, color_ref[0, t], tint)
    shade[...] = tint

    wide = lax.broadcasted_iota(jnp.int32, (16, 2 * LANES), 1)
    marks = jnp.where(
        lax.broadcasted_iota(jnp.int32, (16, 2 * LANES), 0) == wide // 64,
        lax.bitwise_and(wide, 127) + 1,
        0,
    )
    tall = lax.broadcasted_iota(jnp.int32, (OWN * LANES, LANES), 0)
    listed_hot = jnp.concatenate(
        [(tall == listed[pair]).astype(F32).astype(BF16) for pair in range(2)], axis=1
    )
    found = lax.dot_general(
        marks.astype(F32).astype(BF16), listed_hot, NT, preferred_element_type=F32
    )
    has_lower_sub = (sub > 0).astype(jnp.int32)
    has_higher_sub = (sub < n_sub - 1).astype(jnp.int32)
    has_lower_layer = (layer > 0).astype(jnp.int32)
    has_higher_layer = (layer < n_layer - 1).astype(jnp.int32)
    exists = (has_higher_sub, has_lower_sub, has_higher_layer, has_lower_layer)
    for h in range(OWN):
        cols = slice(h * LANES, (h + 1) * LANES)
        times = jnp.ones((8, LANES), F32)
        for half in range(4):
            spot = jnp.broadcast_to(found[half : half + 1, cols], (8, LANES))
            spot = spot.astype(jnp.int32) * exists[half] - 1
            inverse_list[h * 4 + half] = spot
            info[half : half + 1, cols] = spot[0:1].astype(F32)
            times = times + jnp.where(spot >= 0, 1.0, 0.0)
        weight[:, cols] = 1.0 / times
        info[4:8, cols] = (1.0 / times)[0:4]
    for pair in range(2):
        info_out[pair] = pick_listed(pair, 8, info)
    info_trade = trade(1, lambda pair: info_out.at[pair], info_in)
    for copy in info_trade:
        copy.start()
    push[...] = jnp.zeros_like(push)
    impulse[...] = jnp.zeros_like(impulse)
    geo[...] = jnp.ones_like(geo)

    def keep(flag, value):
        return jnp.where(flag > 0, value, 0.0)

    def halves(lane, landed):
        return (
            jnp.where(
                lane < 64, keep(has_lower_sub, landed[0]), keep(has_higher_sub, landed[1])
            ),
            jnp.where(
                lane < 64, keep(has_lower_layer, landed[2]), keep(has_higher_layer, landed[3])
            ),
        )

    for copy in first_trade:
        copy.wait_recv()
    table[:, 512:640], table[:, 640:768] = halves(lane16, [first_in[slot] for slot in range(4)])

    def pick(component, e):
        high = lax.shift_right_logical(index[e], 7)
        low = lax.bitwise_and(index[e], 127)
        got = None
        for h in range(TABLE if e else OWN):
            row = table[component : component + 1, h * LANES : (h + 1) * LANES]
            block = take(jnp.broadcast_to(row, (ROWS, LANES)), low)
            got = block if h == 0 else jnp.where(high == h, block, got)
        return got

    props_a = [pick(8 + i, 0) for i in range(4)]
    props_b = [pick(8 + i, 1) for i in range(4)]
    for i in range(4):
        const[20 + i] = props_a[i]
        const[24 + i] = props_b[i]

    for step in range(1, WIN):
        relay_copy(step).wait_recv()
    for c in range(10):
        rows = slice(c * TILES, (c + 1) * TILES)
        geo[c, 0:TILES] = (
            outgoing[place, rows] + incoming[0, rows] + incoming[1, rows] + incoming[2, rows]
        )

    raw = [geo[i] for i in range(3)]
    length = jnp.sqrt(dot3(raw, raw))
    normal = [r / length for r in raw]
    side = jnp.sqrt(normal[1] * normal[1] + normal[2] * normal[2])
    one_y = normal[2] / side
    one_z = -normal[1] / side
    two = cross(normal, [jnp.zeros_like(side), one_y, one_z])
    frame = [normal, [jnp.zeros_like(side), one_y, one_z], two]
    entry_a = arm_block([geo[3 + i] for i in range(3)], props_a[1:])
    entry_b = arm_block([geo[6 + i] for i in range(3)], props_b[1:])
    mass = props_a[0] + props_b[0]
    xx, yy, zz, xy, xz, yz = [a + b for a, b in zip(entry_a, entry_b)]
    xx, yy, zz = mass + xx, mass + yy, mass + zz
    cxx = yy * zz - yz * yz
    cxy = xz * yz - xy * zz
    cxz = xy * yz - xz * yy
    cyy = xx * zz - xz * xz
    cyz = xy * xz - xx * yz
    czz = xx * yy - xy * xy
    scale = relaxation / (xx * cxx + xy * cxy + xz * cxz)
    solve = [[cxx, cxy, cxz], [cxy, cyy, cyz], [cxz, cyz, czz]]
    for i in range(3):
        row = [dot3(frame[i], solve[j]) * scale for j in range(3)]
        for j in range(3):
            const[8 + 3 * i + j] = row[j]
        const[17 + i] = dot3(row, normal) * geo[9]
    for i in range(3):
        const[i] = normal[i]
        const[5 + i] = two[i]
    const[3] = one_y
    const[4] = one_z

    def color_pass(color, carry):
        vel_a = [pick(c, 0) for c in range(6)]
        vel_b = [pick(c, 1) for c in range(6)]
        arm_a = [geo[3 + i] for i in range(3)]
        arm_b = [geo[6 + i] for i in range(3)]
        turn_a = cross(vel_a[3:], arm_a)
        turn_b = cross(vel_b[3:], arm_b)
        relative = [vel_a[i] + turn_a[i] - vel_b[i] - turn_b[i] for i in range(3)]
        old = [impulse[i] for i in range(3)]
        trial = [
            old[i]
            - dot3([const[8 + 3 * i + j] for j in range(3)], relative)
            - const[17 + i]
            for i in range(3)
        ]
        press = jnp.maximum(trial[0], 0.0)
        slide = jnp.sqrt(trial[1] * trial[1] + trial[2] * trial[2])
        factor = jnp.minimum(1.0, friction * press / jnp.maximum(slide, tangent_floor))
        active = shade[...] == color
        new = [
            jnp.where(active, value, was)
            for value, was in zip([press, trial[1] * factor, trial[2] * factor], old)
        ]
        change = [a - b for a, b in zip(new, old)]
        for i in range(3):
            impulse[i] = new[i]
        force = [
            const[0] * change[0] + const[5] * change[2],
            const[1] * change[0] + const[3] * change[1] + const[6] * change[2],
            const[2] * change[0] + const[4] * change[1] + const[7] * change[2],
        ]
        torque_a = cross(arm_a, force)
        torque_b = cross(arm_b, force)
        for i in range(3):
            lin = slice(i * TILES, (i + 1) * TILES)
            ang = slice((3 + i) * TILES, (4 + i) * TILES)
            push[0, lin] = (const[20] * force[i])[0:TILES]
            push[1, lin] = (-const[24] * force[i])[0:TILES]
            push[0, ang] = (const[21 + i] * torque_a[i])[0:TILES]
            push[1, ang] = (-const[25 + i] * torque_b[i])[0:TILES]
        for e in range(2):
            for t in range(TILES):
                value = push[e, pl.ds(t, 8, stride=TILES), :]
                upper = coarse(value)
                lower = value - upper
                part = lax.shift_right_logical(index[e, t : t + 1], 8)
                pieces = [
                    jnp.where(part == h, half, 0.0) for half in (upper, lower) for h in range(3)
                ]
                at = (e * TILES + t) * LANES
                push_left[:, at : at + LANES] = jnp.concatenate(pieces, axis=0).astype(BF16)
        total = jnp.dot(push_left[...], pair_hot[...], preferred_element_type=F32)
        for h in range(3):
            cols = slice(h * SPLIT, (h + 1) * SPLIT)
            table[0:8, cols] = (
                table[0:8, cols]
                + total[h * 8 : (h + 1) * 8]
                + total[24 + h * 8 : 32 + h * 8]
            )
        return carry

    for copy in info_trade:
        copy.wait_recv()
    hints[0], hints[1] = halves(lane8, [info_in[slot] for slot in range(4)])

    def pull(row_block, pair, row):
        spot = jnp.broadcast_to(hints[pair, row : row + 1], (8, LANES)).astype(jnp.int32)
        return jnp.where(spot >= 0, take(row_block, jnp.maximum(spot, 0)), 0.0)

    def one_sweep(sweep, carry):
        start[...] = table[0:8, :]
        lax.fori_loop(0, NCOLOR, color_pass, 0)
        on = sweep + 1 < SWEEPS
        copied = [slice((OWN + pair) * LANES, (OWN + pair + 1) * LANES) for pair in range(2)]
        for pair in range(2):
            sweep_out[sweep, 1 + pair] = table[0:8, copied[pair]] - start[:, copied[pair]]

        @pl.when(on)
        def _():
            for copy in far_copies(sweep):
                copy.start()

        for pair in range(2):
            sweep_out[sweep, 3 * pair] = pick_listed(pair, 8)
        near = near_copies(sweep)
        for copy in near:
            copy.start()
        for copy in near:
            copy.wait_recv()
        arrived = [
            jnp.where(lane8 < 64, near_in[sweep, 1, 1], near_in[sweep, 0, 1]),
            jnp.where(lane8 < 64, near_in[sweep, 3, 0], near_in[sweep, 2, 0]),
        ]
        for h in range(OWN):
            cols = slice(h * LANES, (h + 1) * LANES)
            total = table[0:8, cols] - start[:, cols]
            for half in range(4):
                spot = inverse_list[h * 4 + half]
                total = total + jnp.where(
                    spot >= 0, take(arrived[half // 2], jnp.maximum(spot, 0)), 0.0
                )
            table[0:8, cols] = start[:, cols] + total * weight[:, cols]

        @pl.when(on)
        def _():
            for copy in far_copies(sweep):
                copy.wait_recv()

            def landed(right, up, pair):
                straight = right == 0 or up == 0
                return far_in[sweep, FAR.index((right, up)), 0 if straight else pair]

            left = lane8 < 64
            for pair in range(2):
                if pair == 0:
                    listed_now = jnp.where(left, near_in[sweep, 0, 0], near_in[sweep, 1, 0])
                    beyond = jnp.where(left, landed(2, 0, 0), landed(-2, 0, 0))
                    side_a = jnp.where(left, landed(-1, 1, 1), landed(-1, -1, 1))
                    side_b = jnp.where(left, landed(1, 1, 1), landed(1, -1, 1))
                else:
                    listed_now = jnp.where(left, near_in[sweep, 2, 1], near_in[sweep, 3, 1])
                    beyond = jnp.where(left, landed(0, 2, 1), landed(0, -2, 1))
                    side_a = jnp.where(left, landed(1, -1, 0), landed(-1, -1, 0))
                    side_b = jnp.where(left, landed(1, 1, 0), landed(-1, 1, 0))
                was = start[:, copied[pair]]
                total = (listed_now - was) + sweep_out[sweep, 1 + pair]
                total = total + jnp.where(
                    left, pull(beyond, pair, 2 * pair + 1), pull(beyond, pair, 2 * pair)
                )
                for row in (2 - 2 * pair, 3 - 2 * pair):
                    total = total + jnp.where(
                        left, pull(side_a, pair, row), pull(side_b, pair, row)
                    )
                table[0:8, copied[pair]] = was + total * hints[pair, 4:5]
            for copy in far_copies(sweep):
                copy.wait_send()

        for copy in near:
            copy.wait_send()
        return carry

    lax.fori_loop(0, SWEEPS, one_sweep, 0)
    for h in range(OWN):
        vel_out[pl.ds(h, 6, stride=OWN), :] = table[0:6, h * LANES : (h + 1) * LANES]
    for i in range(3):
        imp_out[i * TILES : (i + 1) * TILES, :] = impulse[i, 0:TILES]
    for copy in first_trade + info_trade:
        copy.wait_send()
    for step in range(1, WIN):
        relay_copy(step).wait_send()


def on_device(n_sub, n_layer, geometry, dest_slot, pairs, colors, free_vel, inertia, exports):
    vmem = pl.BlockSpec(memory_space=pltpu.VMEM)
    hbm = pl.BlockSpec(memory_space=pltpu.HBM)
    impulse, velocity = pl.pallas_call(
        lambda *refs: kernel(n_sub, n_layer, *refs),
        out_shape=(
            jax.ShapeDtypeStruct((3 * TILES, LANES), F32),
            jax.ShapeDtypeStruct((6 * OWN, LANES), F32),
        ),
        in_specs=[hbm] * 7,
        out_specs=(vmem, vmem),
        scratch_shapes=[
            pltpu.VMEM((10 * TILES, LANES), F32),
            pltpu.VMEM((TILES, LANES), jnp.int32),
            pltpu.VMEM((2 * TILES, LANES), jnp.int32),
            pltpu.SMEM((1, TILES), jnp.int32),
            pltpu.VMEM((6 * OWN, LANES), F32),
            pltpu.VMEM((4 * OWN, LANES), F32),
            pltpu.VMEM((4, 1, 64), jnp.int32),
            pltpu.SemaphoreType.DMA((7,)),
            pltpu.VMEM((SPLIT, TILES * LANES), BF16),
            pltpu.VMEM((2 * TILES * LANES, SPLIT), BF16),
            pltpu.VMEM((32, TILES * LANES), F32),
            pltpu.VMEM((192, TILES * LANES), BF16),
            pltpu.VMEM((48, 2 * TILES * LANES), BF16),
            pltpu.VMEM((WIN, 10 * TILES, LANES), F32),
            pltpu.VMEM((WIN - 1, 10 * TILES, LANES), F32),
            pltpu.VMEM((10, ROWS, LANES), F32),
            pltpu.VMEM((2, ROWS, LANES), jnp.int32),
            pltpu.VMEM((ROWS, LANES), jnp.int32),
            pltpu.VMEM((28, ROWS, LANES), F32),
            pltpu.VMEM((3, ROWS, LANES), F32),
            pltpu.VMEM((2, 8 * TILES, LANES), F32),
            pltpu.VMEM((16, TABLE * LANES), F32),
            pltpu.VMEM((8, TABLE * LANES), F32),
            pltpu.VMEM((16, 8, LANES), jnp.int32),
            pltpu.VMEM((8, OWN * LANES), F32),
            pltpu.VMEM((2, 16, LANES), F32),
            pltpu.VMEM((4, 16, LANES), F32),
            pltpu.VMEM((8, OWN * LANES), F32),
            pltpu.VMEM((2, 8, LANES), F32),
            pltpu.VMEM((4, 8, LANES), F32),
            pltpu.VMEM((2, 8, LANES), F32),
            pltpu.VMEM((SWEEPS, 4, 8, LANES), F32),
            pltpu.VMEM((SWEEPS, 4, 2, 8, LANES), F32),
            pltpu.VMEM((SWEEPS - 1, 8, 2, 8, LANES), F32),
            pltpu.SemaphoreType.DMA((WIN - 1,)),
            pltpu.SemaphoreType.DMA((WIN - 1,)),
            pltpu.SemaphoreType.DMA((2 + SWEEPS, 4)),
            pltpu.SemaphoreType.DMA((2 + SWEEPS, 4)),
            pltpu.SemaphoreType.DMA((SWEEPS - 1, 8)),
            pltpu.SemaphoreType.DMA((SWEEPS - 1, 8)),
        ],
        compiler_params=pltpu.CompilerParams(
            collective_id=0, has_side_effects=True, vmem_limit_bytes=60 << 20
        ),
    )(
        geometry.reshape(10 * TILES, LANES),
        dest_slot.reshape(TILES, 1, LANES),
        pairs.reshape(2 * TILES, LANES),
        colors,
        free_vel.reshape(6 * OWN, LANES),
        inertia.reshape(4 * OWN, LANES),
        exports,
    )
    return impulse.reshape(3, 1, TILES * LANES), velocity.reshape(6, 1, OWN * LANES)


def solution(mesh):
    n_sub, n_layer = mesh.shape["sub"], mesh.shape["layer"]
    placed = (
        P(None, "layer", "sub"),
        P("layer", "sub"),
        P(None, "layer", "sub"),
        P("layer", "sub"),
        P(None, "layer", "sub"),
        P(None, "layer", "sub"),
        P(None, "layer", "sub"),
    )
    return jax.shard_map(
        lambda *arrays: on_device(n_sub, n_layer, *arrays),
        mesh=mesh,
        in_specs=placed,
        out_specs=(P(None, "layer", "sub"), P(None, "layer", "sub")),
        check_vma=False,
    )
```

```python
import jax
import jax.numpy as jnp
from jax import lax
from jax.experimental import pallas as pl
from jax.experimental.pallas import tpu as pltpu
from jax.sharding import PartitionSpec as P

WIN = 4
SWEEPS = 3
NCOLOR = 4
LANES = 128
TILES = 12
ROWS = 16
SPLIT = 256
OWN = 4
TABLE = 6

relaxation = 0.7
friction = 0.6
tangent_floor = 0.1

FAR = ((-2, 0), (2, 0), (0, -2), (0, 2), (-1, -1), (-1, 1), (1, -1), (1, 1))
MESH = pl.DeviceIdType.MESH
F32 = jnp.float32
BF16 = jnp.bfloat16
NT = (((1,), (1,)), ((), ()))


def cross(u, v):
    return [
        u[1] * v[2] - u[2] * v[1],
        u[2] * v[0] - u[0] * v[2],
        u[0] * v[1] - u[1] * v[0],
    ]


def dot3(u, v):
    return u[0] * v[0] + u[1] * v[1] + u[2] * v[2]


def take(row_block, index):
    return jnp.take_along_axis(row_block, index, axis=1, mode="promise_in_bounds")


def coarse(value):
    return value.astype(BF16).astype(F32)


def arm_block(arm, spin):
    return [
        spin[1] * arm[2] * arm[2] + spin[2] * arm[1] * arm[1],
        spin[0] * arm[2] * arm[2] + spin[2] * arm[0] * arm[0],
        spin[0] * arm[1] * arm[1] + spin[1] * arm[0] * arm[0],
        -spin[2] * arm[0] * arm[1],
        -spin[1] * arm[0] * arm[2],
        -spin[0] * arm[1] * arm[2],
    ]


def kernel(
    n_sub,
    n_layer,
    geo_hbm,
    slot_hbm,
    pairs_hbm,
    color_hbm,
    free_hbm,
    inertia_hbm,
    exports_hbm,
    imp_out,
    vel_out,
    geo_ref,
    slot_ref,
    pairs_ref,
    color_ref,
    free_ref,
    inertia_ref,
    exports_ref,
    load_sem,
    slot_hot,
    pair_hot,
    split_geo,
    relay_left,
    push_left,
    outgoing,
    incoming,
    geo,
    index,
    shade,
    const,
    impulse,
    push,
    table,
    start,
    inverse_list,
    weight,
    first_out,
    first_in,
    info,
    info_out,
    info_in,
    hints,
    sweep_out,
    near_in,
    far_in,
    relay_send,
    relay_recv,
    near_send,
    near_recv,
    far_send,
    far_recv,
):
    sub = lax.axis_index("sub")
    layer = lax.axis_index("layer")
    base = (sub // WIN) * WIN
    place = sub - base
    lower_sub = lax.rem(sub + n_sub - 1, n_sub)
    higher_sub = lax.rem(sub + 1, n_sub)
    lower_layer = lax.rem(layer + n_layer - 1, n_layer)
    higher_layer = lax.rem(layer + 1, n_layer)

    def mate(step):
        return base + lax.rem(place + step, WIN)

    around = (
        ((lower_sub, layer), 1, 0),
        ((higher_sub, layer), 0, 0),
        ((sub, lower_layer), 3, 1),
        ((sub, higher_layer), 2, 1),
    )

    far = tuple(
        (
            (lax.rem(sub + n_sub + right, n_sub), lax.rem(layer + n_layer + up, n_layer)),
            FAR.index((-right, -up)),
            2 if right == 0 else 1,
            1 if right == 0 or up == 0 else 2,
        )
        for right, up in FAR
    )

    barrier = pltpu.get_barrier_semaphore()
    for device, _, _ in around:
        pl.semaphore_signal(barrier, inc=1, device_id=device, device_id_type=MESH)
    for step in range(1, WIN):
        pl.semaphore_signal(
            barrier, inc=1, device_id=(mate(step), layer), device_id_type=MESH
        )

    loads = [
        pltpu.make_async_copy(src, dst, load_sem.at[i])
        for i, (src, dst) in enumerate(
            (
                (free_hbm, free_ref),
                (inertia_hbm, inertia_ref),
                (exports_hbm, exports_ref),
                (geo_hbm, geo_ref),
                (slot_hbm.at[:, 0, :], slot_ref),
                (pairs_hbm, pairs_ref),
                (color_hbm, color_ref),
            )
        )
    ]
    for load in loads:
        load.start()

    def trade(step, source_of, dst):
        return [
            pltpu.make_async_remote_copy(
                src_ref=source_of(pair),
                dst_ref=dst.at[slot],
                send_sem=near_send.at[step, slot],
                recv_sem=near_recv.at[step, slot],
                device_id=device,
                device_id_type=MESH,
            )
            for device, slot, pair in around
        ]

    def near_copies(sweep):
        return trade(
            2 + sweep, lambda pair: sweep_out.at[sweep, pl.ds(2 * pair, 2)], near_in.at[sweep]
        )

    def far_copies(sweep):
        return [
            pltpu.make_async_remote_copy(
                src_ref=sweep_out.at[sweep, pl.ds(first, count)],
                dst_ref=far_in.at[sweep, slot, pl.ds(0, count)],
                send_sem=far_send.at[sweep, slot],
                recv_sem=far_recv.at[sweep, slot],
                device_id=device,
                device_id_type=MESH,
            )
            for device, slot, first, count in far
        ]

    lane8 = lax.broadcasted_iota(jnp.int32, (8, LANES), 1)
    lane16 = lax.broadcasted_iota(jnp.int32, (ROWS, LANES), 1)

    table[...] = jnp.zeros_like(table)
    for load in loads[0:3]:
        load.wait()
    for h in range(OWN):
        cols = slice(h * LANES, (h + 1) * LANES)
        table[0:6, cols] = free_ref[pl.ds(h, 6, stride=OWN), :]
        table[8:12, cols] = inertia_ref[pl.ds(h, 4, stride=OWN), :]
    listed = [
        jnp.concatenate([exports_ref[1], exports_ref[0]], axis=1),
        jnp.concatenate([exports_ref[3], exports_ref[2]], axis=1),
    ]

    def pick_listed(pair, rows, source=table):
        high = jnp.broadcast_to(lax.shift_right_logical(listed[pair], 7), (rows, LANES))
        low = jnp.broadcast_to(lax.bitwise_and(listed[pair], 127), (rows, LANES))
        got = take(source[0:rows, 0:LANES], low)
        for h in range(1, OWN):
            block = take(source[0:rows, h * LANES : (h + 1) * LANES], low)
            got = jnp.where(high == h, block, got)
        return got

    for pair in range(2):
        first_out[pair] = pick_listed(pair, 16)

    for load in loads[3:]:
        load.wait()
    for t in range(TILES):
        cols = slice(t * LANES, (t + 1) * LANES)
        main = geo_ref[pl.ds(t, 8, stride=TILES), :]
        rest = geo_ref[pl.ds(8 * TILES + t, 2, stride=TILES), :]
        main_a = coarse(main)
        main_b = coarse(main - main_a)
        rest_a = coarse(rest)
        rest_b = coarse(rest - rest_a)
        split_geo[0:8, cols] = main_a
        split_geo[8:16, cols] = main_b
        split_geo[16:24, cols] = main - main_a - main_b
        split_geo[24:26, cols] = rest_a
        split_geo[26:28, cols] = rest_b
        split_geo[28:30, cols] = rest - rest_a - rest_b
        split_geo[30:32, cols] = jnp.zeros((2, LANES), F32)

    along = lax.broadcasted_iota(jnp.int32, (LANES, SPLIT), 1).astype(F32)

    def upright_hot(codes, hot):
        upright = jnp.transpose(lax.bitwise_and(codes, SPLIT - 1).astype(F32))
        for t in range(codes.shape[0]):
            hot[t * LANES : (t + 1) * LANES, :] = (
                (along == upright[:, t : t + 1]).astype(F32).astype(BF16)
            )

    upright_hot(slot_ref[...], slot_hot)

    pl.semaphore_wait(barrier, 7)
    first_trade = trade(0, lambda pair: first_out.at[pair], first_in)
    for copy in first_trade:
        copy.start()

    def relay_copy(step):
        return pltpu.make_async_remote_copy(
            src_ref=outgoing.at[lax.rem(place + step, WIN)],
            dst_ref=incoming.at[step - 1],
            send_sem=relay_send.at[step - 1],
            recv_sem=relay_recv.at[step - 1],
            device_id=(mate(step), layer),
            device_id_type=MESH,
        )

    def arrange(target):
        for t in range(TILES):
            cols = slice(t * LANES, (t + 1) * LANES)
            part = lax.shift_right_logical(slot_ref[t : t + 1, :], 8)
            part = part - (base + target) * TABLE
            values = split_geo[:, cols]
            for g in range(TABLE):
                relay_left[g * 32 : (g + 1) * 32, cols] = jnp.where(
                    part == g, values, 0.0
                ).astype(BF16)
        placed = jnp.dot(relay_left[...], slot_hot[...], preferred_element_type=F32)
        for g in range(TABLE):
            block = placed[g * 32 : (g + 1) * 32]
            main = block[0:8] + block[8:16] + block[16:24]
            rest = block[24:26] + block[26:28] + block[28:30]
            for j in range(2):
                cols = slice(j * LANES, (j + 1) * LANES)
                t = 2 * g + j
                outgoing[target, pl.ds(t, 8, stride=TILES), :] = main[:, cols]
                outgoing[target, pl.ds(8 * TILES + t, 2, stride=TILES), :] = rest[:, cols]

    def send_part(turn, carry):
        swing = 1 - 2 * lax.rem(place, 2)
        step = 2 + swing * lax.rem(turn, 2) - swing * (turn // 2)
        arrange(lax.rem(place + step, WIN))
        relay_copy(step).start()
        return carry

    lax.fori_loop(0, WIN - 1, send_part, 0)
    arrange(place)

    index[...] = jnp.zeros_like(index)
    for e in range(2):
        index[e, 0:TILES] = pairs_ref[e * TILES : (e + 1) * TILES, :]
    upright_hot(pairs_ref[...], pair_hot)
    row16 = lax.broadcasted_iota(jnp.int32, (ROWS, LANES), 0)
    tint = jnp.full((ROWS, LANES), -1, jnp.int32)
    for t in range(TILES):
        tint = jnp.where(row16 == t, color_ref[0, t], tint)
    shade[...] = tint

    wide = lax.broadcasted_iota(jnp.int32, (16, 2 * LANES), 1)
    marks = jnp.where(
        lax.broadcasted_iota(jnp.int32, (16, 2 * LANES), 0) == wide // 64,
        lax.bitwise_and(wide, 127) + 1,
        0,
    )
    tall = lax.broadcasted_iota(jnp.int32, (OWN * LANES, LANES), 0)
    listed_hot = jnp.concatenate(
        [(tall == listed[pair]).astype(F32).astype(BF16) for pair in range(2)], axis=1
    )
    found = lax.dot_general(
        marks.astype(F32).astype(BF16), listed_hot, NT, preferred_element_type=F32
    )
    has_lower_sub = (sub > 0).astype(jnp.int32)
    has_higher_sub = (sub < n_sub - 1).astype(jnp.int32)
    has_lower_layer = (layer > 0).astype(jnp.int32)
    has_higher_layer = (layer < n_layer - 1).astype(jnp.int32)
    exists = (has_higher_sub, has_lower_sub, has_higher_layer, has_lower_layer)
    for h in range(OWN):
        cols = slice(h * LANES, (h + 1) * LANES)
        times = jnp.ones((8, LANES), F32)
        for half in range(4):
            spot = jnp.broadcast_to(found[half : half + 1, cols], (8, LANES))
            spot = spot.astype(jnp.int32) * exists[half] - 1
            inverse_list[h * 4 + half] = spot
            info[half : half + 1, cols] = spot[0:1].astype(F32)
            times = times + jnp.where(spot >= 0, 1.0, 0.0)
        weight[:, cols] = 1.0 / times
        info[4:8, cols] = (1.0 / times)[0:4]
    for pair in range(2):
        info_out[pair] = pick_listed(pair, 8, info)
    info_trade = trade(1, lambda pair: info_out.at[pair], info_in)
    for copy in info_trade:
        copy.start()
    push[...] = jnp.zeros_like(push)
    impulse[...] = jnp.zeros_like(impulse)
    geo[...] = jnp.ones_like(geo)

    def keep(flag, value):
        return jnp.where(flag > 0, value, 0.0)

    def halves(lane, landed):
        return (
            jnp.where(
                lane < 64, keep(has_lower_sub, landed[0]), keep(has_higher_sub, landed[1])
            ),
            jnp.where(
                lane < 64, keep(has_lower_layer, landed[2]), keep(has_higher_layer, landed[3])
            ),
        )

    for copy in first_trade:
        copy.wait_recv()
    table[:, 512:640], table[:, 640:768] = halves(lane16, [first_in[slot] for slot in range(4)])

    def pick(component, e):
        high = lax.shift_right_logical(index[e], 7)
        low = lax.bitwise_and(index[e], 127)
        got = None
        for h in range(TABLE if e else OWN):
            row = table[component : component + 1, h * LANES : (h + 1) * LANES]
            block = take(jnp.broadcast_to(row, (ROWS, LANES)), low)
            got = block if h == 0 else jnp.where(high == h, block, got)
        return got

    props_a = [pick(8 + i, 0) for i in range(4)]
    props_b = [pick(8 + i, 1) for i in range(4)]
    for i in range(4):
        const[20 + i] = props_a[i]
        const[24 + i] = props_b[i]

    for step in range(1, WIN):
        relay_copy(step).wait_recv()
    for c in range(10):
        rows = slice(c * TILES, (c + 1) * TILES)
        geo[c, 0:TILES] = (
            outgoing[place, rows] + incoming[0, rows] + incoming[1, rows] + incoming[2, rows]
        )

    raw = [geo[i] for i in range(3)]
    length = jnp.sqrt(dot3(raw, raw))
    normal = [r / length for r in raw]
    side = jnp.sqrt(normal[1] * normal[1] + normal[2] * normal[2])
    one_y = normal[2] / side
    one_z = -normal[1] / side
    two = cross(normal, [jnp.zeros_like(side), one_y, one_z])
    frame = [normal, [jnp.zeros_like(side), one_y, one_z], two]
    entry_a = arm_block([geo[3 + i] for i in range(3)], props_a[1:])
    entry_b = arm_block([geo[6 + i] for i in range(3)], props_b[1:])
    mass = props_a[0] + props_b[0]
    xx, yy, zz, xy, xz, yz = [a + b for a, b in zip(entry_a, entry_b)]
    xx, yy, zz = mass + xx, mass + yy, mass + zz
    cxx = yy * zz - yz * yz
    cxy = xz * yz - xy * zz
    cxz = xy * yz - xz * yy
    cyy = xx * zz - xz * xz
    cyz = xy * xz - xx * yz
    czz = xx * yy - xy * xy
    scale = relaxation / (xx * cxx + xy * cxy + xz * cxz)
    solve = [[cxx, cxy, cxz], [cxy, cyy, cyz], [cxz, cyz, czz]]
    for i in range(3):
        row = [dot3(frame[i], solve[j]) * scale for j in range(3)]
        for j in range(3):
            const[8 + 3 * i + j] = row[j]
        const[17 + i] = dot3(row, normal) * geo[9]
    for i in range(3):
        const[i] = normal[i]
        const[5 + i] = two[i]
    const[3] = one_y
    const[4] = one_z

    def color_pass(color, carry):
        vel_a = [pick(c, 0) for c in range(6)]
        vel_b = [pick(c, 1) for c in range(6)]
        arm_a = [geo[3 + i] for i in range(3)]
        arm_b = [geo[6 + i] for i in range(3)]
        turn_a = cross(vel_a[3:], arm_a)
        turn_b = cross(vel_b[3:], arm_b)
        relative = [vel_a[i] + turn_a[i] - vel_b[i] - turn_b[i] for i in range(3)]
        old = [impulse[i] for i in range(3)]
        trial = [
            old[i]
            - dot3([const[8 + 3 * i + j] for j in range(3)], relative)
            - const[17 + i]
            for i in range(3)
        ]
        press = jnp.maximum(trial[0], 0.0)
        slide = jnp.sqrt(trial[1] * trial[1] + trial[2] * trial[2])
        factor = jnp.minimum(1.0, friction * press / jnp.maximum(slide, tangent_floor))
        active = shade[...] == color
        new = [
            jnp.where(active, value, was)
            for value, was in zip([press, trial[1] * factor, trial[2] * factor], old)
        ]
        change = [a - b for a, b in zip(new, old)]
        for i in range(3):
            impulse[i] = new[i]
        force = [
            const[0] * change[0] + const[5] * change[2],
            const[1] * change[0] + const[3] * change[1] + const[6] * change[2],
            const[2] * change[0] + const[4] * change[1] + const[7] * change[2],
        ]
        torque_a = cross(arm_a, force)
        torque_b = cross(arm_b, force)
        for i in range(3):
            lin = slice(i * TILES, (i + 1) * TILES)
            ang = slice((3 + i) * TILES, (4 + i) * TILES)
            push[0, lin] = (const[20] * force[i])[0:TILES]
            push[1, lin] = (-const[24] * force[i])[0:TILES]
            push[0, ang] = (const[21 + i] * torque_a[i])[0:TILES]
            push[1, ang] = (-const[25 + i] * torque_b[i])[0:TILES]
        for e in range(2):
            for t in range(TILES):
                value = push[e, pl.ds(t, 8, stride=TILES), :]
                upper = coarse(value)
                lower = value - upper
                part = lax.shift_right_logical(index[e, t : t + 1], 8)
                pieces = [
                    jnp.where(part == h, half, 0.0) for half in (upper, lower) for h in range(3)
                ]
                at = (e * TILES + t) * LANES
                push_left[:, at : at + LANES] = jnp.concatenate(pieces, axis=0).astype(BF16)
        total = jnp.dot(push_left[...], pair_hot[...], preferred_element_type=F32)
        for h in range(3):
            cols = slice(h * SPLIT, (h + 1) * SPLIT)
            table[0:8, cols] = (
                table[0:8, cols]
                + total[h * 8 : (h + 1) * 8]
                + total[24 + h * 8 : 32 + h * 8]
            )
        return carry

    for copy in info_trade:
        copy.wait_recv()
    hints[0], hints[1] = halves(lane8, [info_in[slot] for slot in range(4)])

    def pull(row_block, pair, row):
        spot = jnp.broadcast_to(hints[pair, row : row + 1], (8, LANES)).astype(jnp.int32)
        return jnp.where(spot >= 0, take(row_block, jnp.maximum(spot, 0)), 0.0)

    def one_sweep(sweep, carry):
        start[...] = table[0:8, :]
        lax.fori_loop(0, NCOLOR, color_pass, 0)
        on = sweep + 1 < SWEEPS
        copied = [slice((OWN + pair) * LANES, (OWN + pair + 1) * LANES) for pair in range(2)]
        for pair in range(2):
            sweep_out[sweep, 1 + pair] = table[0:8, copied[pair]] - start[:, copied[pair]]

        @pl.when(on)
        def _():
            for copy in far_copies(sweep):
                copy.start()

        for pair in range(2):
            sweep_out[sweep, 3 * pair] = pick_listed(pair, 8)
        near = near_copies(sweep)
        for copy in near:
            copy.start()
        for copy in near:
            copy.wait_recv()
        arrived = [
            jnp.where(lane8 < 64, near_in[sweep, 1, 1], near_in[sweep, 0, 1]),
            jnp.where(lane8 < 64, near_in[sweep, 3, 0], near_in[sweep, 2, 0]),
        ]
        for h in range(OWN):
            cols = slice(h * LANES, (h + 1) * LANES)
            total = table[0:8, cols] - start[:, cols]
            for half in range(4):
                spot = inverse_list[h * 4 + half]
                total = total + jnp.where(
                    spot >= 0, take(arrived[half // 2], jnp.maximum(spot, 0)), 0.0
                )
            table[0:8, cols] = start[:, cols] + total * weight[:, cols]

        @pl.when(on)
        def _():
            for copy in far_copies(sweep):
                copy.wait_recv()

            def landed(right, up, pair):
                straight = right == 0 or up == 0
                return far_in[sweep, FAR.index((right, up)), 0 if straight else pair]

            left = lane8 < 64
            for pair in range(2):
                if pair == 0:
                    listed_now = jnp.where(left, near_in[sweep, 0, 0], near_in[sweep, 1, 0])
                    beyond = jnp.where(left, landed(2, 0, 0), landed(-2, 0, 0))
                    side_a = jnp.where(left, landed(-1, 1, 1), landed(-1, -1, 1))
                    side_b = jnp.where(left, landed(1, 1, 1), landed(1, -1, 1))
                else:
                    listed_now = jnp.where(left, near_in[sweep, 2, 1], near_in[sweep, 3, 1])
                    beyond = jnp.where(left, landed(0, 2, 1), landed(0, -2, 1))
                    side_a = jnp.where(left, landed(1, -1, 0), landed(-1, -1, 0))
                    side_b = jnp.where(left, landed(1, 1, 0), landed(-1, 1, 0))
                was = start[:, copied[pair]]
                total = (listed_now - was) + sweep_out[sweep, 1 + pair]
                total = total + jnp.where(
                    left, pull(beyond, pair, 2 * pair + 1), pull(beyond, pair, 2 * pair)
                )
                for row in (2 - 2 * pair, 3 - 2 * pair):
                    total = total + jnp.where(
                        left, pull(side_a, pair, row), pull(side_b, pair, row)
                    )
                table[0:8, copied[pair]] = was + total * hints[pair, 4:5]
            for copy in far_copies(sweep):
                copy.wait_send()

        for copy in near:
            copy.wait_send()
        return carry

    lax.fori_loop(0, SWEEPS, one_sweep, 0)
    for h in range(OWN):
        vel_out[pl.ds(h, 6, stride=OWN), :] = table[0:6, h * LANES : (h + 1) * LANES]
    for i in range(3):
        imp_out[i * TILES : (i + 1) * TILES, :] = impulse[i, 0:TILES]
    for copy in first_trade + info_trade:
        copy.wait_send()
    for step in range(1, WIN):
        relay_copy(step).wait_send()


def on_device(n_sub, n_layer, geometry, dest_slot, pairs, colors, free_vel, inertia, exports):
    vmem = pl.BlockSpec(memory_space=pltpu.VMEM)
    hbm = pl.BlockSpec(memory_space=pltpu.HBM)
    impulse, velocity = pl.pallas_call(
        lambda *refs: kernel(n_sub, n_layer, *refs),
        out_shape=(
            jax.ShapeDtypeStruct((3 * TILES, LANES), F32),
            jax.ShapeDtypeStruct((6 * OWN, LANES), F32),
        ),
        in_specs=[hbm] * 7,
        out_specs=(vmem, vmem),
        scratch_shapes=[
            pltpu.VMEM((10 * TILES, LANES), F32),
            pltpu.VMEM((TILES, LANES), jnp.int32),
            pltpu.VMEM((2 * TILES, LANES), jnp.int32),
            pltpu.SMEM((1, TILES), jnp.int32),
            pltpu.VMEM((6 * OWN, LANES), F32),
            pltpu.VMEM((4 * OWN, LANES), F32),
            pltpu.VMEM((4, 1, 64), jnp.int32),
            pltpu.SemaphoreType.DMA((7,)),
            pltpu.VMEM((TILES * LANES, SPLIT), BF16),
            pltpu.VMEM((2 * TILES * LANES, SPLIT), BF16),
            pltpu.VMEM((32, TILES * LANES), F32),
            pltpu.VMEM((192, TILES * LANES), BF16),
            pltpu.VMEM((48, 2 * TILES * LANES), BF16),
            pltpu.VMEM((WIN, 10 * TILES, LANES), F32),
            pltpu.VMEM((WIN - 1, 10 * TILES, LANES), F32),
            pltpu.VMEM((10, ROWS, LANES), F32),
            pltpu.VMEM((2, ROWS, LANES), jnp.int32),
            pltpu.VMEM((ROWS, LANES), jnp.int32),
            pltpu.VMEM((28, ROWS, LANES), F32),
            pltpu.VMEM((3, ROWS, LANES), F32),
            pltpu.VMEM((2, 8 * TILES, LANES), F32),
            pltpu.VMEM((16, TABLE * LANES), F32),
            pltpu.VMEM((8, TABLE * LANES), F32),
            pltpu.VMEM((16, 8, LANES), jnp.int32),
            pltpu.VMEM((8, OWN * LANES), F32),
            pltpu.VMEM((2, 16, LANES), F32),
            pltpu.VMEM((4, 16, LANES), F32),
            pltpu.VMEM((8, OWN * LANES), F32),
            pltpu.VMEM((2, 8, LANES), F32),
            pltpu.VMEM((4, 8, LANES), F32),
            pltpu.VMEM((2, 8, LANES), F32),
            pltpu.VMEM((SWEEPS, 4, 8, LANES), F32),
            pltpu.VMEM((SWEEPS, 4, 2, 8, LANES), F32),
            pltpu.VMEM((SWEEPS - 1, 8, 2, 8, LANES), F32),
            pltpu.SemaphoreType.DMA((WIN - 1,)),
            pltpu.SemaphoreType.DMA((WIN - 1,)),
            pltpu.SemaphoreType.DMA((2 + SWEEPS, 4)),
            pltpu.SemaphoreType.DMA((2 + SWEEPS, 4)),
            pltpu.SemaphoreType.DMA((SWEEPS - 1, 8)),
            pltpu.SemaphoreType.DMA((SWEEPS - 1, 8)),
        ],
        compiler_params=pltpu.CompilerParams(
            collective_id=0, has_side_effects=True, vmem_limit_bytes=32 << 20
        ),
    )(
        *(
            pltpu.with_memory_space_constraint(array, pltpu.HBM)
            for array in (
                geometry.reshape(10 * TILES, LANES),
                dest_slot.reshape(TILES, 1, LANES),
                pairs.reshape(2 * TILES, LANES),
                colors,
                free_vel.reshape(6 * OWN, LANES),
                inertia.reshape(4 * OWN, LANES),
                exports,
            )
        )
    )
    return impulse.reshape(3, 1, TILES * LANES), velocity.reshape(6, 1, OWN * LANES)


def solution(mesh):
    n_sub, n_layer = mesh.shape["sub"], mesh.shape["layer"]
    placed = (
        P(None, "layer", "sub"),
        P("layer", "sub"),
        P(None, "layer", "sub"),
        P("layer", "sub"),
        P(None, "layer", "sub"),
        P(None, "layer", "sub"),
        P(None, "layer", "sub"),
    )
    return jax.shard_map(
        lambda *arrays: on_device(n_sub, n_layer, *arrays),
        mesh=mesh,
        in_specs=placed,
        out_specs=(P(None, "layer", "sub"), P(None, "layer", "sub")),
        check_vma=False,
    )
```

```python
import jax
import jax.numpy as jnp
from jax import lax
from jax.experimental import pallas as pl
from jax.experimental.pallas import tpu as pltpu
from jax.sharding import PartitionSpec as P

WIN = 4
SWEEPS = 3
NCOLOR = 4
LANES = 128
TILES = 12
ROWS = 16
CHUNK = 2
SPLIT = 256
OWN = 4
TABLE = 6

relaxation = 0.7
friction = 0.6
tangent_floor = 0.1

FAR = ((-2, 0), (2, 0), (0, -2), (0, 2), (-1, -1), (-1, 1), (1, -1), (1, 1))
MESH = pl.DeviceIdType.MESH
F32 = jnp.float32
BF16 = jnp.bfloat16
NT = (((1,), (1,)), ((), ()))


def cross(u, v):
    return [
        u[1] * v[2] - u[2] * v[1],
        u[2] * v[0] - u[0] * v[2],
        u[0] * v[1] - u[1] * v[0],
    ]


def dot3(u, v):
    return u[0] * v[0] + u[1] * v[1] + u[2] * v[2]


def take(row_block, index):
    return jnp.take_along_axis(row_block, index, axis=1, mode="promise_in_bounds")


def coarse(value):
    return value.astype(BF16).astype(F32)


def arm_block(arm, spin):
    return [
        spin[1] * arm[2] * arm[2] + spin[2] * arm[1] * arm[1],
        spin[0] * arm[2] * arm[2] + spin[2] * arm[0] * arm[0],
        spin[0] * arm[1] * arm[1] + spin[1] * arm[0] * arm[0],
        -spin[2] * arm[0] * arm[1],
        -spin[1] * arm[0] * arm[2],
        -spin[0] * arm[1] * arm[2],
    ]


def kernel(
    n_sub,
    n_layer,
    geo_hbm,
    slot_hbm,
    pairs_hbm,
    color_hbm,
    free_hbm,
    inertia_hbm,
    exports_hbm,
    imp_out,
    vel_out,
    geo_ref,
    slot_ref,
    pairs_ref,
    color_ref,
    free_ref,
    inertia_ref,
    exports_ref,
    load_sem,
    slot_hot,
    pair_hot,
    split_geo,
    relay_left,
    block_of,
    outgoing,
    incoming,
    geo,
    index,
    shade,
    const,
    impulse,
    push,
    table,
    start,
    inverse_list,
    weight,
    first_out,
    first_in,
    info,
    info_out,
    info_in,
    hints,
    sweep_out,
    near_in,
    far_in,
    relay_send,
    relay_recv,
    near_send,
    near_recv,
    far_send,
    far_recv,
):
    sub = lax.axis_index("sub")
    layer = lax.axis_index("layer")
    base = (sub // WIN) * WIN
    place = sub - base
    lower_sub = lax.rem(sub + n_sub - 1, n_sub)
    higher_sub = lax.rem(sub + 1, n_sub)
    lower_layer = lax.rem(layer + n_layer - 1, n_layer)
    higher_layer = lax.rem(layer + 1, n_layer)

    def mate(step):
        return base + lax.rem(place + step, WIN)

    around = (
        ((lower_sub, layer), 1, 0),
        ((higher_sub, layer), 0, 0),
        ((sub, lower_layer), 3, 1),
        ((sub, higher_layer), 2, 1),
    )

    far = tuple(
        (
            (lax.rem(sub + n_sub + right, n_sub), lax.rem(layer + n_layer + up, n_layer)),
            FAR.index((-right, -up)),
            2 if right == 0 else 1,
            1 if right == 0 or up == 0 else 2,
        )
        for right, up in FAR
    )

    barrier = pltpu.get_barrier_semaphore()
    for device, _, _ in around:
        pl.semaphore_signal(barrier, inc=1, device_id=device, device_id_type=MESH)
    for step in range(1, WIN):
        pl.semaphore_signal(
            barrier, inc=1, device_id=(mate(step), layer), device_id_type=MESH
        )

    loads = [
        pltpu.make_async_copy(src, dst, load_sem.at[i])
        for i, (src, dst) in enumerate(
            (
                (free_hbm, free_ref),
                (inertia_hbm, inertia_ref),
                (exports_hbm, exports_ref),
                (geo_hbm, geo_ref),
                (slot_hbm.at[:, 0, :], slot_ref),
                (pairs_hbm, pairs_ref),
                (color_hbm, color_ref),
            )
        )
    ]
    for load in loads:
        load.start()

    def trade(step, source_of, dst):
        return [
            pltpu.make_async_remote_copy(
                src_ref=source_of(pair),
                dst_ref=dst.at[slot],
                send_sem=near_send.at[step, slot],
                recv_sem=near_recv.at[step, slot],
                device_id=device,
                device_id_type=MESH,
            )
            for device, slot, pair in around
        ]

    def near_copies(sweep):
        return trade(
            2 + sweep, lambda pair: sweep_out.at[sweep, pl.ds(2 * pair, 2)], near_in.at[sweep]
        )

    def far_copies(sweep):
        return [
            pltpu.make_async_remote_copy(
                src_ref=sweep_out.at[sweep, pl.ds(first, count)],
                dst_ref=far_in.at[sweep, slot, pl.ds(0, count)],
                send_sem=far_send.at[sweep, slot],
                recv_sem=far_recv.at[sweep, slot],
                device_id=device,
                device_id_type=MESH,
            )
            for device, slot, first, count in far
        ]

    lane8 = lax.broadcasted_iota(jnp.int32, (8, LANES), 1)
    lane16 = lax.broadcasted_iota(jnp.int32, (ROWS, LANES), 1)

    table[...] = jnp.zeros_like(table)
    for load in loads[0:3]:
        load.wait()
    for h in range(OWN):
        cols = slice(h * LANES, (h + 1) * LANES)
        table[0:6, cols] = free_ref[pl.ds(h, 6, stride=OWN), :]
        table[8:12, cols] = inertia_ref[pl.ds(h, 4, stride=OWN), :]
    listed = [
        jnp.concatenate([exports_ref[1], exports_ref[0]], axis=1),
        jnp.concatenate([exports_ref[3], exports_ref[2]], axis=1),
    ]

    def pick_listed(pair, rows, source=table):
        high = jnp.broadcast_to(lax.shift_right_logical(listed[pair], 7), (rows, LANES))
        low = jnp.broadcast_to(lax.bitwise_and(listed[pair], 127), (rows, LANES))
        got = take(source[0:rows, 0:LANES], low)
        for h in range(1, OWN):
            block = take(source[0:rows, h * LANES : (h + 1) * LANES], low)
            got = jnp.where(high == h, block, got)
        return got

    for pair in range(2):
        first_out[pair] = pick_listed(pair, 16)

    for load in loads[3:]:
        load.wait()
    for t in range(TILES):
        cols = slice(t * LANES, (t + 1) * LANES)
        main = geo_ref[pl.ds(t, 8, stride=TILES), :]
        rest = geo_ref[pl.ds(8 * TILES + t, 2, stride=TILES), :]
        main_a = coarse(main)
        main_b = coarse(main - main_a)
        rest_a = coarse(rest)
        rest_b = coarse(rest - rest_a)
        split_geo[0:8, cols] = main_a
        split_geo[8:16, cols] = main_b
        split_geo[16:24, cols] = main - main_a - main_b
        split_geo[24:26, cols] = rest_a
        split_geo[26:28, cols] = rest_b
        split_geo[28:30, cols] = rest - rest_a - rest_b
        split_geo[30:32, cols] = jnp.zeros((2, LANES), F32)

    along = lax.broadcasted_iota(jnp.int32, (LANES, SPLIT), 1).astype(F32)

    def upright_hot(codes, hot):
        upright = jnp.transpose(lax.bitwise_and(codes, SPLIT - 1).astype(F32))
        for t in range(codes.shape[0]):
            hot[t * LANES : (t + 1) * LANES, :] = (
                (along == upright[:, t : t + 1]).astype(F32).astype(BF16)
            )

    upright_hot(slot_ref[...], slot_hot)

    pl.semaphore_wait(barrier, 7)
    first_trade = trade(0, lambda pair: first_out.at[pair], first_in)
    for copy in first_trade:
        copy.start()

    def relay_copy(step):
        return pltpu.make_async_remote_copy(
            src_ref=outgoing.at[lax.rem(place + step, WIN)],
            dst_ref=incoming.at[step - 1],
            send_sem=relay_send.at[step - 1],
            recv_sem=relay_recv.at[step - 1],
            device_id=(mate(step), layer),
            device_id_type=MESH,
        )

    def arrange(target):
        for t in range(TILES):
            cols = slice(t * LANES, (t + 1) * LANES)
            part = lax.shift_right_logical(slot_ref[t : t + 1, :], 8)
            part = (part - (base + target) * TABLE).astype(F32)
            part = jnp.broadcast_to(part, (32, LANES)).astype(BF16)
            values = split_geo[:, cols].astype(BF16)
            for g in range(TABLE):
                relay_left[g * 32 : (g + 1) * 32, cols] = jnp.where(
                    part == jnp.asarray(g, BF16), values, jnp.zeros((32, LANES), BF16)
                )
        placed = jnp.dot(relay_left[...], slot_hot[...], preferred_element_type=F32)
        for g in range(TABLE):
            block = placed[g * 32 : (g + 1) * 32]
            main = block[0:8] + block[8:16] + block[16:24]
            rest = block[24:26] + block[26:28] + block[28:30]
            for j in range(2):
                cols = slice(j * LANES, (j + 1) * LANES)
                t = 2 * g + j
                outgoing[target, pl.ds(t, 8, stride=TILES), :] = main[:, cols]
                outgoing[target, pl.ds(8 * TILES + t, 2, stride=TILES), :] = rest[:, cols]

    def send_part(turn, carry):
        swing = 1 - 2 * lax.rem(place, 2)
        step = 2 + swing * lax.rem(turn, 2) - swing * (turn // 2)
        arrange(lax.rem(place + step, WIN))
        relay_copy(step).start()
        return carry

    lax.fori_loop(0, WIN - 1, send_part, 0)
    arrange(place)

    index[...] = jnp.zeros_like(index)
    for e in range(2):
        index[e, 0:TILES] = pairs_ref[e * TILES : (e + 1) * TILES, :]
    upright_hot(pairs_ref[...], pair_hot)
    row16 = lax.broadcasted_iota(jnp.int32, (ROWS, LANES), 0)
    tint = jnp.full((ROWS, LANES), -1, jnp.int32)
    for t in range(TILES):
        tint = jnp.where(row16 == t, color_ref[0, t], tint)
    shade[...] = tint

    wide = lax.broadcasted_iota(jnp.int32, (16, 2 * LANES), 1)
    marks = jnp.where(
        lax.broadcasted_iota(jnp.int32, (16, 2 * LANES), 0) == wide // 64,
        lax.bitwise_and(wide, 127) + 1,
        0,
    )
    tall = lax.broadcasted_iota(jnp.int32, (OWN * LANES, LANES), 0)
    listed_hot = jnp.concatenate(
        [(tall == listed[pair]).astype(F32).astype(BF16) for pair in range(2)], axis=1
    )
    found = lax.dot_general(
        marks.astype(F32).astype(BF16), listed_hot, NT, preferred_element_type=F32
    )
    has_lower_sub = (sub > 0).astype(jnp.int32)
    has_higher_sub = (sub < n_sub - 1).astype(jnp.int32)
    has_lower_layer = (layer > 0).astype(jnp.int32)
    has_higher_layer = (layer < n_layer - 1).astype(jnp.int32)
    exists = (has_higher_sub, has_lower_sub, has_higher_layer, has_lower_layer)
    for h in range(OWN):
        cols = slice(h * LANES, (h + 1) * LANES)
        times = jnp.ones((8, LANES), F32)
        for half in range(4):
            spot = jnp.broadcast_to(found[half : half + 1, cols], (8, LANES))
            spot = spot.astype(jnp.int32) * exists[half] - 1
            inverse_list[h * 4 + half] = spot
            info[half : half + 1, cols] = spot[0:1].astype(F32)
            times = times + jnp.where(spot >= 0, 1.0, 0.0)
        weight[:, cols] = 1.0 / times
        info[4:8, cols] = (1.0 / times)[0:4]
    for pair in range(2):
        info_out[pair] = pick_listed(pair, 8, info)
    info_trade = trade(1, lambda pair: info_out.at[pair], info_in)
    for copy in info_trade:
        copy.start()
    push[...] = jnp.zeros_like(push)
    zero16 = jnp.zeros((16, LANES), BF16)
    for t in range(2 * TILES):
        part = lax.shift_right_logical(pairs_ref[t : t + 1, :], 8).astype(F32)
        block_of[t] = jnp.broadcast_to(part, (16, LANES)).astype(BF16)
    impulse[...] = jnp.zeros_like(impulse)
    geo[...] = jnp.ones_like(geo)

    def keep(flag, value):
        return jnp.where(flag > 0, value, 0.0)

    def halves(lane, landed):
        return (
            jnp.where(
                lane < 64, keep(has_lower_sub, landed[0]), keep(has_higher_sub, landed[1])
            ),
            jnp.where(
                lane < 64, keep(has_lower_layer, landed[2]), keep(has_higher_layer, landed[3])
            ),
        )

    for copy in first_trade:
        copy.wait_recv()
    table[:, 512:640], table[:, 640:768] = halves(lane16, [first_in[slot] for slot in range(4)])

    def pick(component, e):
        high = lax.shift_right_logical(index[e], 7)
        low = lax.bitwise_and(index[e], 127)
        got = None
        for h in range(TABLE if e else OWN):
            row = table[component : component + 1, h * LANES : (h + 1) * LANES]
            block = take(jnp.broadcast_to(row, (ROWS, LANES)), low)
            got = block if h == 0 else jnp.where(high == h, block, got)
        return got

    props_a = [pick(8 + i, 0) for i in range(4)]
    props_b = [pick(8 + i, 1) for i in range(4)]
    for i in range(4):
        const[20 + i] = props_a[i]
        const[24 + i] = props_b[i]

    for step in range(1, WIN):
        relay_copy(step).wait_recv()
    for c in range(10):
        rows = slice(c * TILES, (c + 1) * TILES)
        geo[c, 0:TILES] = (
            outgoing[place, rows] + incoming[0, rows] + incoming[1, rows] + incoming[2, rows]
        )

    raw = [geo[i] for i in range(3)]
    length = jnp.sqrt(dot3(raw, raw))
    normal = [r / length for r in raw]
    side = jnp.sqrt(normal[1] * normal[1] + normal[2] * normal[2])
    one_y = normal[2] / side
    one_z = -normal[1] / side
    two = cross(normal, [jnp.zeros_like(side), one_y, one_z])
    frame = [normal, [jnp.zeros_like(side), one_y, one_z], two]
    entry_a = arm_block([geo[3 + i] for i in range(3)], props_a[1:])
    entry_b = arm_block([geo[6 + i] for i in range(3)], props_b[1:])
    mass = props_a[0] + props_b[0]
    xx, yy, zz, xy, xz, yz = [a + b for a, b in zip(entry_a, entry_b)]
    xx, yy, zz = mass + xx, mass + yy, mass + zz
    cxx = yy * zz - yz * yz
    cxy = xz * yz - xy * zz
    cxz = xy * yz - xz * yy
    cyy = xx * zz - xz * xz
    cyz = xy * xz - xx * yz
    czz = xx * yy - xy * xy
    scale = relaxation / (xx * cxx + xy * cxy + xz * cxz)
    solve = [[cxx, cxy, cxz], [cxy, cyy, cyz], [cxz, cyz, czz]]
    for i in range(3):
        row = [dot3(frame[i], solve[j]) * scale for j in range(3)]
        for j in range(3):
            const[8 + 3 * i + j] = row[j]
        const[17 + i] = dot3(row, normal) * geo[9]
    for i in range(3):
        const[i] = normal[i]
        const[5 + i] = two[i]
    const[3] = one_y
    const[4] = one_z

    def color_pass(color, carry):
        vel_a = [pick(c, 0) for c in range(6)]
        vel_b = [pick(c, 1) for c in range(6)]
        arm_a = [geo[3 + i] for i in range(3)]
        arm_b = [geo[6 + i] for i in range(3)]
        turn_a = cross(vel_a[3:], arm_a)
        turn_b = cross(vel_b[3:], arm_b)
        relative = [vel_a[i] + turn_a[i] - vel_b[i] - turn_b[i] for i in range(3)]
        old = [impulse[i] for i in range(3)]
        trial = [
            old[i]
            - dot3([const[8 + 3 * i + j] for j in range(3)], relative)
            - const[17 + i]
            for i in range(3)
        ]
        press = jnp.maximum(trial[0], 0.0)
        slide = jnp.sqrt(trial[1] * trial[1] + trial[2] * trial[2])
        factor = jnp.minimum(1.0, friction * press / jnp.maximum(slide, tangent_floor))
        active = shade[...] == color
        new = [
            jnp.where(active, value, was)
            for value, was in zip([press, trial[1] * factor, trial[2] * factor], old)
        ]
        change = [a - b for a, b in zip(new, old)]
        for i in range(3):
            impulse[i] = new[i]
        force = [
            const[0] * change[0] + const[5] * change[2],
            const[1] * change[0] + const[3] * change[1] + const[6] * change[2],
            const[2] * change[0] + const[4] * change[1] + const[7] * change[2],
        ]
        torque_a = cross(arm_a, force)
        torque_b = cross(arm_b, force)
        for i in range(3):
            lin = slice(i * TILES, (i + 1) * TILES)
            ang = slice((3 + i) * TILES, (4 + i) * TILES)
            push[0, lin] = (const[20] * force[i])[0:TILES]
            push[1, lin] = (-const[24] * force[i])[0:TILES]
            push[0, ang] = (const[21 + i] * torque_a[i])[0:TILES]
            push[1, ang] = (-const[25 + i] * torque_b[i])[0:TILES]
        lefts = []
        for e in range(2):
            for t in range(TILES):
                value = push[e, pl.ds(t, 8, stride=TILES), :]
                upper = coarse(value)
                both = jnp.concatenate([upper, value - upper], axis=0).astype(BF16)
                lefts.append(
                    jnp.concatenate(
                        [
                            jnp.where(block_of[e * TILES + t] == jnp.asarray(h, BF16), both, zero16)
                            for h in range(2 + e)
                        ],
                        axis=0,
                    )
                )
        def product(first, count):
            return jnp.dot(
                jnp.concatenate(lefts[first : first + count], axis=1),
                pair_hot[first * LANES : (first + count) * LANES, :],
                preferred_element_type=F32,
            )

        total_a = sum(product(f, CHUNK) for f in range(0, TILES, CHUNK))
        total_b = sum(product(f, CHUNK) for f in range(TILES, 2 * TILES, CHUNK))
        for h in range(3):
            cols = slice(h * SPLIT, (h + 1) * SPLIT)
            gain = total_b[h * 16 : h * 16 + 8] + total_b[h * 16 + 8 : h * 16 + 16]
            if h < 2:
                gain = gain + total_a[h * 16 : h * 16 + 8] + total_a[h * 16 + 8 : h * 16 + 16]
            table[0:8, cols] = table[0:8, cols] + gain
        return carry

    for copy in info_trade:
        copy.wait_recv()
    hints[0], hints[1] = halves(lane8, [info_in[slot] for slot in range(4)])

    def pull(row_block, pair, row):
        spot = jnp.broadcast_to(hints[pair, row : row + 1], (8, LANES)).astype(jnp.int32)
        return jnp.where(spot >= 0, take(row_block, jnp.maximum(spot, 0)), 0.0)

    def one_sweep(sweep, carry):
        start[...] = table[0:8, :]
        lax.fori_loop(0, NCOLOR, color_pass, 0)
        on = sweep + 1 < SWEEPS
        copied = [slice((OWN + pair) * LANES, (OWN + pair + 1) * LANES) for pair in range(2)]
        for pair in range(2):
            sweep_out[sweep, 1 + pair] = table[0:8, copied[pair]] - start[:, copied[pair]]

        @pl.when(on)
        def _():
            for copy in far_copies(sweep):
                copy.start()

        for pair in range(2):
            sweep_out[sweep, 3 * pair] = pick_listed(pair, 8)
        near = near_copies(sweep)
        for copy in near:
            copy.start()
        for copy in near:
            copy.wait_recv()
        arrived = [
            jnp.where(lane8 < 64, near_in[sweep, 1, 1], near_in[sweep, 0, 1]),
            jnp.where(lane8 < 64, near_in[sweep, 3, 0], near_in[sweep, 2, 0]),
        ]
        for h in range(OWN):
            cols = slice(h * LANES, (h + 1) * LANES)
            total = table[0:8, cols] - start[:, cols]
            for half in range(4):
                spot = inverse_list[h * 4 + half]
                total = total + jnp.where(
                    spot >= 0, take(arrived[half // 2], jnp.maximum(spot, 0)), 0.0
                )
            table[0:8, cols] = start[:, cols] + total * weight[:, cols]

        @pl.when(on)
        def _():
            for copy in far_copies(sweep):
                copy.wait_recv()

            def landed(right, up, pair):
                straight = right == 0 or up == 0
                return far_in[sweep, FAR.index((right, up)), 0 if straight else pair]

            left = lane8 < 64
            for pair in range(2):
                if pair == 0:
                    listed_now = jnp.where(left, near_in[sweep, 0, 0], near_in[sweep, 1, 0])
                    beyond = jnp.where(left, landed(2, 0, 0), landed(-2, 0, 0))
                    side_a = jnp.where(left, landed(-1, 1, 1), landed(-1, -1, 1))
                    side_b = jnp.where(left, landed(1, 1, 1), landed(1, -1, 1))
                else:
                    listed_now = jnp.where(left, near_in[sweep, 2, 1], near_in[sweep, 3, 1])
                    beyond = jnp.where(left, landed(0, 2, 1), landed(0, -2, 1))
                    side_a = jnp.where(left, landed(1, -1, 0), landed(-1, -1, 0))
                    side_b = jnp.where(left, landed(1, 1, 0), landed(-1, 1, 0))
                was = start[:, copied[pair]]
                total = (listed_now - was) + sweep_out[sweep, 1 + pair]
                total = total + jnp.where(
                    left, pull(beyond, pair, 2 * pair + 1), pull(beyond, pair, 2 * pair)
                )
                for row in (2 - 2 * pair, 3 - 2 * pair):
                    total = total + jnp.where(
                        left, pull(side_a, pair, row), pull(side_b, pair, row)
                    )
                table[0:8, copied[pair]] = was + total * hints[pair, 4:5]
            for copy in far_copies(sweep):
                copy.wait_send()

        for copy in near:
            copy.wait_send()
        return carry

    lax.fori_loop(0, SWEEPS, one_sweep, 0)
    for h in range(OWN):
        vel_out[pl.ds(h, 6, stride=OWN), :] = table[0:6, h * LANES : (h + 1) * LANES]
    for i in range(3):
        imp_out[i * TILES : (i + 1) * TILES, :] = impulse[i, 0:TILES]
    for copy in first_trade + info_trade:
        copy.wait_send()
    for step in range(1, WIN):
        relay_copy(step).wait_send()


def on_device(n_sub, n_layer, geometry, dest_slot, pairs, colors, free_vel, inertia, exports):
    vmem = pl.BlockSpec(memory_space=pltpu.VMEM)
    hbm = pl.BlockSpec(memory_space=pltpu.HBM)
    impulse, velocity = pl.pallas_call(
        lambda *refs: kernel(n_sub, n_layer, *refs),
        out_shape=(
            jax.ShapeDtypeStruct((3 * TILES, LANES), F32),
            jax.ShapeDtypeStruct((6 * OWN, LANES), F32),
        ),
        in_specs=[hbm] * 7,
        out_specs=(vmem, vmem),
        scratch_shapes=[
            pltpu.VMEM((10 * TILES, LANES), F32),
            pltpu.VMEM((TILES, LANES), jnp.int32),
            pltpu.VMEM((2 * TILES, LANES), jnp.int32),
            pltpu.SMEM((1, TILES), jnp.int32),
            pltpu.VMEM((6 * OWN, LANES), F32),
            pltpu.VMEM((4 * OWN, LANES), F32),
            pltpu.VMEM((4, 1, 64), jnp.int32),
            pltpu.SemaphoreType.DMA((7,)),
            pltpu.VMEM((TILES * LANES, SPLIT), BF16),
            pltpu.VMEM((2 * TILES * LANES, SPLIT), BF16),
            pltpu.VMEM((32, TILES * LANES), F32),
            pltpu.VMEM((192, TILES * LANES), BF16),
            pltpu.VMEM((2 * TILES, 16, LANES), BF16),
            pltpu.VMEM((WIN, 10 * TILES, LANES), F32),
            pltpu.VMEM((WIN - 1, 10 * TILES, LANES), F32),
            pltpu.VMEM((10, ROWS, LANES), F32),
            pltpu.VMEM((2, ROWS, LANES), jnp.int32),
            pltpu.VMEM((ROWS, LANES), jnp.int32),
            pltpu.VMEM((28, ROWS, LANES), F32),
            pltpu.VMEM((3, ROWS, LANES), F32),
            pltpu.VMEM((2, 8 * TILES, LANES), F32),
            pltpu.VMEM((16, TABLE * LANES), F32),
            pltpu.VMEM((8, TABLE * LANES), F32),
            pltpu.VMEM((16, 8, LANES), jnp.int32),
            pltpu.VMEM((8, OWN * LANES), F32),
            pltpu.VMEM((2, 16, LANES), F32),
            pltpu.VMEM((4, 16, LANES), F32),
            pltpu.VMEM((8, OWN * LANES), F32),
            pltpu.VMEM((2, 8, LANES), F32),
            pltpu.VMEM((4, 8, LANES), F32),
            pltpu.VMEM((2, 8, LANES), F32),
            pltpu.VMEM((SWEEPS, 4, 8, LANES), F32),
            pltpu.VMEM((SWEEPS, 4, 2, 8, LANES), F32),
            pltpu.VMEM((SWEEPS - 1, 8, 2, 8, LANES), F32),
            pltpu.SemaphoreType.DMA((WIN - 1,)),
            pltpu.SemaphoreType.DMA((WIN - 1,)),
            pltpu.SemaphoreType.DMA((2 + SWEEPS, 4)),
            pltpu.SemaphoreType.DMA((2 + SWEEPS, 4)),
            pltpu.SemaphoreType.DMA((SWEEPS - 1, 8)),
            pltpu.SemaphoreType.DMA((SWEEPS - 1, 8)),
        ],
        compiler_params=pltpu.CompilerParams(
            collective_id=0, has_side_effects=True, vmem_limit_bytes=32 << 20
        ),
    )(
        *(
            pltpu.with_memory_space_constraint(array, pltpu.HBM)
            for array in (
                geometry.reshape(10 * TILES, LANES),
                dest_slot.reshape(TILES, 1, LANES),
                pairs.reshape(2 * TILES, LANES),
                colors,
                free_vel.reshape(6 * OWN, LANES),
                inertia.reshape(4 * OWN, LANES),
                exports,
            )
        )
    )
    return impulse.reshape(3, 1, TILES * LANES), velocity.reshape(6, 1, OWN * LANES)


def solution(mesh):
    n_sub, n_layer = mesh.shape["sub"], mesh.shape["layer"]
    placed = (
        P(None, "layer", "sub"),
        P("layer", "sub"),
        P(None, "layer", "sub"),
        P("layer", "sub"),
        P(None, "layer", "sub"),
        P(None, "layer", "sub"),
        P(None, "layer", "sub"),
    )
    return jax.shard_map(
        lambda *arrays: on_device(n_sub, n_layer, *arrays),
        mesh=mesh,
        in_specs=placed,
        out_specs=(P(None, "layer", "sub"), P(None, "layer", "sub")),
        check_vma=False,
    )
```

```python
import jax
import jax.numpy as jnp
from jax import lax
from jax.experimental import pallas as pl
from jax.experimental.pallas import tpu as pltpu
from jax.sharding import PartitionSpec as P

WIN = 4
SWEEPS = 3
NCOLOR = 4
LANES = 128
TILES = 12
ROWS = 16
CHUNK = 2
SPLIT = 256
OWN = 4
TABLE = 6

relaxation = 0.7
friction = 0.6
tangent_floor = 0.1

FAR = ((-2, 0), (2, 0), (0, -2), (0, 2), (-1, -1), (-1, 1), (1, -1), (1, 1))
MESH = pl.DeviceIdType.MESH
F32 = jnp.float32
BF16 = jnp.bfloat16
NT = (((1,), (1,)), ((), ()))


def cross(u, v):
    return [
        u[1] * v[2] - u[2] * v[1],
        u[2] * v[0] - u[0] * v[2],
        u[0] * v[1] - u[1] * v[0],
    ]


def dot3(u, v):
    return u[0] * v[0] + u[1] * v[1] + u[2] * v[2]


def take(row_block, index):
    return jnp.take_along_axis(row_block, index, axis=1, mode="promise_in_bounds")


def coarse(value):
    return value.astype(BF16).astype(F32)


def arm_block(arm, spin):
    return [
        spin[1] * arm[2] * arm[2] + spin[2] * arm[1] * arm[1],
        spin[0] * arm[2] * arm[2] + spin[2] * arm[0] * arm[0],
        spin[0] * arm[1] * arm[1] + spin[1] * arm[0] * arm[0],
        -spin[2] * arm[0] * arm[1],
        -spin[1] * arm[0] * arm[2],
        -spin[0] * arm[1] * arm[2],
    ]


def kernel(
    n_sub,
    n_layer,
    geo_hbm,
    slot_hbm,
    pairs_hbm,
    color_hbm,
    free_hbm,
    inertia_hbm,
    exports_hbm,
    imp_out,
    vel_out,
    geo_ref,
    slot_ref,
    pairs_ref,
    color_ref,
    free_ref,
    inertia_ref,
    exports_ref,
    load_sem,
    slot_hot,
    pair_hot,
    split_geo,
    relay_left,
    block_of,
    outgoing,
    incoming,
    geo,
    index,
    shade,
    const,
    impulse,
    push,
    table,
    start,
    inverse_list,
    weight,
    first_out,
    first_in,
    info,
    info_out,
    info_in,
    hints,
    sweep_out,
    near_in,
    far_in,
    relay_send,
    relay_recv,
    near_send,
    near_recv,
    far_send,
    far_recv,
):
    sub = lax.axis_index("sub")
    layer = lax.axis_index("layer")
    base = (sub // WIN) * WIN
    place = sub - base
    lower_sub = lax.rem(sub + n_sub - 1, n_sub)
    higher_sub = lax.rem(sub + 1, n_sub)
    lower_layer = lax.rem(layer + n_layer - 1, n_layer)
    higher_layer = lax.rem(layer + 1, n_layer)

    def mate(step):
        return base + lax.rem(place + step, WIN)

    around = (
        ((lower_sub, layer), 1, 0),
        ((higher_sub, layer), 0, 0),
        ((sub, lower_layer), 3, 1),
        ((sub, higher_layer), 2, 1),
    )

    far = tuple(
        (
            (lax.rem(sub + n_sub + right, n_sub), lax.rem(layer + n_layer + up, n_layer)),
            FAR.index((-right, -up)),
            2 if right == 0 else 1,
            1 if right == 0 or up == 0 else 2,
        )
        for right, up in FAR
    )

    barrier = pltpu.get_barrier_semaphore()
    for device, _, _ in around:
        pl.semaphore_signal(barrier, inc=1, device_id=device, device_id_type=MESH)
    for step in range(1, WIN):
        pl.semaphore_signal(
            barrier, inc=1, device_id=(mate(step), layer), device_id_type=MESH
        )

    loads = [
        pltpu.make_async_copy(src, dst, load_sem.at[i])
        for i, (src, dst) in enumerate(
            (
                (free_hbm, free_ref),
                (inertia_hbm, inertia_ref),
                (exports_hbm, exports_ref),
                (geo_hbm, geo_ref),
                (slot_hbm.at[:, 0, :], slot_ref),
                (pairs_hbm, pairs_ref),
                (color_hbm, color_ref),
            )
        )
    ]
    for load in loads:
        load.start()

    def trade(step, source_of, dst):
        return [
            pltpu.make_async_remote_copy(
                src_ref=source_of(pair),
                dst_ref=dst.at[slot],
                send_sem=near_send.at[step, slot],
                recv_sem=near_recv.at[step, slot],
                device_id=device,
                device_id_type=MESH,
            )
            for device, slot, pair in around
        ]

    def near_copies(sweep):
        return trade(
            2 + sweep, lambda pair: sweep_out.at[sweep, pl.ds(2 * pair, 2)], near_in.at[sweep]
        )

    def far_copies(sweep):
        return [
            pltpu.make_async_remote_copy(
                src_ref=sweep_out.at[sweep, pl.ds(first, count)],
                dst_ref=far_in.at[sweep, slot, pl.ds(0, count)],
                send_sem=far_send.at[sweep, slot],
                recv_sem=far_recv.at[sweep, slot],
                device_id=device,
                device_id_type=MESH,
            )
            for device, slot, first, count in far
        ]

    lane8 = lax.broadcasted_iota(jnp.int32, (8, LANES), 1)
    lane16 = lax.broadcasted_iota(jnp.int32, (ROWS, LANES), 1)

    table[...] = jnp.zeros_like(table)
    for load in loads[0:3]:
        load.wait()
    for h in range(OWN):
        cols = slice(h * LANES, (h + 1) * LANES)
        table[0:6, cols] = free_ref[pl.ds(h, 6, stride=OWN), :]
        table[8:12, cols] = inertia_ref[pl.ds(h, 4, stride=OWN), :]
    listed = [
        jnp.concatenate([exports_ref[1], exports_ref[0]], axis=1),
        jnp.concatenate([exports_ref[3], exports_ref[2]], axis=1),
    ]

    def pick_listed(pair, rows, source=table):
        high = jnp.broadcast_to(lax.shift_right_logical(listed[pair], 7), (rows, LANES))
        low = jnp.broadcast_to(lax.bitwise_and(listed[pair], 127), (rows, LANES))
        got = take(source[0:rows, 0:LANES], low)
        for h in range(1, OWN):
            block = take(source[0:rows, h * LANES : (h + 1) * LANES], low)
            got = jnp.where(high == h, block, got)
        return got

    for pair in range(2):
        first_out[pair] = pick_listed(pair, 16)

    for load in loads[3:]:
        load.wait()
    for t in range(TILES):
        cols = slice(t * LANES, (t + 1) * LANES)
        main = geo_ref[pl.ds(t, 8, stride=TILES), :]
        rest = geo_ref[pl.ds(8 * TILES + t, 2, stride=TILES), :]
        main_a = coarse(main)
        main_b = coarse(main - main_a)
        rest_a = coarse(rest)
        rest_b = coarse(rest - rest_a)
        split_geo[0:8, cols] = main_a
        split_geo[8:16, cols] = main_b
        split_geo[16:24, cols] = main - main_a - main_b
        split_geo[24:26, cols] = rest_a
        split_geo[26:28, cols] = rest_b
        split_geo[28:30, cols] = rest - rest_a - rest_b
        split_geo[30:32, cols] = jnp.zeros((2, LANES), F32)

    along = lax.broadcasted_iota(jnp.int32, (LANES, SPLIT), 1).astype(F32)

    def upright_hot(codes, hot):
        upright = jnp.transpose(lax.bitwise_and(codes, SPLIT - 1).astype(F32))
        for t in range(codes.shape[0]):
            hot[t * LANES : (t + 1) * LANES, :] = (
                (along == upright[:, t : t + 1]).astype(F32).astype(BF16)
            )

    upright_hot(slot_ref[...], slot_hot)

    def relay_copy(step):
        return pltpu.make_async_remote_copy(
            src_ref=outgoing.at[lax.rem(place + step, WIN)],
            dst_ref=incoming.at[step - 1],
            send_sem=relay_send.at[step - 1],
            recv_sem=relay_recv.at[step - 1],
            device_id=(mate(step), layer),
            device_id_type=MESH,
        )

    def arrange(target):
        for t in range(TILES):
            cols = slice(t * LANES, (t + 1) * LANES)
            part = lax.shift_right_logical(slot_ref[t : t + 1, :], 8)
            part = (part - (base + target) * TABLE).astype(F32)
            part = jnp.broadcast_to(part, (32, LANES)).astype(BF16)
            values = split_geo[:, cols].astype(BF16)
            for g in range(TABLE):
                relay_left[g * 32 : (g + 1) * 32, cols] = jnp.where(
                    part == jnp.asarray(g, BF16), values, jnp.zeros((32, LANES), BF16)
                )
        placed = jnp.dot(relay_left[...], slot_hot[...], preferred_element_type=F32)
        for g in range(TABLE):
            block = placed[g * 32 : (g + 1) * 32]
            main = block[0:8] + block[8:16] + block[16:24]
            rest = block[24:26] + block[26:28] + block[28:30]
            for j in range(2):
                cols = slice(j * LANES, (j + 1) * LANES)
                t = 2 * g + j
                outgoing[target, pl.ds(t, 8, stride=TILES), :] = main[:, cols]
                outgoing[target, pl.ds(8 * TILES + t, 2, stride=TILES), :] = rest[:, cols]

    def arrange_for(step, carry):
        arrange(lax.rem(place + step, WIN))
        return carry

    lax.fori_loop(1, WIN, arrange_for, 0)
    pl.semaphore_wait(barrier, 7)
    first_trade = trade(0, lambda pair: first_out.at[pair], first_in)
    for copy in first_trade:
        copy.start()
    for step in (2, 1, 3):
        relay_copy(step).start()
    arrange(place)

    index[...] = jnp.zeros_like(index)
    for e in range(2):
        index[e, 0:TILES] = pairs_ref[e * TILES : (e + 1) * TILES, :]
    upright_hot(pairs_ref[...], pair_hot)
    row16 = lax.broadcasted_iota(jnp.int32, (ROWS, LANES), 0)
    tint = jnp.full((ROWS, LANES), -1, jnp.int32)
    for t in range(TILES):
        tint = jnp.where(row16 == t, color_ref[0, t], tint)
    shade[...] = tint

    wide = lax.broadcasted_iota(jnp.int32, (16, 2 * LANES), 1)
    marks = jnp.where(
        lax.broadcasted_iota(jnp.int32, (16, 2 * LANES), 0) == wide // 64,
        lax.bitwise_and(wide, 127) + 1,
        0,
    )
    tall = lax.broadcasted_iota(jnp.int32, (OWN * LANES, LANES), 0)
    listed_hot = jnp.concatenate(
        [(tall == listed[pair]).astype(F32).astype(BF16) for pair in range(2)], axis=1
    )
    found = lax.dot_general(
        marks.astype(F32).astype(BF16), listed_hot, NT, preferred_element_type=F32
    )
    has_lower_sub = (sub > 0).astype(jnp.int32)
    has_higher_sub = (sub < n_sub - 1).astype(jnp.int32)
    has_lower_layer = (layer > 0).astype(jnp.int32)
    has_higher_layer = (layer < n_layer - 1).astype(jnp.int32)
    exists = (has_higher_sub, has_lower_sub, has_higher_layer, has_lower_layer)
    for h in range(OWN):
        cols = slice(h * LANES, (h + 1) * LANES)
        times = jnp.ones((8, LANES), F32)
        for half in range(4):
            spot = jnp.broadcast_to(found[half : half + 1, cols], (8, LANES))
            spot = spot.astype(jnp.int32) * exists[half] - 1
            inverse_list[h * 4 + half] = spot
            info[half : half + 1, cols] = spot[0:1].astype(F32)
            times = times + jnp.where(spot >= 0, 1.0, 0.0)
        weight[:, cols] = 1.0 / times
        info[4:8, cols] = (1.0 / times)[0:4]
    for pair in range(2):
        info_out[pair] = pick_listed(pair, 8, info)
    info_trade = trade(1, lambda pair: info_out.at[pair], info_in)
    for copy in info_trade:
        copy.start()
    push[...] = jnp.zeros_like(push)
    zero16 = jnp.zeros((16, LANES), BF16)
    for t in range(2 * TILES):
        part = lax.shift_right_logical(pairs_ref[t : t + 1, :], 8).astype(F32)
        block_of[t] = jnp.broadcast_to(part, (16, LANES)).astype(BF16)
    impulse[...] = jnp.zeros_like(impulse)
    geo[...] = jnp.ones_like(geo)

    def keep(flag, value):
        return jnp.where(flag > 0, value, 0.0)

    def halves(lane, landed):
        return (
            jnp.where(
                lane < 64, keep(has_lower_sub, landed[0]), keep(has_higher_sub, landed[1])
            ),
            jnp.where(
                lane < 64, keep(has_lower_layer, landed[2]), keep(has_higher_layer, landed[3])
            ),
        )

    for copy in first_trade:
        copy.wait_recv()
    table[:, 512:640], table[:, 640:768] = halves(lane16, [first_in[slot] for slot in range(4)])

    def pick(component, e):
        high = lax.shift_right_logical(index[e], 7)
        low = lax.bitwise_and(index[e], 127)
        got = None
        for h in range(TABLE if e else OWN):
            row = table[component : component + 1, h * LANES : (h + 1) * LANES]
            block = take(jnp.broadcast_to(row, (ROWS, LANES)), low)
            got = block if h == 0 else jnp.where(high == h, block, got)
        return got

    props_a = [pick(8 + i, 0) for i in range(4)]
    props_b = [pick(8 + i, 1) for i in range(4)]
    for i in range(4):
        const[20 + i] = props_a[i]
        const[24 + i] = props_b[i]

    for step in range(1, WIN):
        relay_copy(step).wait_recv()
    for c in range(10):
        rows = slice(c * TILES, (c + 1) * TILES)
        geo[c, 0:TILES] = (
            outgoing[place, rows] + incoming[0, rows] + incoming[1, rows] + incoming[2, rows]
        )

    raw = [geo[i] for i in range(3)]
    length = jnp.sqrt(dot3(raw, raw))
    normal = [r / length for r in raw]
    side = jnp.sqrt(normal[1] * normal[1] + normal[2] * normal[2])
    one_y = normal[2] / side
    one_z = -normal[1] / side
    two = cross(normal, [jnp.zeros_like(side), one_y, one_z])
    frame = [normal, [jnp.zeros_like(side), one_y, one_z], two]
    entry_a = arm_block([geo[3 + i] for i in range(3)], props_a[1:])
    entry_b = arm_block([geo[6 + i] for i in range(3)], props_b[1:])
    mass = props_a[0] + props_b[0]
    xx, yy, zz, xy, xz, yz = [a + b for a, b in zip(entry_a, entry_b)]
    xx, yy, zz = mass + xx, mass + yy, mass + zz
    cxx = yy * zz - yz * yz
    cxy = xz * yz - xy * zz
    cxz = xy * yz - xz * yy
    cyy = xx * zz - xz * xz
    cyz = xy * xz - xx * yz
    czz = xx * yy - xy * xy
    scale = relaxation / (xx * cxx + xy * cxy + xz * cxz)
    solve = [[cxx, cxy, cxz], [cxy, cyy, cyz], [cxz, cyz, czz]]
    for i in range(3):
        row = [dot3(frame[i], solve[j]) * scale for j in range(3)]
        for j in range(3):
            const[8 + 3 * i + j] = row[j]
        const[17 + i] = dot3(row, normal) * geo[9]
    for i in range(3):
        const[i] = normal[i]
        const[5 + i] = two[i]
    const[3] = one_y
    const[4] = one_z

    def color_pass(color, carry):
        vel_a = [pick(c, 0) for c in range(6)]
        vel_b = [pick(c, 1) for c in range(6)]
        arm_a = [geo[3 + i] for i in range(3)]
        arm_b = [geo[6 + i] for i in range(3)]
        turn_a = cross(vel_a[3:], arm_a)
        turn_b = cross(vel_b[3:], arm_b)
        relative = [vel_a[i] + turn_a[i] - vel_b[i] - turn_b[i] for i in range(3)]
        old = [impulse[i] for i in range(3)]
        trial = [
            old[i]
            - dot3([const[8 + 3 * i + j] for j in range(3)], relative)
            - const[17 + i]
            for i in range(3)
        ]
        press = jnp.maximum(trial[0], 0.0)
        slide = jnp.sqrt(trial[1] * trial[1] + trial[2] * trial[2])
        factor = jnp.minimum(1.0, friction * press / jnp.maximum(slide, tangent_floor))
        active = shade[...] == color
        new = [
            jnp.where(active, value, was)
            for value, was in zip([press, trial[1] * factor, trial[2] * factor], old)
        ]
        change = [a - b for a, b in zip(new, old)]
        for i in range(3):
            impulse[i] = new[i]
        force = [
            const[0] * change[0] + const[5] * change[2],
            const[1] * change[0] + const[3] * change[1] + const[6] * change[2],
            const[2] * change[0] + const[4] * change[1] + const[7] * change[2],
        ]
        torque_a = cross(arm_a, force)
        torque_b = cross(arm_b, force)
        for i in range(3):
            lin = slice(i * TILES, (i + 1) * TILES)
            ang = slice((3 + i) * TILES, (4 + i) * TILES)
            push[0, lin] = (const[20] * force[i])[0:TILES]
            push[1, lin] = (-const[24] * force[i])[0:TILES]
            push[0, ang] = (const[21 + i] * torque_a[i])[0:TILES]
            push[1, ang] = (-const[25 + i] * torque_b[i])[0:TILES]
        lefts = []
        for e in range(2):
            for t in range(TILES):
                value = push[e, pl.ds(t, 8, stride=TILES), :]
                upper = coarse(value)
                both = jnp.concatenate([upper, value - upper], axis=0).astype(BF16)
                lefts.append(
                    jnp.concatenate(
                        [
                            jnp.where(block_of[e * TILES + t] == jnp.asarray(h, BF16), both, zero16)
                            for h in range(2 + e)
                        ],
                        axis=0,
                    )
                )
        def product(first, count):
            return jnp.dot(
                jnp.concatenate(lefts[first : first + count], axis=1),
                pair_hot[first * LANES : (first + count) * LANES, :],
                preferred_element_type=F32,
            )

        total_a = sum(product(f, CHUNK) for f in range(0, TILES, CHUNK))
        total_b = sum(product(f, CHUNK) for f in range(TILES, 2 * TILES, CHUNK))
        for h in range(3):
            cols = slice(h * SPLIT, (h + 1) * SPLIT)
            gain = total_b[h * 16 : h * 16 + 8] + total_b[h * 16 + 8 : h * 16 + 16]
            if h < 2:
                gain = gain + total_a[h * 16 : h * 16 + 8] + total_a[h * 16 + 8 : h * 16 + 16]
            table[0:8, cols] = table[0:8, cols] + gain
        return carry

    for copy in info_trade:
        copy.wait_recv()
    hints[0], hints[1] = halves(lane8, [info_in[slot] for slot in range(4)])

    def pull(row_block, pair, row):
        spot = jnp.broadcast_to(hints[pair, row : row + 1], (8, LANES)).astype(jnp.int32)
        return jnp.where(spot >= 0, take(row_block, jnp.maximum(spot, 0)), 0.0)

    def one_sweep(sweep, carry):
        start[...] = table[0:8, :]
        lax.fori_loop(0, NCOLOR, color_pass, 0)
        on = sweep + 1 < SWEEPS
        copied = [slice((OWN + pair) * LANES, (OWN + pair + 1) * LANES) for pair in range(2)]
        for pair in range(2):
            sweep_out[sweep, 1 + pair] = table[0:8, copied[pair]] - start[:, copied[pair]]

        @pl.when(on)
        def _():
            for copy in far_copies(sweep):
                copy.start()

        for pair in range(2):
            sweep_out[sweep, 3 * pair] = pick_listed(pair, 8)
        near = near_copies(sweep)
        for copy in near:
            copy.start()
        for copy in near:
            copy.wait_recv()
        arrived = [
            jnp.where(lane8 < 64, near_in[sweep, 1, 1], near_in[sweep, 0, 1]),
            jnp.where(lane8 < 64, near_in[sweep, 3, 0], near_in[sweep, 2, 0]),
        ]
        for h in range(OWN):
            cols = slice(h * LANES, (h + 1) * LANES)
            total = table[0:8, cols] - start[:, cols]
            for half in range(4):
                spot = inverse_list[h * 4 + half]
                total = total + jnp.where(
                    spot >= 0, take(arrived[half // 2], jnp.maximum(spot, 0)), 0.0
                )
            table[0:8, cols] = start[:, cols] + total * weight[:, cols]

        @pl.when(on)
        def _():
            for copy in far_copies(sweep):
                copy.wait_recv()

            def landed(right, up, pair):
                straight = right == 0 or up == 0
                return far_in[sweep, FAR.index((right, up)), 0 if straight else pair]

            left = lane8 < 64
            for pair in range(2):
                if pair == 0:
                    listed_now = jnp.where(left, near_in[sweep, 0, 0], near_in[sweep, 1, 0])
                    beyond = jnp.where(left, landed(2, 0, 0), landed(-2, 0, 0))
                    side_a = jnp.where(left, landed(-1, 1, 1), landed(-1, -1, 1))
                    side_b = jnp.where(left, landed(1, 1, 1), landed(1, -1, 1))
                else:
                    listed_now = jnp.where(left, near_in[sweep, 2, 1], near_in[sweep, 3, 1])
                    beyond = jnp.where(left, landed(0, 2, 1), landed(0, -2, 1))
                    side_a = jnp.where(left, landed(1, -1, 0), landed(-1, -1, 0))
                    side_b = jnp.where(left, landed(1, 1, 0), landed(-1, 1, 0))
                was = start[:, copied[pair]]
                total = (listed_now - was) + sweep_out[sweep, 1 + pair]
                total = total + jnp.where(
                    left, pull(beyond, pair, 2 * pair + 1), pull(beyond, pair, 2 * pair)
                )
                for row in (2 - 2 * pair, 3 - 2 * pair):
                    total = total + jnp.where(
                        left, pull(side_a, pair, row), pull(side_b, pair, row)
                    )
                table[0:8, copied[pair]] = was + total * hints[pair, 4:5]
            for copy in far_copies(sweep):
                copy.wait_send()

        for copy in near:
            copy.wait_send()
        return carry

    lax.fori_loop(0, SWEEPS, one_sweep, 0)
    for h in range(OWN):
        vel_out[pl.ds(h, 6, stride=OWN), :] = table[0:6, h * LANES : (h + 1) * LANES]
    for i in range(3):
        imp_out[i * TILES : (i + 1) * TILES, :] = impulse[i, 0:TILES]
    for copy in first_trade + info_trade:
        copy.wait_send()
    for step in range(1, WIN):
        relay_copy(step).wait_send()


def on_device(n_sub, n_layer, geometry, dest_slot, pairs, colors, free_vel, inertia, exports):
    vmem = pl.BlockSpec(memory_space=pltpu.VMEM)
    hbm = pl.BlockSpec(memory_space=pltpu.HBM)
    impulse, velocity = pl.pallas_call(
        lambda *refs: kernel(n_sub, n_layer, *refs),
        out_shape=(
            jax.ShapeDtypeStruct((3 * TILES, LANES), F32),
            jax.ShapeDtypeStruct((6 * OWN, LANES), F32),
        ),
        in_specs=[hbm] * 7,
        out_specs=(vmem, vmem),
        scratch_shapes=[
            pltpu.VMEM((10 * TILES, LANES), F32),
            pltpu.VMEM((TILES, LANES), jnp.int32),
            pltpu.VMEM((2 * TILES, LANES), jnp.int32),
            pltpu.SMEM((1, TILES), jnp.int32),
            pltpu.VMEM((6 * OWN, LANES), F32),
            pltpu.VMEM((4 * OWN, LANES), F32),
            pltpu.VMEM((4, 1, 64), jnp.int32),
            pltpu.SemaphoreType.DMA((7,)),
            pltpu.VMEM((TILES * LANES, SPLIT), BF16),
            pltpu.VMEM((2 * TILES * LANES, SPLIT), BF16),
            pltpu.VMEM((32, TILES * LANES), F32),
            pltpu.VMEM((192, TILES * LANES), BF16),
            pltpu.VMEM((2 * TILES, 16, LANES), BF16),
            pltpu.VMEM((WIN, 10 * TILES, LANES), F32),
            pltpu.VMEM((WIN - 1, 10 * TILES, LANES), F32),
            pltpu.VMEM((10, ROWS, LANES), F32),
            pltpu.VMEM((2, ROWS, LANES), jnp.int32),
            pltpu.VMEM((ROWS, LANES), jnp.int32),
            pltpu.VMEM((28, ROWS, LANES), F32),
            pltpu.VMEM((3, ROWS, LANES), F32),
            pltpu.VMEM((2, 8 * TILES, LANES), F32),
            pltpu.VMEM((16, TABLE * LANES), F32),
            pltpu.VMEM((8, TABLE * LANES), F32),
            pltpu.VMEM((16, 8, LANES), jnp.int32),
            pltpu.VMEM((8, OWN * LANES), F32),
            pltpu.VMEM((2, 16, LANES), F32),
            pltpu.VMEM((4, 16, LANES), F32),
            pltpu.VMEM((8, OWN * LANES), F32),
            pltpu.VMEM((2, 8, LANES), F32),
            pltpu.VMEM((4, 8, LANES), F32),
            pltpu.VMEM((2, 8, LANES), F32),
            pltpu.VMEM((SWEEPS, 4, 8, LANES), F32),
            pltpu.VMEM((SWEEPS, 4, 2, 8, LANES), F32),
            pltpu.VMEM((SWEEPS - 1, 8, 2, 8, LANES), F32),
            pltpu.SemaphoreType.DMA((WIN - 1,)),
            pltpu.SemaphoreType.DMA((WIN - 1,)),
            pltpu.SemaphoreType.DMA((2 + SWEEPS, 4)),
            pltpu.SemaphoreType.DMA((2 + SWEEPS, 4)),
            pltpu.SemaphoreType.DMA((SWEEPS - 1, 8)),
            pltpu.SemaphoreType.DMA((SWEEPS - 1, 8)),
        ],
        compiler_params=pltpu.CompilerParams(
            collective_id=0, has_side_effects=True, vmem_limit_bytes=32 << 20
        ),
    )(
        *(
            pltpu.with_memory_space_constraint(array, pltpu.HBM)
            for array in (
                geometry.reshape(10 * TILES, LANES),
                dest_slot.reshape(TILES, 1, LANES),
                pairs.reshape(2 * TILES, LANES),
                colors,
                free_vel.reshape(6 * OWN, LANES),
                inertia.reshape(4 * OWN, LANES),
                exports,
            )
        )
    )
    return impulse.reshape(3, 1, TILES * LANES), velocity.reshape(6, 1, OWN * LANES)


def solution(mesh):
    n_sub, n_layer = mesh.shape["sub"], mesh.shape["layer"]
    placed = (
        P(None, "layer", "sub"),
        P("layer", "sub"),
        P(None, "layer", "sub"),
        P("layer", "sub"),
        P(None, "layer", "sub"),
        P(None, "layer", "sub"),
        P(None, "layer", "sub"),
    )
    return jax.shard_map(
        lambda *arrays: on_device(n_sub, n_layer, *arrays),
        mesh=mesh,
        in_specs=placed,
        out_specs=(P(None, "layer", "sub"), P(None, "layer", "sub")),
        check_vma=False,
    )
```

```python
import jax
import jax.numpy as jnp
from jax import lax
from jax.experimental import pallas as pl
from jax.experimental.pallas import tpu as pltpu
from jax.sharding import PartitionSpec as P

WIN = 4
SWEEPS = 3
NCOLOR = 4
LANES = 128
TILES = 12
ROWS = 16
CHUNK = 2
SPLIT = 256
OWN = 4
TABLE = 6

relaxation = 0.7
friction = 0.6
tangent_floor = 0.1

NEAR = ((-1, 0), (1, 0), (0, -1), (0, 1))
FAR = ((-2, 0), (2, 0), (0, -2), (0, 2), (-1, -1), (-1, 1), (1, -1), (1, 1))
MESH = pl.DeviceIdType.MESH
F32 = jnp.float32
BF16 = jnp.bfloat16
NT = (((1,), (1,)), ((), ()))


def cross(u, v):
    return [
        u[1] * v[2] - u[2] * v[1],
        u[2] * v[0] - u[0] * v[2],
        u[0] * v[1] - u[1] * v[0],
    ]


def dot3(u, v):
    return u[0] * v[0] + u[1] * v[1] + u[2] * v[2]


def take(row_block, index):
    return jnp.take_along_axis(row_block, index, axis=1, mode="promise_in_bounds")


def coarse(value):
    return value.astype(BF16).astype(F32)


def arm_block(arm, spin):
    return [
        spin[1] * arm[2] * arm[2] + spin[2] * arm[1] * arm[1],
        spin[0] * arm[2] * arm[2] + spin[2] * arm[0] * arm[0],
        spin[0] * arm[1] * arm[1] + spin[1] * arm[0] * arm[0],
        -spin[2] * arm[0] * arm[1],
        -spin[1] * arm[0] * arm[2],
        -spin[0] * arm[1] * arm[2],
    ]


def kernel(
    n_sub,
    n_layer,
    geo_hbm,
    slot_hbm,
    pairs_hbm,
    color_hbm,
    free_hbm,
    inertia_hbm,
    exports_hbm,
    imp_out,
    vel_out,
    geo_ref,
    slot_ref,
    pairs_ref,
    color_ref,
    free_ref,
    inertia_ref,
    exports_ref,
    load_sem,
    slot_hot,
    pair_hot,
    split_geo,
    relay_left,
    block_of,
    outgoing,
    incoming,
    geo,
    index,
    shade,
    const,
    impulse,
    push,
    table,
    start,
    inverse_list,
    weight,
    first_out,
    first_in,
    info,
    info_out,
    info_in,
    hints,
    sweep_out,
    near_in,
    far_in,
    relay_send,
    relay_recv,
    near_send,
    near_recv,
    far_send,
    far_recv,
):
    sub = lax.axis_index("sub")
    layer = lax.axis_index("layer")
    base = (sub // WIN) * WIN
    place = sub - base
    def mate(step):
        return base + lax.rem(place + step, WIN)

    def reach(right, up):
        there, above = sub + right, layer + up
        return (there >= 0) & (there < n_sub) & (above >= 0) & (above < n_layer)

    def device(right, up):
        return (
            lax.rem(sub + n_sub + right, n_sub),
            lax.rem(layer + n_layer + up, n_layer),
        )

    def start_all(copies):
        for copy, right, up in copies:
            pl.when(reach(right, up))(copy.start)

    def take_all(copies):
        for copy, right, up in copies:
            pl.when(reach(-right, -up))(copy.wait_recv)

    def sent_all(copies):
        for copy, right, up in copies:
            pl.when(reach(right, up))(copy.wait_send)

    first_in[...] = jnp.zeros_like(first_in)
    info_in[...] = jnp.zeros_like(info_in)
    near_in[...] = jnp.zeros_like(near_in)
    far_in[...] = jnp.zeros_like(far_in)

    barrier = pltpu.get_barrier_semaphore()
    greeted = jnp.int32(WIN - 1)
    for right, up in NEAR:

        @pl.when(reach(right, up))
        def _():
            pl.semaphore_signal(
                barrier, inc=1, device_id=device(right, up), device_id_type=MESH
            )

        greeted = greeted + reach(right, up).astype(jnp.int32)
    for step in range(1, WIN):
        pl.semaphore_signal(
            barrier, inc=1, device_id=(mate(step), layer), device_id_type=MESH
        )

    loads = [
        pltpu.make_async_copy(src, dst, load_sem.at[i])
        for i, (src, dst) in enumerate(
            (
                (free_hbm, free_ref),
                (inertia_hbm, inertia_ref),
                (exports_hbm, exports_ref),
                (geo_hbm, geo_ref),
                (slot_hbm.at[:, 0, :], slot_ref),
                (pairs_hbm, pairs_ref),
                (color_hbm, color_ref),
            )
        )
    ]
    for load in loads:
        load.start()

    def trade(step, source_of, dst):
        copies = []
        for right, up in NEAR:
            slot = NEAR.index((-right, -up))
            copy = pltpu.make_async_remote_copy(
                src_ref=source_of(0 if up == 0 else 1),
                dst_ref=dst.at[slot],
                send_sem=near_send.at[step, slot],
                recv_sem=near_recv.at[step, slot],
                device_id=device(right, up),
                device_id_type=MESH,
            )
            copies.append((copy, right, up))
        return copies

    def near_copies(sweep):
        return trade(
            2 + sweep, lambda pair: sweep_out.at[sweep, pl.ds(2 * pair, 2)], near_in.at[sweep]
        )

    def far_copies(sweep):
        copies = []
        for right, up in FAR:
            slot = FAR.index((-right, -up))
            first, count = 2 if right == 0 else 1, 1 if right == 0 or up == 0 else 2
            copy = pltpu.make_async_remote_copy(
                src_ref=sweep_out.at[sweep, pl.ds(first, count)],
                dst_ref=far_in.at[sweep, slot, pl.ds(0, count)],
                send_sem=far_send.at[sweep, slot],
                recv_sem=far_recv.at[sweep, slot],
                device_id=device(right, up),
                device_id_type=MESH,
            )
            copies.append((copy, right, up))
        return copies

    lane8 = lax.broadcasted_iota(jnp.int32, (8, LANES), 1)
    lane16 = lax.broadcasted_iota(jnp.int32, (ROWS, LANES), 1)

    table[...] = jnp.zeros_like(table)
    for load in loads[0:3]:
        load.wait()
    for h in range(OWN):
        cols = slice(h * LANES, (h + 1) * LANES)
        table[0:6, cols] = free_ref[pl.ds(h, 6, stride=OWN), :]
        table[8:12, cols] = inertia_ref[pl.ds(h, 4, stride=OWN), :]
    listed = [
        jnp.concatenate([exports_ref[1], exports_ref[0]], axis=1),
        jnp.concatenate([exports_ref[3], exports_ref[2]], axis=1),
    ]

    def pick_listed(pair, rows, source=table):
        high = jnp.broadcast_to(lax.shift_right_logical(listed[pair], 7), (rows, LANES))
        low = jnp.broadcast_to(lax.bitwise_and(listed[pair], 127), (rows, LANES))
        got = take(source[0:rows, 0:LANES], low)
        for h in range(1, OWN):
            block = take(source[0:rows, h * LANES : (h + 1) * LANES], low)
            got = jnp.where(high == h, block, got)
        return got

    for pair in range(2):
        first_out[pair] = pick_listed(pair, 16)

    for load in loads[3:]:
        load.wait()
    for t in range(TILES):
        cols = slice(t * LANES, (t + 1) * LANES)
        main = geo_ref[pl.ds(t, 8, stride=TILES), :]
        rest = geo_ref[pl.ds(8 * TILES + t, 2, stride=TILES), :]
        main_a = coarse(main)
        main_b = coarse(main - main_a)
        rest_a = coarse(rest)
        rest_b = coarse(rest - rest_a)
        split_geo[0:8, cols] = main_a
        split_geo[8:16, cols] = main_b
        split_geo[16:24, cols] = main - main_a - main_b
        split_geo[24:26, cols] = rest_a
        split_geo[26:28, cols] = rest_b
        split_geo[28:30, cols] = rest - rest_a - rest_b
        split_geo[30:32, cols] = jnp.zeros((2, LANES), F32)

    along = lax.broadcasted_iota(jnp.int32, (LANES, SPLIT), 1).astype(F32)

    def upright_hot(codes, hot):
        upright = jnp.transpose(lax.bitwise_and(codes, SPLIT - 1).astype(F32))
        for t in range(codes.shape[0]):
            hot[t * LANES : (t + 1) * LANES, :] = (
                (along == upright[:, t : t + 1]).astype(F32).astype(BF16)
            )

    upright_hot(slot_ref[...], slot_hot)

    def relay_copy(step):
        return pltpu.make_async_remote_copy(
            src_ref=outgoing.at[lax.rem(place + step, WIN)],
            dst_ref=incoming.at[step - 1],
            send_sem=relay_send.at[step - 1],
            recv_sem=relay_recv.at[step - 1],
            device_id=(mate(step), layer),
            device_id_type=MESH,
        )

    def arrange(target):
        for t in range(TILES):
            cols = slice(t * LANES, (t + 1) * LANES)
            part = lax.shift_right_logical(slot_ref[t : t + 1, :], 8)
            part = (part - (base + target) * TABLE).astype(F32)
            part = jnp.broadcast_to(part, (32, LANES)).astype(BF16)
            values = split_geo[:, cols].astype(BF16)
            for g in range(TABLE):
                relay_left[g * 32 : (g + 1) * 32, cols] = jnp.where(
                    part == jnp.asarray(g, BF16), values, jnp.zeros((32, LANES), BF16)
                )
        placed = jnp.dot(relay_left[...], slot_hot[...], preferred_element_type=F32)
        for g in range(TABLE):
            block = placed[g * 32 : (g + 1) * 32]
            main = block[0:8] + block[8:16] + block[16:24]
            rest = block[24:26] + block[26:28] + block[28:30]
            for j in range(2):
                cols = slice(j * LANES, (j + 1) * LANES)
                t = 2 * g + j
                outgoing[target, pl.ds(t, 8, stride=TILES), :] = main[:, cols]
                outgoing[target, pl.ds(8 * TILES + t, 2, stride=TILES), :] = rest[:, cols]

    def arrange_for(step, carry):
        arrange(lax.rem(place + step, WIN))
        return carry

    lax.fori_loop(1, WIN, arrange_for, 0)
    pl.semaphore_wait(barrier, greeted)
    first_trade = trade(0, lambda pair: first_out.at[pair], first_in)
    start_all(first_trade)
    for step in (2, 1, 3):
        relay_copy(step).start()
    arrange(place)

    index[...] = jnp.zeros_like(index)
    for e in range(2):
        index[e, 0:TILES] = pairs_ref[e * TILES : (e + 1) * TILES, :]
    upright_hot(pairs_ref[...], pair_hot)
    row16 = lax.broadcasted_iota(jnp.int32, (ROWS, LANES), 0)
    tint = jnp.full((ROWS, LANES), -1, jnp.int32)
    for t in range(TILES):
        tint = jnp.where(row16 == t, color_ref[0, t], tint)
    shade[...] = tint

    wide = lax.broadcasted_iota(jnp.int32, (16, 2 * LANES), 1)
    marks = jnp.where(
        lax.broadcasted_iota(jnp.int32, (16, 2 * LANES), 0) == wide // 64,
        lax.bitwise_and(wide, 127) + 1,
        0,
    )
    tall = lax.broadcasted_iota(jnp.int32, (OWN * LANES, LANES), 0)
    listed_hot = jnp.concatenate(
        [(tall == listed[pair]).astype(F32).astype(BF16) for pair in range(2)], axis=1
    )
    found = lax.dot_general(
        marks.astype(F32).astype(BF16), listed_hot, NT, preferred_element_type=F32
    )
    has_lower_sub = (sub > 0).astype(jnp.int32)
    has_higher_sub = (sub < n_sub - 1).astype(jnp.int32)
    has_lower_layer = (layer > 0).astype(jnp.int32)
    has_higher_layer = (layer < n_layer - 1).astype(jnp.int32)
    exists = (has_higher_sub, has_lower_sub, has_higher_layer, has_lower_layer)
    for h in range(OWN):
        cols = slice(h * LANES, (h + 1) * LANES)
        times = jnp.ones((8, LANES), F32)
        for half in range(4):
            spot = jnp.broadcast_to(found[half : half + 1, cols], (8, LANES))
            spot = spot.astype(jnp.int32) * exists[half] - 1
            inverse_list[h * 4 + half] = spot
            info[half : half + 1, cols] = spot[0:1].astype(F32)
            times = times + jnp.where(spot >= 0, 1.0, 0.0)
        weight[:, cols] = 1.0 / times
        info[4:8, cols] = (1.0 / times)[0:4]
    for pair in range(2):
        info_out[pair] = pick_listed(pair, 8, info)
    info_trade = trade(1, lambda pair: info_out.at[pair], info_in)
    start_all(info_trade)
    push[...] = jnp.zeros_like(push)
    zero16 = jnp.zeros((16, LANES), BF16)
    for t in range(2 * TILES):
        part = lax.shift_right_logical(pairs_ref[t : t + 1, :], 8).astype(F32)
        block_of[t] = jnp.broadcast_to(part, (16, LANES)).astype(BF16)
    impulse[...] = jnp.zeros_like(impulse)
    geo[...] = jnp.ones_like(geo)

    def keep(flag, value):
        return jnp.where(flag > 0, value, 0.0)

    def halves(lane, landed):
        return (
            jnp.where(
                lane < 64, keep(has_lower_sub, landed[0]), keep(has_higher_sub, landed[1])
            ),
            jnp.where(
                lane < 64, keep(has_lower_layer, landed[2]), keep(has_higher_layer, landed[3])
            ),
        )

    take_all(first_trade)
    table[:, 512:640], table[:, 640:768] = halves(lane16, [first_in[slot] for slot in range(4)])

    def pick(component, e):
        high = lax.shift_right_logical(index[e], 7)
        low = lax.bitwise_and(index[e], 127)
        got = None
        for h in range(TABLE if e else OWN):
            row = table[component : component + 1, h * LANES : (h + 1) * LANES]
            block = take(jnp.broadcast_to(row, (ROWS, LANES)), low)
            got = block if h == 0 else jnp.where(high == h, block, got)
        return got

    props_a = [pick(8 + i, 0) for i in range(4)]
    props_b = [pick(8 + i, 1) for i in range(4)]
    for i in range(4):
        const[20 + i] = props_a[i]
        const[24 + i] = props_b[i]

    for step in range(1, WIN):
        relay_copy(step).wait_recv()
    for c in range(10):
        rows = slice(c * TILES, (c + 1) * TILES)
        geo[c, 0:TILES] = (
            outgoing[place, rows] + incoming[0, rows] + incoming[1, rows] + incoming[2, rows]
        )

    raw = [geo[i] for i in range(3)]
    length = jnp.sqrt(dot3(raw, raw))
    normal = [r / length for r in raw]
    side = jnp.sqrt(normal[1] * normal[1] + normal[2] * normal[2])
    one_y = normal[2] / side
    one_z = -normal[1] / side
    two = cross(normal, [jnp.zeros_like(side), one_y, one_z])
    frame = [normal, [jnp.zeros_like(side), one_y, one_z], two]
    entry_a = arm_block([geo[3 + i] for i in range(3)], props_a[1:])
    entry_b = arm_block([geo[6 + i] for i in range(3)], props_b[1:])
    mass = props_a[0] + props_b[0]
    xx, yy, zz, xy, xz, yz = [a + b for a, b in zip(entry_a, entry_b)]
    xx, yy, zz = mass + xx, mass + yy, mass + zz
    cxx = yy * zz - yz * yz
    cxy = xz * yz - xy * zz
    cxz = xy * yz - xz * yy
    cyy = xx * zz - xz * xz
    cyz = xy * xz - xx * yz
    czz = xx * yy - xy * xy
    scale = relaxation / (xx * cxx + xy * cxy + xz * cxz)
    solve = [[cxx, cxy, cxz], [cxy, cyy, cyz], [cxz, cyz, czz]]
    for i in range(3):
        row = [dot3(frame[i], solve[j]) * scale for j in range(3)]
        for j in range(3):
            const[8 + 3 * i + j] = row[j]
        const[17 + i] = dot3(row, normal) * geo[9]
    for i in range(3):
        const[i] = normal[i]
        const[5 + i] = two[i]
    const[3] = one_y
    const[4] = one_z

    def color_pass(color, carry):
        vel_a = [pick(c, 0) for c in range(6)]
        vel_b = [pick(c, 1) for c in range(6)]
        arm_a = [geo[3 + i] for i in range(3)]
        arm_b = [geo[6 + i] for i in range(3)]
        turn_a = cross(vel_a[3:], arm_a)
        turn_b = cross(vel_b[3:], arm_b)
        relative = [vel_a[i] + turn_a[i] - vel_b[i] - turn_b[i] for i in range(3)]
        old = [impulse[i] for i in range(3)]
        trial = [
            old[i]
            - dot3([const[8 + 3 * i + j] for j in range(3)], relative)
            - const[17 + i]
            for i in range(3)
        ]
        press = jnp.maximum(trial[0], 0.0)
        slide = jnp.sqrt(trial[1] * trial[1] + trial[2] * trial[2])
        factor = jnp.minimum(1.0, friction * press / jnp.maximum(slide, tangent_floor))
        active = shade[...] == color
        new = [
            jnp.where(active, value, was)
            for value, was in zip([press, trial[1] * factor, trial[2] * factor], old)
        ]
        change = [a - b for a, b in zip(new, old)]
        for i in range(3):
            impulse[i] = new[i]
        force = [
            const[0] * change[0] + const[5] * change[2],
            const[1] * change[0] + const[3] * change[1] + const[6] * change[2],
            const[2] * change[0] + const[4] * change[1] + const[7] * change[2],
        ]
        torque_a = cross(arm_a, force)
        torque_b = cross(arm_b, force)
        for i in range(3):
            lin = slice(i * TILES, (i + 1) * TILES)
            ang = slice((3 + i) * TILES, (4 + i) * TILES)
            push[0, lin] = (const[20] * force[i])[0:TILES]
            push[1, lin] = (-const[24] * force[i])[0:TILES]
            push[0, ang] = (const[21 + i] * torque_a[i])[0:TILES]
            push[1, ang] = (-const[25 + i] * torque_b[i])[0:TILES]
        lefts = []
        for e in range(2):
            for t in range(TILES):
                value = push[e, pl.ds(t, 8, stride=TILES), :]
                upper = coarse(value)
                both = jnp.concatenate([upper, value - upper], axis=0).astype(BF16)
                lefts.append(
                    jnp.concatenate(
                        [
                            jnp.where(block_of[e * TILES + t] == jnp.asarray(h, BF16), both, zero16)
                            for h in range(2 + e)
                        ],
                        axis=0,
                    )
                )
        def product(first, count):
            return jnp.dot(
                jnp.concatenate(lefts[first : first + count], axis=1),
                pair_hot[first * LANES : (first + count) * LANES, :],
                preferred_element_type=F32,
            )

        total_a = sum(product(f, CHUNK) for f in range(0, TILES, CHUNK))
        total_b = sum(product(f, CHUNK) for f in range(TILES, 2 * TILES, CHUNK))
        for h in range(3):
            cols = slice(h * SPLIT, (h + 1) * SPLIT)
            gain = total_b[h * 16 : h * 16 + 8] + total_b[h * 16 + 8 : h * 16 + 16]
            if h < 2:
                gain = gain + total_a[h * 16 : h * 16 + 8] + total_a[h * 16 + 8 : h * 16 + 16]
            table[0:8, cols] = table[0:8, cols] + gain
        return carry

    take_all(info_trade)
    hints[0], hints[1] = halves(lane8, [info_in[slot] for slot in range(4)])

    def pull(row_block, pair, row):
        spot = jnp.broadcast_to(hints[pair, row : row + 1], (8, LANES)).astype(jnp.int32)
        return jnp.where(spot >= 0, take(row_block, jnp.maximum(spot, 0)), 0.0)

    def one_sweep(sweep, carry):
        start[...] = table[0:8, :]
        lax.fori_loop(0, NCOLOR, color_pass, 0)
        on = sweep + 1 < SWEEPS
        copied = [slice((OWN + pair) * LANES, (OWN + pair + 1) * LANES) for pair in range(2)]
        for pair in range(2):
            sweep_out[sweep, 1 + pair] = table[0:8, copied[pair]] - start[:, copied[pair]]

        @pl.when(on)
        def _():
            start_all(far_copies(sweep))

        for pair in range(2):
            sweep_out[sweep, 3 * pair] = pick_listed(pair, 8)
        near = near_copies(sweep)
        start_all(near)
        take_all(near)
        arrived = [
            jnp.where(lane8 < 64, near_in[sweep, 1, 1], near_in[sweep, 0, 1]),
            jnp.where(lane8 < 64, near_in[sweep, 3, 0], near_in[sweep, 2, 0]),
        ]
        for h in range(OWN):
            cols = slice(h * LANES, (h + 1) * LANES)
            total = table[0:8, cols] - start[:, cols]
            for half in range(4):
                spot = inverse_list[h * 4 + half]
                total = total + jnp.where(
                    spot >= 0, take(arrived[half // 2], jnp.maximum(spot, 0)), 0.0
                )
            table[0:8, cols] = start[:, cols] + total * weight[:, cols]

        @pl.when(on)
        def _():
            take_all(far_copies(sweep))

            def landed(right, up, pair):
                straight = right == 0 or up == 0
                return far_in[sweep, FAR.index((right, up)), 0 if straight else pair]

            left = lane8 < 64
            for pair in range(2):
                if pair == 0:
                    listed_now = jnp.where(left, near_in[sweep, 0, 0], near_in[sweep, 1, 0])
                    beyond = jnp.where(left, landed(2, 0, 0), landed(-2, 0, 0))
                    side_a = jnp.where(left, landed(-1, 1, 1), landed(-1, -1, 1))
                    side_b = jnp.where(left, landed(1, 1, 1), landed(1, -1, 1))
                else:
                    listed_now = jnp.where(left, near_in[sweep, 2, 1], near_in[sweep, 3, 1])
                    beyond = jnp.where(left, landed(0, 2, 1), landed(0, -2, 1))
                    side_a = jnp.where(left, landed(1, -1, 0), landed(-1, -1, 0))
                    side_b = jnp.where(left, landed(1, 1, 0), landed(-1, 1, 0))
                was = start[:, copied[pair]]
                total = (listed_now - was) + sweep_out[sweep, 1 + pair]
                total = total + jnp.where(
                    left, pull(beyond, pair, 2 * pair + 1), pull(beyond, pair, 2 * pair)
                )
                for row in (2 - 2 * pair, 3 - 2 * pair):
                    total = total + jnp.where(
                        left, pull(side_a, pair, row), pull(side_b, pair, row)
                    )
                table[0:8, copied[pair]] = was + total * hints[pair, 4:5]
            sent_all(far_copies(sweep))

        sent_all(near)
        return carry

    lax.fori_loop(0, SWEEPS, one_sweep, 0)
    for h in range(OWN):
        vel_out[pl.ds(h, 6, stride=OWN), :] = table[0:6, h * LANES : (h + 1) * LANES]
    for i in range(3):
        imp_out[i * TILES : (i + 1) * TILES, :] = impulse[i, 0:TILES]
    sent_all(first_trade + info_trade)
    for step in range(1, WIN):
        relay_copy(step).wait_send()


def on_device(n_sub, n_layer, geometry, dest_slot, pairs, colors, free_vel, inertia, exports):
    vmem = pl.BlockSpec(memory_space=pltpu.VMEM)
    hbm = pl.BlockSpec(memory_space=pltpu.HBM)
    impulse, velocity = pl.pallas_call(
        lambda *refs: kernel(n_sub, n_layer, *refs),
        out_shape=(
            jax.ShapeDtypeStruct((3 * TILES, LANES), F32),
            jax.ShapeDtypeStruct((6 * OWN, LANES), F32),
        ),
        in_specs=[hbm] * 7,
        out_specs=(vmem, vmem),
        scratch_shapes=[
            pltpu.VMEM((10 * TILES, LANES), F32),
            pltpu.VMEM((TILES, LANES), jnp.int32),
            pltpu.VMEM((2 * TILES, LANES), jnp.int32),
            pltpu.SMEM((1, TILES), jnp.int32),
            pltpu.VMEM((6 * OWN, LANES), F32),
            pltpu.VMEM((4 * OWN, LANES), F32),
            pltpu.VMEM((4, 1, 64), jnp.int32),
            pltpu.SemaphoreType.DMA((7,)),
            pltpu.VMEM((TILES * LANES, SPLIT), BF16),
            pltpu.VMEM((2 * TILES * LANES, SPLIT), BF16),
            pltpu.VMEM((32, TILES * LANES), F32),
            pltpu.VMEM((192, TILES * LANES), BF16),
            pltpu.VMEM((2 * TILES, 16, LANES), BF16),
            pltpu.VMEM((WIN, 10 * TILES, LANES), F32),
            pltpu.VMEM((WIN - 1, 10 * TILES, LANES), F32),
            pltpu.VMEM((10, ROWS, LANES), F32),
            pltpu.VMEM((2, ROWS, LANES), jnp.int32),
            pltpu.VMEM((ROWS, LANES), jnp.int32),
            pltpu.VMEM((28, ROWS, LANES), F32),
            pltpu.VMEM((3, ROWS, LANES), F32),
            pltpu.VMEM((2, 8 * TILES, LANES), F32),
            pltpu.VMEM((16, TABLE * LANES), F32),
            pltpu.VMEM((8, TABLE * LANES), F32),
            pltpu.VMEM((16, 8, LANES), jnp.int32),
            pltpu.VMEM((8, OWN * LANES), F32),
            pltpu.VMEM((2, 16, LANES), F32),
            pltpu.VMEM((4, 16, LANES), F32),
            pltpu.VMEM((8, OWN * LANES), F32),
            pltpu.VMEM((2, 8, LANES), F32),
            pltpu.VMEM((4, 8, LANES), F32),
            pltpu.VMEM((2, 8, LANES), F32),
            pltpu.VMEM((SWEEPS, 4, 8, LANES), F32),
            pltpu.VMEM((SWEEPS, 4, 2, 8, LANES), F32),
            pltpu.VMEM((SWEEPS - 1, 8, 2, 8, LANES), F32),
            pltpu.SemaphoreType.DMA((WIN - 1,)),
            pltpu.SemaphoreType.DMA((WIN - 1,)),
            pltpu.SemaphoreType.DMA((2 + SWEEPS, 4)),
            pltpu.SemaphoreType.DMA((2 + SWEEPS, 4)),
            pltpu.SemaphoreType.DMA((SWEEPS - 1, 8)),
            pltpu.SemaphoreType.DMA((SWEEPS - 1, 8)),
        ],
        compiler_params=pltpu.CompilerParams(
            collective_id=0, has_side_effects=True, vmem_limit_bytes=32 << 20
        ),
    )(
        *(
            pltpu.with_memory_space_constraint(array, pltpu.HBM)
            for array in (
                geometry.reshape(10 * TILES, LANES),
                dest_slot.reshape(TILES, 1, LANES),
                pairs.reshape(2 * TILES, LANES),
                colors,
                free_vel.reshape(6 * OWN, LANES),
                inertia.reshape(4 * OWN, LANES),
                exports,
            )
        )
    )
    return impulse.reshape(3, 1, TILES * LANES), velocity.reshape(6, 1, OWN * LANES)


def solution(mesh):
    n_sub, n_layer = mesh.shape["sub"], mesh.shape["layer"]
    placed = (
        P(None, "layer", "sub"),
        P("layer", "sub"),
        P(None, "layer", "sub"),
        P("layer", "sub"),
        P(None, "layer", "sub"),
        P(None, "layer", "sub"),
        P(None, "layer", "sub"),
    )
    return jax.shard_map(
        lambda *arrays: on_device(n_sub, n_layer, *arrays),
        mesh=mesh,
        in_specs=placed,
        out_specs=(P(None, "layer", "sub"), P(None, "layer", "sub")),
        check_vma=False,
    )
```

```python
import jax
import jax.numpy as jnp
from jax import lax
from jax.experimental import pallas as pl
from jax.experimental.pallas import tpu as pltpu
from jax.sharding import PartitionSpec as P

WIN = 4
SWEEPS = 3
NCOLOR = 4
LANES = 128
TILES = 12
ROWS = 16
CHUNK = 2
SPLIT = 256
OWN = 4
TABLE = 6

relaxation = 0.7
friction = 0.6
tangent_floor = 0.1

NEAR = ((-1, 0), (1, 0), (0, -1), (0, 1))
FAR = ((-2, 0), (2, 0), (0, -2), (0, 2), (-1, -1), (-1, 1), (1, -1), (1, 1))
MESH = pl.DeviceIdType.MESH
F32 = jnp.float32
BF16 = jnp.bfloat16
NT = (((1,), (1,)), ((), ()))


def cross(u, v):
    return [
        u[1] * v[2] - u[2] * v[1],
        u[2] * v[0] - u[0] * v[2],
        u[0] * v[1] - u[1] * v[0],
    ]


def dot3(u, v):
    return u[0] * v[0] + u[1] * v[1] + u[2] * v[2]


def take(row_block, index):
    return jnp.take_along_axis(row_block, index, axis=1, mode="promise_in_bounds")


def coarse(value):
    return value.astype(BF16).astype(F32)


def arm_block(arm, spin):
    return [
        spin[1] * arm[2] * arm[2] + spin[2] * arm[1] * arm[1],
        spin[0] * arm[2] * arm[2] + spin[2] * arm[0] * arm[0],
        spin[0] * arm[1] * arm[1] + spin[1] * arm[0] * arm[0],
        -spin[2] * arm[0] * arm[1],
        -spin[1] * arm[0] * arm[2],
        -spin[0] * arm[1] * arm[2],
    ]


def kernel(
    n_sub,
    n_layer,
    geo_hbm,
    slot_hbm,
    pairs_hbm,
    color_hbm,
    free_hbm,
    inertia_hbm,
    exports_hbm,
    imp_out,
    vel_out,
    geo_ref,
    slot_ref,
    pairs_ref,
    color_ref,
    free_ref,
    inertia_ref,
    exports_ref,
    load_sem,
    slot_hot,
    pair_hot,
    split_geo,
    relay_left,
    block_of,
    outgoing,
    incoming,
    geo,
    index,
    shade,
    const,
    impulse,
    push,
    table,
    start,
    inverse_list,
    weight,
    first_out,
    first_in,
    info,
    info_out,
    info_in,
    hints,
    sweep_out,
    near_in,
    far_in,
    relay_send,
    relay_recv,
    near_send,
    near_recv,
    far_send,
    far_recv,
):
    sub = lax.axis_index("sub")
    layer = lax.axis_index("layer")
    base = (sub // WIN) * WIN
    place = sub - base
    def mate(step):
        return base + lax.rem(place + step, WIN)

    def reach(right, up):
        there, above = sub + right, layer + up
        return (there >= 0) & (there < n_sub) & (above >= 0) & (above < n_layer)

    def device(right, up):
        return (
            lax.rem(sub + n_sub + right, n_sub),
            lax.rem(layer + n_layer + up, n_layer),
        )

    def start_all(copies):
        for copy, right, up in copies:
            pl.when(reach(right, up))(copy.start)

    def take_all(copies):
        for copy, right, up in copies:
            pl.when(reach(-right, -up))(copy.wait_recv)

    def sent_all(copies):
        for copy, right, up in copies:
            pl.when(reach(right, up))(copy.wait_send)

    first_in[...] = jnp.zeros_like(first_in)
    info_in[...] = jnp.zeros_like(info_in)
    near_in[...] = jnp.zeros_like(near_in)
    far_in[...] = jnp.zeros_like(far_in)

    barrier = pltpu.get_barrier_semaphore()
    greeted = jnp.int32(WIN - 1)
    for right, up in NEAR:

        @pl.when(reach(right, up))
        def _():
            pl.semaphore_signal(
                barrier, inc=1, device_id=device(right, up), device_id_type=MESH
            )

        greeted = greeted + reach(right, up).astype(jnp.int32)
    for step in range(1, WIN):
        pl.semaphore_signal(
            barrier, inc=1, device_id=(mate(step), layer), device_id_type=MESH
        )

    loads = [
        pltpu.make_async_copy(src, dst, load_sem.at[i])
        for i, (src, dst) in enumerate(
            (
                (free_hbm, free_ref),
                (inertia_hbm, inertia_ref),
                (exports_hbm, exports_ref),
                (geo_hbm, geo_ref),
                (slot_hbm.at[:, 0, :], slot_ref),
                (pairs_hbm, pairs_ref),
                (color_hbm, color_ref),
            )
        )
    ]
    for load in loads:
        load.start()

    def trade(step, source_of, dst):
        copies = []
        for right, up in NEAR:
            slot = NEAR.index((-right, -up))
            copy = pltpu.make_async_remote_copy(
                src_ref=source_of(0 if up == 0 else 1),
                dst_ref=dst.at[slot],
                send_sem=near_send.at[step, slot],
                recv_sem=near_recv.at[step, slot],
                device_id=device(right, up),
                device_id_type=MESH,
            )
            copies.append((copy, right, up))
        return copies

    def near_copies(sweep):
        return trade(
            2 + sweep, lambda pair: sweep_out.at[sweep, pl.ds(2 * pair, 2)], near_in.at[sweep]
        )

    def far_copies(sweep):
        copies = []
        for right, up in FAR:
            slot = FAR.index((-right, -up))
            first, count = 2 if right == 0 else 1, 1 if right == 0 or up == 0 else 2
            copy = pltpu.make_async_remote_copy(
                src_ref=sweep_out.at[sweep, pl.ds(first, count)],
                dst_ref=far_in.at[sweep, slot, pl.ds(0, count)],
                send_sem=far_send.at[sweep, slot],
                recv_sem=far_recv.at[sweep, slot],
                device_id=device(right, up),
                device_id_type=MESH,
            )
            copies.append((copy, right, up))
        return copies

    lane8 = lax.broadcasted_iota(jnp.int32, (8, LANES), 1)
    lane16 = lax.broadcasted_iota(jnp.int32, (ROWS, LANES), 1)

    table[...] = jnp.zeros_like(table)
    for load in loads[0:3]:
        load.wait()
    for h in range(OWN):
        cols = slice(h * LANES, (h + 1) * LANES)
        table[0:6, cols] = free_ref[pl.ds(h, 6, stride=OWN), :]
        table[8:12, cols] = inertia_ref[pl.ds(h, 4, stride=OWN), :]
    listed = [
        jnp.concatenate([exports_ref[1], exports_ref[0]], axis=1),
        jnp.concatenate([exports_ref[3], exports_ref[2]], axis=1),
    ]

    def pick_listed(pair, rows, source=table):
        high = jnp.broadcast_to(lax.shift_right_logical(listed[pair], 7), (rows, LANES))
        low = jnp.broadcast_to(lax.bitwise_and(listed[pair], 127), (rows, LANES))
        got = take(source[0:rows, 0:LANES], low)
        for h in range(1, OWN):
            block = take(source[0:rows, h * LANES : (h + 1) * LANES], low)
            got = jnp.where(high == h, block, got)
        return got

    for pair in range(2):
        first_out[pair] = pick_listed(pair, 16)

    for load in loads[3:]:
        load.wait()
    for t in range(TILES):
        cols = slice(t * LANES, (t + 1) * LANES)
        main = geo_ref[pl.ds(t, 8, stride=TILES), :]
        rest = geo_ref[pl.ds(8 * TILES + t, 2, stride=TILES), :]
        main_a = coarse(main)
        main_b = coarse(main - main_a)
        rest_a = coarse(rest)
        rest_b = coarse(rest - rest_a)
        split_geo[0:8, cols] = main_a
        split_geo[8:16, cols] = main_b
        split_geo[16:24, cols] = main - main_a - main_b
        split_geo[24:26, cols] = rest_a
        split_geo[26:28, cols] = rest_b
        split_geo[28:30, cols] = rest - rest_a - rest_b
        split_geo[30:32, cols] = jnp.zeros((2, LANES), F32)

    along = lax.broadcasted_iota(jnp.int32, (LANES, SPLIT), 1).astype(F32)

    def upright_hot(codes, hot):
        upright = jnp.transpose(lax.bitwise_and(codes, SPLIT - 1).astype(F32))
        for t in range(codes.shape[0]):
            hot[t * LANES : (t + 1) * LANES, :] = (
                (along == upright[:, t : t + 1]).astype(F32).astype(BF16)
            )

    upright_hot(slot_ref[...], slot_hot)

    def relay_copy(step):
        return pltpu.make_async_remote_copy(
            src_ref=outgoing.at[lax.rem(place + step, WIN)],
            dst_ref=incoming.at[step - 1],
            send_sem=relay_send.at[step - 1],
            recv_sem=relay_recv.at[step - 1],
            device_id=(mate(step), layer),
            device_id_type=MESH,
        )

    def arrange(target):
        for t in range(TILES):
            cols = slice(t * LANES, (t + 1) * LANES)
            part = lax.shift_right_logical(slot_ref[t : t + 1, :], 8)
            part = (part - (base + target) * TABLE).astype(F32)
            part = jnp.broadcast_to(part, (32, LANES)).astype(BF16)
            values = split_geo[:, cols].astype(BF16)
            for g in range(TABLE):
                relay_left[g * 32 : (g + 1) * 32, cols] = jnp.where(
                    part == jnp.asarray(g, BF16), values, jnp.zeros((32, LANES), BF16)
                )
        placed = jnp.dot(relay_left[...], slot_hot[...], preferred_element_type=F32)
        for g in range(TABLE):
            block = placed[g * 32 : (g + 1) * 32]
            main = block[0:8] + block[8:16] + block[16:24]
            rest = block[24:26] + block[26:28] + block[28:30]
            for j in range(2):
                cols = slice(j * LANES, (j + 1) * LANES)
                t = 2 * g + j
                outgoing[target, pl.ds(t, 8, stride=TILES), :] = main[:, cols]
                outgoing[target, pl.ds(8 * TILES + t, 2, stride=TILES), :] = rest[:, cols]

    def arrange_for(step, carry):
        arrange(lax.rem(place + step, WIN))
        return carry

    lax.fori_loop(1, 2, arrange_for, 0)
    pl.semaphore_wait(barrier, greeted)
    first_trade = trade(0, lambda pair: first_out.at[pair], first_in)
    start_all(first_trade)
    relay_copy(1).start()

    def arrange_send(step, carry):
        arrange(lax.rem(place + step, WIN))
        relay_copy(step).start()
        return carry

    lax.fori_loop(2, 4, arrange_send, 0)
    arrange(place)

    index[...] = jnp.zeros_like(index)
    for e in range(2):
        index[e, 0:TILES] = pairs_ref[e * TILES : (e + 1) * TILES, :]
    upright_hot(pairs_ref[...], pair_hot)
    row16 = lax.broadcasted_iota(jnp.int32, (ROWS, LANES), 0)
    tint = jnp.full((ROWS, LANES), -1, jnp.int32)
    for t in range(TILES):
        tint = jnp.where(row16 == t, color_ref[0, t], tint)
    shade[...] = tint

    wide = lax.broadcasted_iota(jnp.int32, (16, 2 * LANES), 1)
    marks = jnp.where(
        lax.broadcasted_iota(jnp.int32, (16, 2 * LANES), 0) == wide // 64,
        lax.bitwise_and(wide, 127) + 1,
        0,
    )
    tall = lax.broadcasted_iota(jnp.int32, (OWN * LANES, LANES), 0)
    listed_hot = jnp.concatenate(
        [(tall == listed[pair]).astype(F32).astype(BF16) for pair in range(2)], axis=1
    )
    found = lax.dot_general(
        marks.astype(F32).astype(BF16), listed_hot, NT, preferred_element_type=F32
    )
    has_lower_sub = (sub > 0).astype(jnp.int32)
    has_higher_sub = (sub < n_sub - 1).astype(jnp.int32)
    has_lower_layer = (layer > 0).astype(jnp.int32)
    has_higher_layer = (layer < n_layer - 1).astype(jnp.int32)
    exists = (has_higher_sub, has_lower_sub, has_higher_layer, has_lower_layer)
    for h in range(OWN):
        cols = slice(h * LANES, (h + 1) * LANES)
        times = jnp.ones((8, LANES), F32)
        for half in range(4):
            spot = jnp.broadcast_to(found[half : half + 1, cols], (8, LANES))
            spot = spot.astype(jnp.int32) * exists[half] - 1
            inverse_list[h * 4 + half] = spot
            info[half : half + 1, cols] = spot[0:1].astype(F32)
            times = times + jnp.where(spot >= 0, 1.0, 0.0)
        weight[:, cols] = 1.0 / times
        info[4:8, cols] = (1.0 / times)[0:4]
    for pair in range(2):
        info_out[pair] = pick_listed(pair, 8, info)
    info_trade = trade(1, lambda pair: info_out.at[pair], info_in)
    start_all(info_trade)
    push[...] = jnp.zeros_like(push)
    zero16 = jnp.zeros((16, LANES), BF16)
    for t in range(2 * TILES):
        part = lax.shift_right_logical(pairs_ref[t : t + 1, :], 8).astype(F32)
        block_of[t] = jnp.broadcast_to(part, (16, LANES)).astype(BF16)
    impulse[...] = jnp.zeros_like(impulse)
    geo[...] = jnp.ones_like(geo)

    def keep(flag, value):
        return jnp.where(flag > 0, value, 0.0)

    def halves(lane, landed):
        return (
            jnp.where(
                lane < 64, keep(has_lower_sub, landed[0]), keep(has_higher_sub, landed[1])
            ),
            jnp.where(
                lane < 64, keep(has_lower_layer, landed[2]), keep(has_higher_layer, landed[3])
            ),
        )

    take_all(first_trade)
    table[:, 512:640], table[:, 640:768] = halves(lane16, [first_in[slot] for slot in range(4)])

    def pick(component, e):
        high = lax.shift_right_logical(index[e], 7)
        low = lax.bitwise_and(index[e], 127)
        got = None
        for h in range(TABLE if e else OWN):
            row = table[component : component + 1, h * LANES : (h + 1) * LANES]
            block = take(jnp.broadcast_to(row, (ROWS, LANES)), low)
            got = block if h == 0 else jnp.where(high == h, block, got)
        return got

    props_a = [pick(8 + i, 0) for i in range(4)]
    props_b = [pick(8 + i, 1) for i in range(4)]
    for i in range(4):
        const[20 + i] = props_a[i]
        const[24 + i] = props_b[i]

    for step in range(1, WIN):
        relay_copy(step).wait_recv()
    for c in range(10):
        rows = slice(c * TILES, (c + 1) * TILES)
        geo[c, 0:TILES] = (
            outgoing[place, rows] + incoming[0, rows] + incoming[1, rows] + incoming[2, rows]
        )

    raw = [geo[i] for i in range(3)]
    length = jnp.sqrt(dot3(raw, raw))
    normal = [r / length for r in raw]
    side = jnp.sqrt(normal[1] * normal[1] + normal[2] * normal[2])
    one_y = normal[2] / side
    one_z = -normal[1] / side
    two = cross(normal, [jnp.zeros_like(side), one_y, one_z])
    frame = [normal, [jnp.zeros_like(side), one_y, one_z], two]
    entry_a = arm_block([geo[3 + i] for i in range(3)], props_a[1:])
    entry_b = arm_block([geo[6 + i] for i in range(3)], props_b[1:])
    mass = props_a[0] + props_b[0]
    xx, yy, zz, xy, xz, yz = [a + b for a, b in zip(entry_a, entry_b)]
    xx, yy, zz = mass + xx, mass + yy, mass + zz
    cxx = yy * zz - yz * yz
    cxy = xz * yz - xy * zz
    cxz = xy * yz - xz * yy
    cyy = xx * zz - xz * xz
    cyz = xy * xz - xx * yz
    czz = xx * yy - xy * xy
    scale = relaxation / (xx * cxx + xy * cxy + xz * cxz)
    solve = [[cxx, cxy, cxz], [cxy, cyy, cyz], [cxz, cyz, czz]]
    for i in range(3):
        row = [dot3(frame[i], solve[j]) * scale for j in range(3)]
        for j in range(3):
            const[8 + 3 * i + j] = row[j]
        const[17 + i] = dot3(row, normal) * geo[9]
    for i in range(3):
        const[i] = normal[i]
        const[5 + i] = two[i]
    const[3] = one_y
    const[4] = one_z

    def color_pass(color, carry):
        vel_a = [pick(c, 0) for c in range(6)]
        vel_b = [pick(c, 1) for c in range(6)]
        arm_a = [geo[3 + i] for i in range(3)]
        arm_b = [geo[6 + i] for i in range(3)]
        turn_a = cross(vel_a[3:], arm_a)
        turn_b = cross(vel_b[3:], arm_b)
        relative = [vel_a[i] + turn_a[i] - vel_b[i] - turn_b[i] for i in range(3)]
        old = [impulse[i] for i in range(3)]
        trial = [
            old[i]
            - dot3([const[8 + 3 * i + j] for j in range(3)], relative)
            - const[17 + i]
            for i in range(3)
        ]
        press = jnp.maximum(trial[0], 0.0)
        slide = jnp.sqrt(trial[1] * trial[1] + trial[2] * trial[2])
        factor = jnp.minimum(1.0, friction * press / jnp.maximum(slide, tangent_floor))
        active = shade[...] == color
        new = [
            jnp.where(active, value, was)
            for value, was in zip([press, trial[1] * factor, trial[2] * factor], old)
        ]
        change = [a - b for a, b in zip(new, old)]
        for i in range(3):
            impulse[i] = new[i]
        force = [
            const[0] * change[0] + const[5] * change[2],
            const[1] * change[0] + const[3] * change[1] + const[6] * change[2],
            const[2] * change[0] + const[4] * change[1] + const[7] * change[2],
        ]
        torque_a = cross(arm_a, force)
        torque_b = cross(arm_b, force)
        for i in range(3):
            lin = slice(i * TILES, (i + 1) * TILES)
            ang = slice((3 + i) * TILES, (4 + i) * TILES)
            push[0, lin] = (const[20] * force[i])[0:TILES]
            push[1, lin] = (-const[24] * force[i])[0:TILES]
            push[0, ang] = (const[21 + i] * torque_a[i])[0:TILES]
            push[1, ang] = (-const[25 + i] * torque_b[i])[0:TILES]
        lefts = []
        for e in range(2):
            for t in range(TILES):
                value = push[e, pl.ds(t, 8, stride=TILES), :]
                upper = coarse(value)
                both = jnp.concatenate([upper, value - upper], axis=0).astype(BF16)
                lefts.append(
                    jnp.concatenate(
                        [
                            jnp.where(block_of[e * TILES + t] == jnp.asarray(h, BF16), both, zero16)
                            for h in range(2 + e)
                        ],
                        axis=0,
                    )
                )
        def product(first, count):
            return jnp.dot(
                jnp.concatenate(lefts[first : first + count], axis=1),
                pair_hot[first * LANES : (first + count) * LANES, :],
                preferred_element_type=F32,
            )

        total_a = sum(product(f, CHUNK) for f in range(0, TILES, CHUNK))
        total_b = sum(product(f, CHUNK) for f in range(TILES, 2 * TILES, CHUNK))
        for h in range(3):
            cols = slice(h * SPLIT, (h + 1) * SPLIT)
            gain = total_b[h * 16 : h * 16 + 8] + total_b[h * 16 + 8 : h * 16 + 16]
            if h < 2:
                gain = gain + total_a[h * 16 : h * 16 + 8] + total_a[h * 16 + 8 : h * 16 + 16]
            table[0:8, cols] = table[0:8, cols] + gain
        return carry

    take_all(info_trade)
    hints[0], hints[1] = halves(lane8, [info_in[slot] for slot in range(4)])

    def pull(row_block, pair, row):
        spot = jnp.broadcast_to(hints[pair, row : row + 1], (8, LANES)).astype(jnp.int32)
        return jnp.where(spot >= 0, take(row_block, jnp.maximum(spot, 0)), 0.0)

    def one_sweep(sweep, carry):
        start[...] = table[0:8, :]
        lax.fori_loop(0, NCOLOR, color_pass, 0)
        on = sweep + 1 < SWEEPS
        copied = [slice((OWN + pair) * LANES, (OWN + pair + 1) * LANES) for pair in range(2)]
        for pair in range(2):
            sweep_out[sweep, 1 + pair] = table[0:8, copied[pair]] - start[:, copied[pair]]

        @pl.when(on)
        def _():
            start_all(far_copies(sweep))

        for pair in range(2):
            sweep_out[sweep, 3 * pair] = pick_listed(pair, 8)
        near = near_copies(sweep)
        start_all(near)
        take_all(near)
        arrived = [
            jnp.where(lane8 < 64, near_in[sweep, 1, 1], near_in[sweep, 0, 1]),
            jnp.where(lane8 < 64, near_in[sweep, 3, 0], near_in[sweep, 2, 0]),
        ]
        for h in range(OWN):
            cols = slice(h * LANES, (h + 1) * LANES)
            total = table[0:8, cols] - start[:, cols]
            for half in range(4):
                spot = inverse_list[h * 4 + half]
                total = total + jnp.where(
                    spot >= 0, take(arrived[half // 2], jnp.maximum(spot, 0)), 0.0
                )
            table[0:8, cols] = start[:, cols] + total * weight[:, cols]

        @pl.when(on)
        def _():
            take_all(far_copies(sweep))

            def landed(right, up, pair):
                straight = right == 0 or up == 0
                return far_in[sweep, FAR.index((right, up)), 0 if straight else pair]

            left = lane8 < 64
            for pair in range(2):
                if pair == 0:
                    listed_now = jnp.where(left, near_in[sweep, 0, 0], near_in[sweep, 1, 0])
                    beyond = jnp.where(left, landed(2, 0, 0), landed(-2, 0, 0))
                    side_a = jnp.where(left, landed(-1, 1, 1), landed(-1, -1, 1))
                    side_b = jnp.where(left, landed(1, 1, 1), landed(1, -1, 1))
                else:
                    listed_now = jnp.where(left, near_in[sweep, 2, 1], near_in[sweep, 3, 1])
                    beyond = jnp.where(left, landed(0, 2, 1), landed(0, -2, 1))
                    side_a = jnp.where(left, landed(1, -1, 0), landed(-1, -1, 0))
                    side_b = jnp.where(left, landed(1, 1, 0), landed(-1, 1, 0))
                was = start[:, copied[pair]]
                total = (listed_now - was) + sweep_out[sweep, 1 + pair]
                total = total + jnp.where(
                    left, pull(beyond, pair, 2 * pair + 1), pull(beyond, pair, 2 * pair)
                )
                for row in (2 - 2 * pair, 3 - 2 * pair):
                    total = total + jnp.where(
                        left, pull(side_a, pair, row), pull(side_b, pair, row)
                    )
                table[0:8, copied[pair]] = was + total * hints[pair, 4:5]
            sent_all(far_copies(sweep))

        sent_all(near)
        return carry

    lax.fori_loop(0, SWEEPS, one_sweep, 0)
    for h in range(OWN):
        vel_out[pl.ds(h, 6, stride=OWN), :] = table[0:6, h * LANES : (h + 1) * LANES]
    for i in range(3):
        imp_out[i * TILES : (i + 1) * TILES, :] = impulse[i, 0:TILES]
    sent_all(first_trade + info_trade)
    for step in range(1, WIN):
        relay_copy(step).wait_send()


def on_device(n_sub, n_layer, geometry, dest_slot, pairs, colors, free_vel, inertia, exports):
    vmem = pl.BlockSpec(memory_space=pltpu.VMEM)
    hbm = pl.BlockSpec(memory_space=pltpu.HBM)
    impulse, velocity = pl.pallas_call(
        lambda *refs: kernel(n_sub, n_layer, *refs),
        out_shape=(
            jax.ShapeDtypeStruct((3 * TILES, LANES), F32),
            jax.ShapeDtypeStruct((6 * OWN, LANES), F32),
        ),
        in_specs=[hbm] * 7,
        out_specs=(vmem, vmem),
        scratch_shapes=[
            pltpu.VMEM((10 * TILES, LANES), F32),
            pltpu.VMEM((TILES, LANES), jnp.int32),
            pltpu.VMEM((2 * TILES, LANES), jnp.int32),
            pltpu.SMEM((1, TILES), jnp.int32),
            pltpu.VMEM((6 * OWN, LANES), F32),
            pltpu.VMEM((4 * OWN, LANES), F32),
            pltpu.VMEM((4, 1, 64), jnp.int32),
            pltpu.SemaphoreType.DMA((7,)),
            pltpu.VMEM((TILES * LANES, SPLIT), BF16),
            pltpu.VMEM((2 * TILES * LANES, SPLIT), BF16),
            pltpu.VMEM((32, TILES * LANES), F32),
            pltpu.VMEM((192, TILES * LANES), BF16),
            pltpu.VMEM((2 * TILES, 16, LANES), BF16),
            pltpu.VMEM((WIN, 10 * TILES, LANES), F32),
            pltpu.VMEM((WIN - 1, 10 * TILES, LANES), F32),
            pltpu.VMEM((10, ROWS, LANES), F32),
            pltpu.VMEM((2, ROWS, LANES), jnp.int32),
            pltpu.VMEM((ROWS, LANES), jnp.int32),
            pltpu.VMEM((28, ROWS, LANES), F32),
            pltpu.VMEM((3, ROWS, LANES), F32),
            pltpu.VMEM((2, 8 * TILES, LANES), F32),
            pltpu.VMEM((16, TABLE * LANES), F32),
            pltpu.VMEM((8, TABLE * LANES), F32),
            pltpu.VMEM((16, 8, LANES), jnp.int32),
            pltpu.VMEM((8, OWN * LANES), F32),
            pltpu.VMEM((2, 16, LANES), F32),
            pltpu.VMEM((4, 16, LANES), F32),
            pltpu.VMEM((8, OWN * LANES), F32),
            pltpu.VMEM((2, 8, LANES), F32),
            pltpu.VMEM((4, 8, LANES), F32),
            pltpu.VMEM((2, 8, LANES), F32),
            pltpu.VMEM((SWEEPS, 4, 8, LANES), F32),
            pltpu.VMEM((SWEEPS, 4, 2, 8, LANES), F32),
            pltpu.VMEM((SWEEPS - 1, 8, 2, 8, LANES), F32),
            pltpu.SemaphoreType.DMA((WIN - 1,)),
            pltpu.SemaphoreType.DMA((WIN - 1,)),
            pltpu.SemaphoreType.DMA((2 + SWEEPS, 4)),
            pltpu.SemaphoreType.DMA((2 + SWEEPS, 4)),
            pltpu.SemaphoreType.DMA((SWEEPS - 1, 8)),
            pltpu.SemaphoreType.DMA((SWEEPS - 1, 8)),
        ],
        compiler_params=pltpu.CompilerParams(
            collective_id=0, has_side_effects=True, vmem_limit_bytes=32 << 20
        ),
    )(
        *(
            pltpu.with_memory_space_constraint(array, pltpu.HBM)
            for array in (
                geometry.reshape(10 * TILES, LANES),
                dest_slot.reshape(TILES, 1, LANES),
                pairs.reshape(2 * TILES, LANES),
                colors,
                free_vel.reshape(6 * OWN, LANES),
                inertia.reshape(4 * OWN, LANES),
                exports,
            )
        )
    )
    return impulse.reshape(3, 1, TILES * LANES), velocity.reshape(6, 1, OWN * LANES)


def solution(mesh):
    n_sub, n_layer = mesh.shape["sub"], mesh.shape["layer"]
    placed = (
        P(None, "layer", "sub"),
        P("layer", "sub"),
        P(None, "layer", "sub"),
        P("layer", "sub"),
        P(None, "layer", "sub"),
        P(None, "layer", "sub"),
        P(None, "layer", "sub"),
    )
    return jax.shard_map(
        lambda *arrays: on_device(n_sub, n_layer, *arrays),
        mesh=mesh,
        in_specs=placed,
        out_specs=(P(None, "layer", "sub"), P(None, "layer", "sub")),
        check_vma=False,
    )
```

```python
import jax
import jax.numpy as jnp
from jax import lax
from jax.experimental import pallas as pl
from jax.experimental.pallas import tpu as pltpu
from jax.sharding import PartitionSpec as P

WIN = 4
SWEEPS = 3
NCOLOR = 4
LANES = 128
TILES = 12
ROWS = 16
CHUNK = 2
SPLIT = 256
OWN = 4
TABLE = 6

relaxation = 0.7
friction = 0.6
tangent_floor = 0.1

NEAR = ((-1, 0), (1, 0), (0, -1), (0, 1))
FAR = ((-2, 0), (2, 0), (0, -2), (0, 2), (-1, -1), (-1, 1), (1, -1), (1, 1))
MESH = pl.DeviceIdType.MESH
F32 = jnp.float32
BF16 = jnp.bfloat16
NT = (((1,), (1,)), ((), ()))


def cross(u, v):
    return [
        u[1] * v[2] - u[2] * v[1],
        u[2] * v[0] - u[0] * v[2],
        u[0] * v[1] - u[1] * v[0],
    ]


def dot3(u, v):
    return u[0] * v[0] + u[1] * v[1] + u[2] * v[2]


def take(row_block, index):
    return jnp.take_along_axis(row_block, index, axis=1, mode="promise_in_bounds")


def coarse(value):
    return value.astype(BF16).astype(F32)


def arm_block(arm, spin):
    return [
        spin[1] * arm[2] * arm[2] + spin[2] * arm[1] * arm[1],
        spin[0] * arm[2] * arm[2] + spin[2] * arm[0] * arm[0],
        spin[0] * arm[1] * arm[1] + spin[1] * arm[0] * arm[0],
        -spin[2] * arm[0] * arm[1],
        -spin[1] * arm[0] * arm[2],
        -spin[0] * arm[1] * arm[2],
    ]


def kernel(
    n_sub,
    n_layer,
    geo_hbm,
    slot_hbm,
    pairs_hbm,
    color_hbm,
    free_hbm,
    inertia_hbm,
    exports_hbm,
    imp_out,
    vel_out,
    geo_ref,
    slot_ref,
    pairs_ref,
    color_ref,
    free_ref,
    inertia_ref,
    exports_ref,
    load_sem,
    slot_hot,
    pair_hot,
    split_geo,
    relay_left,
    block_of,
    outgoing,
    incoming,
    geo,
    index,
    shade,
    const,
    impulse,
    push,
    table,
    start,
    inverse_list,
    weight,
    first_out,
    first_in,
    info,
    info_out,
    info_in,
    hints,
    far_spot,
    sweep_out,
    near_in,
    far_in,
    relay_send,
    relay_recv,
    near_send,
    near_recv,
    far_send,
    far_recv,
):
    sub = lax.axis_index("sub")
    layer = lax.axis_index("layer")
    base = (sub // WIN) * WIN
    place = sub - base
    def mate(step):
        return base + lax.rem(place + step, WIN)

    def reach(right, up):
        there, above = sub + right, layer + up
        return (there >= 0) & (there < n_sub) & (above >= 0) & (above < n_layer)

    def device(right, up):
        return (
            lax.rem(sub + n_sub + right, n_sub),
            lax.rem(layer + n_layer + up, n_layer),
        )

    def start_all(copies):
        for copy, right, up in copies:
            pl.when(reach(right, up))(copy.start)

    def take_all(copies):
        for copy, right, up in copies:
            pl.when(reach(-right, -up))(copy.wait_recv)

    def sent_all(copies):
        for copy, right, up in copies:
            pl.when(reach(right, up))(copy.wait_send)

    first_in[...] = jnp.zeros_like(first_in)
    info_in[...] = jnp.zeros_like(info_in)
    near_in[...] = jnp.zeros_like(near_in)
    far_in[...] = jnp.zeros_like(far_in)

    barrier = pltpu.get_barrier_semaphore()
    greeted = jnp.int32(WIN - 1)
    for right, up in NEAR:

        @pl.when(reach(right, up))
        def _():
            pl.semaphore_signal(
                barrier, inc=1, device_id=device(right, up), device_id_type=MESH
            )

        greeted = greeted + reach(right, up).astype(jnp.int32)
    for step in range(1, WIN):
        pl.semaphore_signal(
            barrier, inc=1, device_id=(mate(step), layer), device_id_type=MESH
        )

    loads = [
        pltpu.make_async_copy(src, dst, load_sem.at[i])
        for i, (src, dst) in enumerate(
            (
                (free_hbm, free_ref),
                (inertia_hbm, inertia_ref),
                (exports_hbm, exports_ref),
                (geo_hbm, geo_ref),
                (slot_hbm.at[:, 0, :], slot_ref),
                (pairs_hbm, pairs_ref),
                (color_hbm, color_ref),
            )
        )
    ]
    for load in loads:
        load.start()

    def trade(step, source_of, dst):
        copies = []
        for right, up in NEAR:
            slot = NEAR.index((-right, -up))
            copy = pltpu.make_async_remote_copy(
                src_ref=source_of(0 if up == 0 else 1),
                dst_ref=dst.at[slot],
                send_sem=near_send.at[step, slot],
                recv_sem=near_recv.at[step, slot],
                device_id=device(right, up),
                device_id_type=MESH,
            )
            copies.append((copy, right, up))
        return copies

    def near_copies(sweep):
        return trade(
            2 + sweep, lambda pair: sweep_out.at[sweep, pl.ds(2 * pair, 2)], near_in.at[sweep]
        )

    def far_copies(sweep):
        copies = []
        for right, up in FAR:
            slot = FAR.index((-right, -up))
            first, count = 2 if right == 0 else 1, 1 if right == 0 or up == 0 else 2
            copy = pltpu.make_async_remote_copy(
                src_ref=sweep_out.at[sweep, pl.ds(first, count)],
                dst_ref=far_in.at[sweep, slot, pl.ds(0, count)],
                send_sem=far_send.at[sweep, slot],
                recv_sem=far_recv.at[sweep, slot],
                device_id=device(right, up),
                device_id_type=MESH,
            )
            copies.append((copy, right, up))
        return copies

    lane8 = lax.broadcasted_iota(jnp.int32, (8, LANES), 1)
    lane16 = lax.broadcasted_iota(jnp.int32, (ROWS, LANES), 1)

    table[...] = jnp.zeros_like(table)
    for load in loads[0:3]:
        load.wait()
    for h in range(OWN):
        cols = slice(h * LANES, (h + 1) * LANES)
        table[0:6, cols] = free_ref[pl.ds(h, 6, stride=OWN), :]
        table[8:12, cols] = inertia_ref[pl.ds(h, 4, stride=OWN), :]
    listed = [
        jnp.concatenate([exports_ref[1], exports_ref[0]], axis=1),
        jnp.concatenate([exports_ref[3], exports_ref[2]], axis=1),
    ]

    def pick_listed(pair, rows, source=table):
        high = jnp.broadcast_to(lax.shift_right_logical(listed[pair], 7), (rows, LANES))
        low = jnp.broadcast_to(lax.bitwise_and(listed[pair], 127), (rows, LANES))
        got = take(source[0:rows, 0:LANES], low)
        for h in range(1, OWN):
            block = take(source[0:rows, h * LANES : (h + 1) * LANES], low)
            got = jnp.where(high == h, block, got)
        return got

    for pair in range(2):
        first_out[pair] = pick_listed(pair, 16)

    for load in loads[3:]:
        load.wait()
    for t in range(TILES):
        cols = slice(t * LANES, (t + 1) * LANES)
        main = geo_ref[pl.ds(t, 8, stride=TILES), :]
        rest = geo_ref[pl.ds(8 * TILES + t, 2, stride=TILES), :]
        main_a = coarse(main)
        main_b = coarse(main - main_a)
        rest_a = coarse(rest)
        rest_b = coarse(rest - rest_a)
        split_geo[0:8, cols] = main_a
        split_geo[8:16, cols] = main_b
        split_geo[16:24, cols] = main - main_a - main_b
        split_geo[24:26, cols] = rest_a
        split_geo[26:28, cols] = rest_b
        split_geo[28:30, cols] = rest - rest_a - rest_b
        split_geo[30:32, cols] = jnp.zeros((2, LANES), F32)

    along = lax.broadcasted_iota(jnp.int32, (LANES, SPLIT), 1).astype(F32)

    def upright_hot(codes, hot):
        upright = jnp.transpose(lax.bitwise_and(codes, SPLIT - 1).astype(F32))
        for t in range(codes.shape[0]):
            hot[t * LANES : (t + 1) * LANES, :] = (
                (along == upright[:, t : t + 1]).astype(F32).astype(BF16)
            )

    upright_hot(slot_ref[...], slot_hot)

    def relay_copy(step):
        return pltpu.make_async_remote_copy(
            src_ref=outgoing.at[lax.rem(place + step, WIN)],
            dst_ref=incoming.at[step - 1],
            send_sem=relay_send.at[step - 1],
            recv_sem=relay_recv.at[step - 1],
            device_id=(mate(step), layer),
            device_id_type=MESH,
        )

    def arrange(target):
        for t in range(TILES):
            cols = slice(t * LANES, (t + 1) * LANES)
            part = lax.shift_right_logical(slot_ref[t : t + 1, :], 8)
            part = (part - (base + target) * TABLE).astype(F32)
            part = jnp.broadcast_to(part, (32, LANES)).astype(BF16)
            values = split_geo[:, cols].astype(BF16)
            for g in range(TABLE):
                relay_left[g * 32 : (g + 1) * 32, cols] = jnp.where(
                    part == jnp.asarray(g, BF16), values, jnp.zeros((32, LANES), BF16)
                )
        placed = jnp.dot(relay_left[...], slot_hot[...], preferred_element_type=F32)
        for g in range(TABLE):
            block = placed[g * 32 : (g + 1) * 32]
            main = block[0:8] + block[8:16] + block[16:24]
            rest = block[24:26] + block[26:28] + block[28:30]
            for j in range(2):
                cols = slice(j * LANES, (j + 1) * LANES)
                t = 2 * g + j
                outgoing[target, pl.ds(t, 8, stride=TILES), :] = main[:, cols]
                outgoing[target, pl.ds(8 * TILES + t, 2, stride=TILES), :] = rest[:, cols]

    def arrange_for(step, carry):
        arrange(lax.rem(place + step, WIN))
        return carry

    arrange_for(2, 0)
    pl.semaphore_wait(barrier, greeted)
    first_trade = trade(0, lambda pair: first_out.at[pair], first_in)
    start_all(first_trade)
    relay_copy(2).start()

    def arrange_send(turn, carry):
        step = 1 + 2 * turn
        arrange(lax.rem(place + step, WIN))
        relay_copy(step).start()
        return carry

    lax.fori_loop(0, 2, arrange_send, 0)
    arrange(place)

    index[...] = jnp.zeros_like(index)
    for e in range(2):
        index[e, 0:TILES] = pairs_ref[e * TILES : (e + 1) * TILES, :]
    upright_hot(pairs_ref[...], pair_hot)
    row16 = lax.broadcasted_iota(jnp.int32, (ROWS, LANES), 0)
    tint = jnp.full((ROWS, LANES), -1, jnp.int32)
    for t in range(TILES):
        tint = jnp.where(row16 == t, color_ref[0, t], tint)
    shade[...] = tint

    wide = lax.broadcasted_iota(jnp.int32, (16, 2 * LANES), 1)
    marks = jnp.where(
        lax.broadcasted_iota(jnp.int32, (16, 2 * LANES), 0) == wide // 64,
        lax.bitwise_and(wide, 127) + 1,
        0,
    )
    tall = lax.broadcasted_iota(jnp.int32, (OWN * LANES, LANES), 0)
    listed_hot = jnp.concatenate(
        [(tall == listed[pair]).astype(F32).astype(BF16) for pair in range(2)], axis=1
    )
    found = lax.dot_general(
        marks.astype(F32).astype(BF16), listed_hot, NT, preferred_element_type=F32
    )
    has_lower_sub = (sub > 0).astype(jnp.int32)
    has_higher_sub = (sub < n_sub - 1).astype(jnp.int32)
    has_lower_layer = (layer > 0).astype(jnp.int32)
    has_higher_layer = (layer < n_layer - 1).astype(jnp.int32)
    exists = (has_higher_sub, has_lower_sub, has_higher_layer, has_lower_layer)
    for h in range(OWN):
        cols = slice(h * LANES, (h + 1) * LANES)
        times = jnp.ones((8, LANES), F32)
        for half in range(4):
            spot = jnp.broadcast_to(found[half : half + 1, cols], (8, LANES))
            spot = spot.astype(jnp.int32) * exists[half] - 1
            inverse_list[h * 4 + half] = spot
            info[half : half + 1, cols] = spot[0:1].astype(F32)
            times = times + jnp.where(spot >= 0, 1.0, 0.0)
        weight[:, cols] = 1.0 / times
        info[4:8, cols] = (1.0 / times)[0:4]
    for pair in range(2):
        info_out[pair] = pick_listed(pair, 8, info)
    info_trade = trade(1, lambda pair: info_out.at[pair], info_in)
    start_all(info_trade)
    push[...] = jnp.zeros_like(push)
    zero16 = jnp.zeros((16, LANES), BF16)
    for t in range(2 * TILES):
        part = lax.shift_right_logical(pairs_ref[t : t + 1, :], 8).astype(F32)
        block_of[t] = jnp.broadcast_to(part, (16, LANES)).astype(BF16)
    impulse[...] = jnp.zeros_like(impulse)
    geo[...] = jnp.ones_like(geo)

    def keep(flag, value):
        return jnp.where(flag > 0, value, 0.0)

    def halves(lane, landed):
        return (
            jnp.where(
                lane < 64, keep(has_lower_sub, landed[0]), keep(has_higher_sub, landed[1])
            ),
            jnp.where(
                lane < 64, keep(has_lower_layer, landed[2]), keep(has_higher_layer, landed[3])
            ),
        )

    take_all(first_trade)
    table[:, 512:640], table[:, 640:768] = halves(lane16, [first_in[slot] for slot in range(4)])

    def pick(component, e):
        high = lax.shift_right_logical(index[e], 7)
        low = lax.bitwise_and(index[e], 127)
        got = None
        for h in range(TABLE if e else OWN):
            row = table[component : component + 1, h * LANES : (h + 1) * LANES]
            block = take(jnp.broadcast_to(row, (ROWS, LANES)), low)
            got = block if h == 0 else jnp.where(high == h, block, got)
        return got

    props_a = [pick(8 + i, 0) for i in range(4)]
    props_b = [pick(8 + i, 1) for i in range(4)]
    for i in range(4):
        const[20 + i] = props_a[i]
        const[24 + i] = props_b[i]

    for step in range(1, WIN):
        relay_copy(step).wait_recv()
    for c in range(10):
        rows = slice(c * TILES, (c + 1) * TILES)
        geo[c, 0:TILES] = (
            outgoing[place, rows] + incoming[0, rows] + incoming[1, rows] + incoming[2, rows]
        )

    raw = [geo[i] for i in range(3)]
    length = jnp.sqrt(dot3(raw, raw))
    normal = [r / length for r in raw]
    side = jnp.sqrt(normal[1] * normal[1] + normal[2] * normal[2])
    one_y = normal[2] / side
    one_z = -normal[1] / side
    two = cross(normal, [jnp.zeros_like(side), one_y, one_z])
    frame = [normal, [jnp.zeros_like(side), one_y, one_z], two]
    entry_a = arm_block([geo[3 + i] for i in range(3)], props_a[1:])
    entry_b = arm_block([geo[6 + i] for i in range(3)], props_b[1:])
    mass = props_a[0] + props_b[0]
    xx, yy, zz, xy, xz, yz = [a + b for a, b in zip(entry_a, entry_b)]
    xx, yy, zz = mass + xx, mass + yy, mass + zz
    cxx = yy * zz - yz * yz
    cxy = xz * yz - xy * zz
    cxz = xy * yz - xz * yy
    cyy = xx * zz - xz * xz
    cyz = xy * xz - xx * yz
    czz = xx * yy - xy * xy
    scale = relaxation / (xx * cxx + xy * cxy + xz * cxz)
    solve = [[cxx, cxy, cxz], [cxy, cyy, cyz], [cxz, cyz, czz]]
    for i in range(3):
        row = [dot3(frame[i], solve[j]) * scale for j in range(3)]
        for j in range(3):
            const[8 + 3 * i + j] = row[j]
        const[17 + i] = dot3(row, normal) * geo[9]
    for i in range(3):
        const[i] = normal[i]
        const[5 + i] = two[i]
    const[3] = one_y
    const[4] = one_z

    def color_pass(color, carry):
        vel_a = [pick(c, 0) for c in range(6)]
        vel_b = [pick(c, 1) for c in range(6)]
        arm_a = [geo[3 + i] for i in range(3)]
        arm_b = [geo[6 + i] for i in range(3)]
        turn_a = cross(vel_a[3:], arm_a)
        turn_b = cross(vel_b[3:], arm_b)
        relative = [vel_a[i] + turn_a[i] - vel_b[i] - turn_b[i] for i in range(3)]
        old = [impulse[i] for i in range(3)]
        trial = [
            old[i]
            - dot3([const[8 + 3 * i + j] for j in range(3)], relative)
            - const[17 + i]
            for i in range(3)
        ]
        press = jnp.maximum(trial[0], 0.0)
        slide = jnp.sqrt(trial[1] * trial[1] + trial[2] * trial[2])
        factor = jnp.minimum(1.0, friction * press / jnp.maximum(slide, tangent_floor))
        active = shade[...] == color
        new = [
            jnp.where(active, value, was)
            for value, was in zip([press, trial[1] * factor, trial[2] * factor], old)
        ]
        change = [a - b for a, b in zip(new, old)]
        for i in range(3):
            impulse[i] = new[i]
        force = [
            const[0] * change[0] + const[5] * change[2],
            const[1] * change[0] + const[3] * change[1] + const[6] * change[2],
            const[2] * change[0] + const[4] * change[1] + const[7] * change[2],
        ]
        torque_a = cross(arm_a, force)
        torque_b = cross(arm_b, force)
        for i in range(3):
            lin = slice(i * TILES, (i + 1) * TILES)
            ang = slice((3 + i) * TILES, (4 + i) * TILES)
            push[0, lin] = (const[20] * force[i])[0:TILES]
            push[1, lin] = (-const[24] * force[i])[0:TILES]
            push[0, ang] = (const[21 + i] * torque_a[i])[0:TILES]
            push[1, ang] = (-const[25 + i] * torque_b[i])[0:TILES]
        lefts = []
        for e in range(2):
            for t in range(TILES):
                value = push[e, pl.ds(t, 8, stride=TILES), :]
                upper = coarse(value)
                both = jnp.concatenate([upper, value - upper], axis=0).astype(BF16)
                lefts.append(
                    jnp.concatenate(
                        [
                            jnp.where(block_of[e * TILES + t] == jnp.asarray(h, BF16), both, zero16)
                            for h in range(2 + e)
                        ],
                        axis=0,
                    )
                )
        def product(first, count):
            return jnp.dot(
                jnp.concatenate(lefts[first : first + count], axis=1),
                pair_hot[first * LANES : (first + count) * LANES, :],
                preferred_element_type=F32,
            )

        total_a = sum(product(f, CHUNK) for f in range(0, TILES, CHUNK))
        total_b = sum(product(f, CHUNK) for f in range(TILES, 2 * TILES, CHUNK))
        for h in range(3):
            cols = slice(h * SPLIT, (h + 1) * SPLIT)
            gain = total_b[h * 16 : h * 16 + 8] + total_b[h * 16 + 8 : h * 16 + 16]
            if h < 2:
                gain = gain + total_a[h * 16 : h * 16 + 8] + total_a[h * 16 + 8 : h * 16 + 16]
            table[0:8, cols] = table[0:8, cols] + gain
        return carry

    def pull(row_block, pair, row):
        spot = far_spot[pair * 4 + row]
        return jnp.where(spot >= 0, take(row_block, jnp.maximum(spot, 0)), 0.0)

    def one_sweep(sweep, carry):
        start[...] = table[0:8, :]
        lax.fori_loop(0, NCOLOR, color_pass, 0)
        on = sweep + 1 < SWEEPS
        copied = [slice((OWN + pair) * LANES, (OWN + pair + 1) * LANES) for pair in range(2)]
        for pair in range(2):
            sweep_out[sweep, 1 + pair] = table[0:8, copied[pair]] - start[:, copied[pair]]

        @pl.when(on)
        def _():
            start_all(far_copies(sweep))

        for pair in range(2):
            sweep_out[sweep, 3 * pair] = pick_listed(pair, 8)
        near = near_copies(sweep)
        start_all(near)

        @pl.when(sweep == 0)
        def _():
            take_all(info_trade)
            hints[0], hints[1] = halves(lane8, [info_in[slot] for slot in range(4)])
            for pair in range(2):
                for row in range(4):
                    far_spot[pair * 4 + row] = jnp.broadcast_to(
                        hints[pair, row : row + 1], (8, LANES)
                    ).astype(jnp.int32)
            sent_all(first_trade + info_trade)
            for step in range(1, WIN):
                relay_copy(step).wait_send()

        @pl.when(sweep > 0)
        def _():
            sent_all(near_copies(sweep - 1) + far_copies(sweep - 1))

        take_all(near)
        arrived = [
            jnp.where(lane8 < 64, near_in[sweep, 1, 1], near_in[sweep, 0, 1]),
            jnp.where(lane8 < 64, near_in[sweep, 3, 0], near_in[sweep, 2, 0]),
        ]
        for h in range(OWN):
            cols = slice(h * LANES, (h + 1) * LANES)
            total = table[0:8, cols] - start[:, cols]
            for half in range(4):
                spot = inverse_list[h * 4 + half]
                total = total + jnp.where(
                    spot >= 0, take(arrived[half // 2], jnp.maximum(spot, 0)), 0.0
                )
            table[0:8, cols] = start[:, cols] + total * weight[:, cols]

        @pl.when(on)
        def _():
            take_all(far_copies(sweep))

            def landed(right, up, pair):
                straight = right == 0 or up == 0
                return far_in[sweep, FAR.index((right, up)), 0 if straight else pair]

            left = lane8 < 64
            for pair in range(2):
                if pair == 0:
                    listed_now = jnp.where(left, near_in[sweep, 0, 0], near_in[sweep, 1, 0])
                    beyond = jnp.where(left, landed(2, 0, 0), landed(-2, 0, 0))
                    side_a = jnp.where(left, landed(-1, 1, 1), landed(-1, -1, 1))
                    side_b = jnp.where(left, landed(1, 1, 1), landed(1, -1, 1))
                else:
                    listed_now = jnp.where(left, near_in[sweep, 2, 1], near_in[sweep, 3, 1])
                    beyond = jnp.where(left, landed(0, 2, 1), landed(0, -2, 1))
                    side_a = jnp.where(left, landed(1, -1, 0), landed(-1, -1, 0))
                    side_b = jnp.where(left, landed(1, 1, 0), landed(-1, 1, 0))
                was = start[:, copied[pair]]
                total = (listed_now - was) + sweep_out[sweep, 1 + pair]
                total = total + jnp.where(
                    left, pull(beyond, pair, 2 * pair + 1), pull(beyond, pair, 2 * pair)
                )
                for row in (2 - 2 * pair, 3 - 2 * pair):
                    total = total + jnp.where(
                        left, pull(side_a, pair, row), pull(side_b, pair, row)
                    )
                table[0:8, copied[pair]] = was + total * hints[pair, 4:5]

        return carry

    lax.fori_loop(0, SWEEPS, one_sweep, 0)
    for h in range(OWN):
        vel_out[pl.ds(h, 6, stride=OWN), :] = table[0:6, h * LANES : (h + 1) * LANES]
    for i in range(3):
        imp_out[i * TILES : (i + 1) * TILES, :] = impulse[i, 0:TILES]
    sent_all(near_copies(SWEEPS - 1))


def on_device(n_sub, n_layer, geometry, dest_slot, pairs, colors, free_vel, inertia, exports):
    vmem = pl.BlockSpec(memory_space=pltpu.VMEM)
    hbm = pl.BlockSpec(memory_space=pltpu.HBM)
    impulse, velocity = pl.pallas_call(
        lambda *refs: kernel(n_sub, n_layer, *refs),
        out_shape=(
            jax.ShapeDtypeStruct((3 * TILES, LANES), F32),
            jax.ShapeDtypeStruct((6 * OWN, LANES), F32),
        ),
        in_specs=[hbm] * 7,
        out_specs=(vmem, vmem),
        scratch_shapes=[
            pltpu.VMEM((10 * TILES, LANES), F32),
            pltpu.VMEM((TILES, LANES), jnp.int32),
            pltpu.VMEM((2 * TILES, LANES), jnp.int32),
            pltpu.SMEM((1, TILES), jnp.int32),
            pltpu.VMEM((6 * OWN, LANES), F32),
            pltpu.VMEM((4 * OWN, LANES), F32),
            pltpu.VMEM((4, 1, 64), jnp.int32),
            pltpu.SemaphoreType.DMA((7,)),
            pltpu.VMEM((TILES * LANES, SPLIT), BF16),
            pltpu.VMEM((2 * TILES * LANES, SPLIT), BF16),
            pltpu.VMEM((32, TILES * LANES), F32),
            pltpu.VMEM((192, TILES * LANES), BF16),
            pltpu.VMEM((2 * TILES, 16, LANES), BF16),
            pltpu.VMEM((WIN, 10 * TILES, LANES), F32),
            pltpu.VMEM((WIN - 1, 10 * TILES, LANES), F32),
            pltpu.VMEM((10, ROWS, LANES), F32),
            pltpu.VMEM((2, ROWS, LANES), jnp.int32),
            pltpu.VMEM((ROWS, LANES), jnp.int32),
            pltpu.VMEM((28, ROWS, LANES), F32),
            pltpu.VMEM((3, ROWS, LANES), F32),
            pltpu.VMEM((2, 8 * TILES, LANES), F32),
            pltpu.VMEM((16, TABLE * LANES), F32),
            pltpu.VMEM((8, TABLE * LANES), F32),
            pltpu.VMEM((16, 8, LANES), jnp.int32),
            pltpu.VMEM((8, OWN * LANES), F32),
            pltpu.VMEM((2, 16, LANES), F32),
            pltpu.VMEM((4, 16, LANES), F32),
            pltpu.VMEM((8, OWN * LANES), F32),
            pltpu.VMEM((2, 8, LANES), F32),
            pltpu.VMEM((4, 8, LANES), F32),
            pltpu.VMEM((2, 8, LANES), F32),
            pltpu.VMEM((8, 8, LANES), jnp.int32),
            pltpu.VMEM((SWEEPS, 4, 8, LANES), F32),
            pltpu.VMEM((SWEEPS, 4, 2, 8, LANES), F32),
            pltpu.VMEM((SWEEPS - 1, 8, 2, 8, LANES), F32),
            pltpu.SemaphoreType.DMA((WIN - 1,)),
            pltpu.SemaphoreType.DMA((WIN - 1,)),
            pltpu.SemaphoreType.DMA((2 + SWEEPS, 4)),
            pltpu.SemaphoreType.DMA((2 + SWEEPS, 4)),
            pltpu.SemaphoreType.DMA((SWEEPS - 1, 8)),
            pltpu.SemaphoreType.DMA((SWEEPS - 1, 8)),
        ],
        compiler_params=pltpu.CompilerParams(
            collective_id=0, has_side_effects=True, vmem_limit_bytes=32 << 20
        ),
    )(
        *(
            pltpu.with_memory_space_constraint(array, pltpu.HBM)
            for array in (
                geometry.reshape(10 * TILES, LANES),
                dest_slot.reshape(TILES, 1, LANES),
                pairs.reshape(2 * TILES, LANES),
                colors,
                free_vel.reshape(6 * OWN, LANES),
                inertia.reshape(4 * OWN, LANES),
                exports,
            )
        )
    )
    return impulse.reshape(3, 1, TILES * LANES), velocity.reshape(6, 1, OWN * LANES)


def solution(mesh):
    n_sub, n_layer = mesh.shape["sub"], mesh.shape["layer"]
    placed = (
        P(None, "layer", "sub"),
        P("layer", "sub"),
        P(None, "layer", "sub"),
        P("layer", "sub"),
        P(None, "layer", "sub"),
        P(None, "layer", "sub"),
        P(None, "layer", "sub"),
    )
    return jax.shard_map(
        lambda *arrays: on_device(n_sub, n_layer, *arrays),
        mesh=mesh,
        in_specs=placed,
        out_specs=(P(None, "layer", "sub"), P(None, "layer", "sub")),
        check_vma=False,
    )
```
